32 devices in a mesh: seq: 8 (over z, x), req: 4 (over y, core).
Axes of the slice: x: 2, y: 2, z: 4, core: 2. Of those that a mesh axis runs over, the one named last changes fastest.
Arguments:
- tokens: bfloat16 [32, 4, 2048], P('req'), may hold values from -6 to 6
- lengths: int32 [32], P('req'), may hold values from 1 to 508, as said below
- cache_keys: bfloat16 [32, 512, 2048], P('req', 'seq'), may hold values from -120 to 120
- cache_values: bfloat16 [32, 512, 2048], P('req', 'seq'), may hold values from -6 to 6
- norm1_gain: float32 [2048], replicated, may hold values from 0.5 to 1.5
- norm1_bias: float32 [2048], replicated, may hold values from -1.75 to 1.75
- w_query: bfloat16 [2048, 2048], P('req', 'seq'), may hold values from -0.125 to 0.125
- b_query: float32 [2048], P('seq'), may hold values from -3 to 3
- w_key: bfloat16 [2048, 2048], P('req', 'seq'), may hold values from -0.125 to 0.125
- b_key: float32 [2048], P('seq'), may hold values from -3 to 3
- w_value: bfloat16 [2048, 2048], P('req', 'seq'), may hold values from -0.125 to 0.125
- b_value: float32 [2048], P('seq'), may hold values from -3 to 3
- w_out: bfloat16 [2048, 2048], P('req', 'seq'), may hold values from -0.125 to 0.125
- b_out: float32 [2048], P('seq'), may hold values from -3 to 3
- norm2_gain: float32 [2048], replicated, may hold values from 0.5 to 1.5
- norm2_bias: float32 [2048], replicated, may hold values from -1.75 to 1.75
- w_up: bfloat16 [2048, 8192], P('req', 'seq'), may hold values from -0.125 to 0.125
- b_up: float32 [8192], P('seq'), may hold values from -3 to 3
- w_down: bfloat16 [8192, 2048], P('seq', 'req'), may hold values from -0.0625 to 0.0625
- b_down: float32 [2048], replicated, may hold values from -3 to 3
Outputs:
- hidden_out: bfloat16 [32, 4, 2048], P('req')
- new_keys: bfloat16 [32, 512, 2048], P('req', 'seq')
- new_values: bfloat16 [32, 512, 2048], P('req', 'seq')
The draws below stay inside these ranges and needn't reach their ends.
Inputs may be any that keep to these rules, and one draw needn't show every extreme that they name: `lengths`: one request has exactly 508 cached positions.
All inputs are finite; a program needn't handle non-finite values.
Results may differ from the reference program's by a relative error of at most 0.033.
Values may be sent and summed in bfloat16 or wider, within the bound.
No kernel may reach another device: no remote copies, remote signals or barrier semaphores. Data moves between devices by JAX's collectives and lax.ppermute only.
A program may use at most 64 MiB of HBM per device.

```python
import jax
import jax.numpy as jnp
from jax import lax

D = 2048
HEADS = 16
HEAD = 128
FF = 8192
STEPS = 4
REQS = 32
CACHE = 512


def draw_lengths(key, part):
    top = CACHE - STEPS
    first, second, third = jax.random.split(jax.random.fold_in(key, 11), 3)
    left = jax.random.randint(first, (REQS,), 0, top)
    right = jax.random.randint(second, (REQS,), 0, top)
    base = left * right // top + 1
    chosen = jax.random.randint(third, (), 0, REQS)
    return jnp.where(jnp.arange(REQS) == chosen, top, base).astype(jnp.int32)


def draw_cache_keys(key, part):
    first = jax.random.fold_in(jax.random.fold_in(key, 23), 0)
    values = jnp.clip(jax.random.normal(first, (REQS, CACHE, D), jnp.float32), -4.0, 4.0)
    return values.astype(jnp.bfloat16)


def block_scale(own_key, extent, cuts, low, high):
    def one(dim, shards_of):
        steps = jax.random.uniform(jax.random.fold_in(jax.random.fold_in(own_key, 6), dim), (shards_of,), jnp.float32, low / len(cuts), high / len(cuts))
        return jnp.repeat(jnp.exp(steps), extent[dim] // shards_of).reshape((-1,) + (1,) * (len(extent) - dim - 1))

    factor_of = one(*cuts[0])
    for cut in cuts[1:]:
        factor_of = factor_of * one(*cut)
    return factor_of


def scatter_about(rng, extent, width, reach, cuts=(), kind=jnp.bfloat16):
    result = jax.random.normal(rng, extent, jnp.float32) * width
    if len(cuts) > 0:
        result = block_scale(rng, extent, cuts, -0.22, 0.18) * result
    return jnp.clip(result, min=-reach, max=reach).astype(kind)


def setup_inputs(seed: int = 0) -> dict:
    key_of = jax.random.split(jax.random.key(seed), 21)
    return {
        "tokens": scatter_about(key_of[0], (REQS, STEPS, D), 1.0, 6.0, ((0, 4),)),
        "lengths": draw_lengths(jax.random.fold_in(key_of[20], 71), 0),
        "cache_keys": draw_cache_keys(jax.random.fold_in(key_of[20], 71), 0),
        "cache_values": scatter_about(key_of[3], (REQS, CACHE, D), 1.0, 6.0, ((0, 4), (1, 8))),
        "norm1_gain": jnp.clip(jax.random.uniform(key_of[4], (D,), jnp.float32, 0.5, 1.5), 0.5, 1.5),
        "norm1_bias": scatter_about(key_of[5], (D,), 0.3, 1.75, (), jnp.float32),
        "w_query": scatter_about(key_of[6], (D, D), D ** -0.5, 0.125, ((0, 4), (1, 8))),
        "b_query": scatter_about(key_of[7], (D,), 0.5, 3.0, ((0, 8),), jnp.float32),
        "w_key": scatter_about(key_of[8], (D, D), D ** -0.5, 0.125, ((0, 4), (1, 8))),
        "b_key": scatter_about(key_of[9], (D,), 0.5, 3.0, ((0, 8),), jnp.float32),
        "w_value": scatter_about(key_of[10], (D, D), D ** -0.5, 0.125, ((0, 4), (1, 8))),
        "b_value": scatter_about(key_of[11], (D,), 0.5, 3.0, ((0, 8),), jnp.float32),
        "w_out": scatter_about(key_of[12], (D, D), D ** -0.5, 0.125, ((0, 4), (1, 8))),
        "b_out": scatter_about(key_of[13], (D,), 0.5, 3.0, ((0, 8),), jnp.float32),
        "norm2_gain": jnp.clip(jax.random.uniform(key_of[14], (D,), jnp.float32, 0.5, 1.5), 0.5, 1.5),
        "norm2_bias": scatter_about(key_of[15], (D,), 0.3, 1.75, (), jnp.float32),
        "w_up": scatter_about(key_of[16], (D, FF), D ** -0.5, 0.125, ((0, 4), (1, 8))),
        "b_up": scatter_about(key_of[17], (FF,), 0.5, 3.0, ((0, 8),), jnp.float32),
        "w_down": scatter_about(key_of[18], (FF, D), FF ** -0.5, 0.0625, ((0, 8), (1, 4))),
        "b_down": scatter_about(key_of[19], (D,), 0.5, 3.0, (), jnp.float32),
    }


def layer_norm(values, gain, shift):
    center = values - lax.optimization_barrier(jnp.mean(values, axis=-1, keepdims=True))
    spread = lax.optimization_barrier(jnp.mean(center * center, axis=-1, keepdims=True))
    return center * lax.rsqrt(spread + 1e-05) * gain + shift

def reference(tokens, lengths, cache_keys, cache_values, norm1_gain, norm1_bias, w_query, b_query, w_key, b_key, w_value, b_value, w_out, b_out, norm2_gain, norm2_bias, w_up, b_up, w_down, b_down):
    residual = tokens.astype(jnp.float32)
    normed = layer_norm(residual, norm1_gain, norm1_bias).astype(jnp.bfloat16)
    query = (jnp.dot(normed, w_query, preferred_element_type=jnp.float32) + b_query).astype(jnp.bfloat16)
    key_rows = (jnp.dot(normed, w_key, preferred_element_type=jnp.float32) + b_key).astype(jnp.bfloat16)
    value_rows = (jnp.dot(normed, w_value, preferred_element_type=jnp.float32) + b_value).astype(jnp.bfloat16)
    position = jnp.arange(CACHE, dtype=jnp.int32)
    offsets = jnp.arange(STEPS, dtype=jnp.int32)
    factor = HEAD ** (-0.5)

    def one_request(items):
        keys, values, length, query_row, key_new, value_new = items
        for step in range(STEPS):
            hit = (position == length + step)[:, None]
            keys = jnp.where(hit, key_new[step][None, :], keys)
            values = jnp.where(hit, value_new[step][None, :], values)
        query_heads = query_row.reshape(STEPS, HEADS, HEAD).astype(jnp.float32)
        key_heads = keys.reshape(CACHE, HEADS, HEAD).astype(jnp.float32)
        value_heads = values.reshape(CACHE, HEADS, HEAD).astype(jnp.float32)
        scores = jnp.einsum('thd,shd->ths', query_heads, key_heads) * factor
        valid = position[None, None, :] <= (length + offsets)[:, None, None]
        masked = jnp.where(valid, scores, -1e+30)
        peak = lax.optimization_barrier(jnp.max(masked, axis=-1))
        expo = jnp.where(valid, jnp.exp(masked - peak[..., None]), 0.0)
        total = lax.optimization_barrier(jnp.sum(expo, axis=-1))
        probs = expo.astype(jnp.bfloat16).astype(jnp.float32)
        mixed = jnp.einsum('ths,shd->thd', probs, value_heads) / total[..., None]
        return (keys, values, mixed.reshape(STEPS, D).astype(jnp.bfloat16))
    new_keys, new_values, attn = lax.map(one_request, (cache_keys, cache_values, lengths, query, key_rows, value_rows))
    projected = (jnp.dot(attn, w_out, preferred_element_type=jnp.float32) + b_out).astype(jnp.bfloat16)
    mid = residual + projected.astype(jnp.float32)
    normed2 = layer_norm(mid, norm2_gain, norm2_bias).astype(jnp.bfloat16)
    hidden = jax.nn.gelu(jnp.dot(normed2, w_up, preferred_element_type=jnp.float32) + b_up, approximate=False).astype(jnp.bfloat16)
    hidden_out = (mid + jnp.dot(hidden, w_down, preferred_element_type=jnp.float32) + b_down).astype(jnp.bfloat16)
    return (hidden_out, new_keys, new_values)
```

```python
import jax
import jax.numpy as jnp
from jax import lax
from jax.sharding import PartitionSpec as P

HEAD = 128
BF16 = jnp.bfloat16
F32 = jnp.float32


def layer_norm(values, gain, shift):
    center = values - jnp.mean(values, axis=-1, keepdims=True)
    spread = jnp.mean(center * center, axis=-1, keepdims=True)
    return center * lax.rsqrt(spread + 1e-05) * gain + shift


def gather_blocks(x, axis):
    n = lax.axis_size(axis)
    me = lax.axis_index(axis)
    parts = [x]
    for k in range(1, n):
        parts.append(lax.ppermute(x, axis, [(i, (i - k) % n) for i in range(n)]))
    stacked = jnp.stack(parts)
    return jnp.roll(stacked, me, axis=0)


def columns(blocks):
    n, rows, c = blocks.shape
    return blocks.transpose(1, 0, 2).reshape(rows, n * c)


def swap(x, axis):
    return lax.all_to_all(x, axis, 0, 0, tiled=False)


def project(x, weight):
    parts = lax.axis_size("req")
    rows, depth = x.shape
    sent = x.reshape(rows, parts, depth // parts).transpose(1, 0, 2)
    mine = swap(sent, "req").reshape(parts * rows, depth // parts)
    partial = jnp.dot(mine, weight, preferred_element_type=F32)
    back = swap(partial.reshape(parts, rows, weight.shape[1]), "req")
    return jnp.sum(back, axis=0)


def body(
    tokens,
    lengths,
    cache_keys,
    cache_values,
    norm1_gain,
    norm1_bias,
    w_query,
    b_query,
    w_key,
    b_key,
    w_value,
    b_value,
    w_out,
    b_out,
    norm2_gain,
    norm2_bias,
    w_up,
    b_up,
    w_down,
    b_down,
):
    seqs = lax.axis_size("seq")
    reqs = lax.axis_size("req")
    seq = lax.axis_index("seq")
    group, steps, width = tokens.shape
    slots = cache_keys.shape[1]
    rows = group * steps
    heads = width // HEAD
    cols = width // seqs

    residual = tokens.reshape(rows, width).astype(F32)
    normed = layer_norm(residual, norm1_gain, norm1_bias).astype(BF16)
    w_qkv = jnp.concatenate([w_query, w_key, w_value], axis=1)
    b_qkv = jnp.concatenate([b_query, b_key, b_value])
    qkv = (project(normed, w_qkv) + b_qkv).astype(BF16)
    every = gather_blocks(qkv, "seq").reshape(seqs, rows, 3, cols)
    query = columns(every[:, :, 0]).reshape(group, steps, width)
    key_rows = columns(every[:, :, 1]).reshape(group, steps, width)
    value_rows = columns(every[:, :, 2]).reshape(group, steps, width)

    position = seq * slots + jnp.arange(slots, dtype=jnp.int32)
    new_keys = cache_keys
    new_values = cache_values
    for step in range(steps):
        hit = (position[None, :] == lengths[:, None] + step)[:, :, None]
        new_keys = jnp.where(hit, key_rows[:, step][:, None, :], new_keys)
        new_values = jnp.where(hit, value_rows[:, step][:, None, :], new_values)
    scores = (
        jnp.einsum(
            "rthd,rshd->rths",
            query.reshape(group, steps, heads, HEAD),
            new_keys.reshape(group, slots, heads, HEAD),
            preferred_element_type=F32,
        )
        * HEAD ** (-0.5)
    )
    limit = lengths[:, None] + jnp.arange(steps, dtype=jnp.int32)[None, :]
    valid = position[None, None, None, :] <= limit[:, :, None, None]
    masked = jnp.where(valid, scores, -1e30)
    peak = jnp.max(masked, axis=-1)
    expo = jnp.where(valid, jnp.exp(masked - peak[..., None]), 0.0)
    total = jnp.sum(expo, axis=-1)
    part = jnp.einsum(
        "rths,rshd->rthd",
        expo.astype(BF16),
        new_values.reshape(group, slots, heads, HEAD),
        preferred_element_type=F32,
    )
    stats = jnp.concatenate([peak, total], axis=-1).reshape(rows, 2 * heads)
    stats = jnp.pad(stats, ((0, 0), (0, HEAD - 2 * heads)))
    blocks = part.reshape(rows, seqs, cols).transpose(1, 0, 2)
    message = jnp.concatenate([blocks, jnp.broadcast_to(stats[None], (seqs, rows, HEAD))], axis=-1)
    got = swap(message, "seq")
    peaks = got[:, :, cols : cols + heads]
    totals = got[:, :, cols + heads : cols + 2 * heads]
    scale = jnp.exp(peaks - jnp.max(peaks, axis=0, keepdims=True))
    whole = jnp.sum(totals * scale, axis=0)
    factor = scale / whole
    head_of = (seq * cols + jnp.arange(cols)) // HEAD
    attn = jnp.sum(got[:, :, :cols] * jnp.take(factor, head_of, axis=2), axis=0).astype(BF16)

    attn = columns(gather_blocks(attn, "seq"))
    out_part = (project(attn, w_out) + b_out).astype(BF16)
    projected = columns(gather_blocks(out_part, "seq"))
    mid = residual + projected.astype(F32)
    normed2 = layer_norm(mid, norm2_gain, norm2_bias).astype(BF16)
    hidden = jax.nn.gelu(project(normed2, w_up) + b_up, approximate=False).astype(BF16)

    everyone = gather_blocks(hidden, "req").reshape(reqs * rows, hidden.shape[1])
    feed = jnp.dot(everyone, w_down, preferred_element_type=F32)
    ncols = feed.shape[1]
    share = rows * reqs // seqs
    own = jnp.sum(swap(feed.reshape(seqs, share, ncols), "seq"), axis=0).astype(BF16)
    pieces = lax.all_gather(own, "req")
    full = pieces.transpose(1, 0, 2).reshape(share, width)
    spread = gather_blocks(full, "seq").reshape(reqs, rows, width)
    summed = lax.dynamic_index_in_dim(spread, lax.axis_index("req"), 0, keepdims=False)
    out = (mid + summed.astype(F32) + b_down).astype(BF16)
    return (out.reshape(group, steps, width), new_keys, new_values)


def solution(mesh):
    in_specs = (
        P("req", None, None),
        P("req"),
        P("req", "seq", None),
        P("req", "seq", None),
        P(),
        P(),
        P("req", "seq"),
        P("seq"),
        P("req", "seq"),
        P("seq"),
        P("req", "seq"),
        P("seq"),
        P("req", "seq"),
        P("seq"),
        P(),
        P(),
        P("req", "seq"),
        P("seq"),
        P("seq", "req"),
        P(),
    )
    out_specs = (P("req", None, None), P("req", "seq", None), P("req", "seq", None))
    return jax.shard_map(body, mesh=mesh, in_specs=in_specs, out_specs=out_specs, check_vma=False)
```

```python
import functools

import jax
import jax.numpy as jnp
from jax import lax
from jax.experimental import pallas as pl
from jax.experimental.pallas import tpu as pltpu
from jax.sharding import PartitionSpec as P

HEAD = 128
LANES = 128
CORES = 2
BF16 = jnp.bfloat16
F32 = jnp.float32
VMEM = pl.BlockSpec(memory_space=pltpu.VMEM)
SMEM = pl.BlockSpec(memory_space=pltpu.SMEM)
ANY = pl.BlockSpec(memory_space=pl.ANY)


class Place:
    def __init__(self, seqs, reqs):
        self.ny = reqs // CORES
        self.nx = self.ny if seqs % self.ny == 0 else 1
        self.nz = seqs // self.nx
        self.seqs = seqs

    def x(self):
        return lax.rem(lax.axis_index("seq"), self.nx)

    def y(self):
        return lax.div(lax.axis_index("req"), CORES)

    def core(self):
        return lax.rem(lax.axis_index("req"), CORES)

    def x_before(self, dx):
        return lax.rem(self.x() + self.nx - dx, self.nx)

    def x_after(self, dx):
        return lax.rem(self.x() + dx, self.nx)

    def y_before(self, dy):
        return lax.rem(self.y() + self.ny - dy, self.ny)

    def z_before(self, dz):
        return lax.rem(lax.div(lax.axis_index("seq"), self.nx) + self.nz - dz, self.nz)

    def move(self, value, dx=0, dy=0, dc=0, dz=0):
        pairs = []
        for z in range(self.nz):
            for x in range(self.nx):
                for y in range(self.ny):
                    for c in range(CORES):
                        to_x, to_y, to_c = (x + dx) % self.nx, (y + dy) % self.ny, (c + dc) % CORES
                        to_z = (z + dz) % self.nz
                        pairs.append(
                            (
                                ((z * self.nx + x) * self.ny + y) * CORES + c,
                                ((to_z * self.nx + to_x) * self.ny + to_y) * CORES + to_c,
                            )
                        )
        return lax.ppermute(value, ("seq", "req"), pairs)

    def gather_z(self, value):
        return [value] + [self.move(value, dz=dz) for dz in range(1, self.nz)]


def layer_norm(values, gain, shift):
    center = values - jnp.mean(values, axis=-1, keepdims=True)
    spread = jnp.mean(center * center, axis=-1, keepdims=True)
    return center * lax.rsqrt(spread + 1e-05) * gain + shift


def dot(a, b):
    return jnp.dot(a, b, preferred_element_type=F32)


def at(index, size):
    return pl.ds(pl.multiple_of(index * size, size), size)


def call(kernel, name, ins, outs, in_specs=None, out_specs=None, scratch=()):
    single = not isinstance(outs, (list, tuple))
    specs = out_specs or (VMEM if single else [VMEM] * len(outs))
    return pl.pallas_call(
        kernel,
        name=name,
        out_shape=outs,
        in_specs=in_specs or [VMEM] * len(ins),
        out_specs=specs,
        scratch_shapes=list(scratch),
        compiler_params=pltpu.CompilerParams(vmem_limit_bytes=20 * 1024 * 1024),
    )(*ins)


def side_by_side(blocks, start, size):
    return jnp.concatenate(
        [blocks[x, :, start : start + size].astype(F32) for x in range(blocks.shape[0])], axis=1
    )


def two_halves(rows_by_k, own, sibling):
    depth = own.shape[0]
    req = lax.axis_index("req")
    other = req + 1 - 2 * lax.rem(req, CORES)
    return dot(rows_by_k[:, at(req, depth)], own[...]) + dot(
        rows_by_k[:, at(other, depth)], sibling[...]
    )


def qkv_kernel(place, *refs):
    ny = place.ny
    toks = refs[:ny]
    gain, shift, own, sibling, bias = refs[ny : ny + 5]
    outs = refs[ny + 5 : 2 * ny + 5]
    flat, normed = refs[2 * ny + 5 :]
    group, steps, _ = toks[0].shape
    rows = group * steps
    for j in range(ny):
        for i in range(group):
            flat[j * rows + i * steps : j * rows + (i + 1) * steps, :] = toks[j][i].astype(F32)
    normed[...] = layer_norm(flat[...], gain[...], shift[...]).astype(BF16)
    acc = two_halves(normed, own, sibling)
    for j in range(ny):
        part = acc[j * rows : (j + 1) * rows]
        if j == 0:
            part = part + bias[...]
        outs[(ny - j) % ny][...] = part.astype(BF16)


def add_columns_kernel(place, *refs):
    out = refs[-1]
    for dx in range(place.nx):
        total = refs[dx * place.ny][...].astype(F32)
        for dy in range(1, place.ny):
            total = total + refs[dx * place.ny + dy][...].astype(F32)
        out[place.x_before(dx)] = total.astype(BF16)


def split_three(value):
    first = value.astype(BF16).astype(F32)
    rest = value - first
    second = rest.astype(BF16).astype(F32)
    return first, second, rest - second


def turn(value, by):
    return pltpu.roll(value, by % LANES, 1)


def attention_kernel(place, heads, *refs):
    nx, nz = place.nx, place.nz
    gathered = refs[:nz]
    lengths, keys_in, values_in, keys_out, values_out = refs[nz : nz + 5]
    messages = refs[nz + 5 : nz + 5 + nx]
    qs, ks, vs, part, stats, flat, flat_stats, mask, keys, values, in_sems, out_sems = refs[
        nz + 5 + nx :
    ]
    group, slots, width = keys.shape
    steps = qs.shape[1]
    cols = width // place.seqs
    seq = lax.axis_index("seq")

    def copy_in(i, source, target, which):
        return pltpu.make_async_copy(source.at[i], target.at[i], in_sems.at[which, i])

    def copy_out(i, source, target, which):
        return pltpu.make_async_copy(source.at[i], target.at[i], out_sems.at[which, i])

    for i in range(group):
        copy_in(i, keys_in, keys, 0).start()
        copy_in(i, values_in, values, 1).start()
    for dz in range(nz):
        span = at(place.z_before(dz), nx * cols)
        for k, target in enumerate((qs, ks, vs)):
            block = side_by_side(gathered[dz], k * cols, cols)
            for i in range(group):
                target[i, :, span] = block[i * steps : (i + 1) * steps]
    across = steps * heads
    row_head = lax.rem(lax.broadcasted_iota(jnp.int32, (across, width), 0), heads)
    column_head = lax.div(lax.broadcasted_iota(jnp.int32, (across, width), 1), HEAD)
    mask[...] = (row_head == column_head).astype(F32)

    def one(i, carry):
        length = lengths[i]
        base = length - seq * slots
        copy_in(i, keys_in, keys, 0).wait()
        copy_in(i, values_in, values, 1).wait()

        @pl.when((base > -steps) & (base < slots))
        def _():
            slot = lax.broadcasted_iota(jnp.int32, (slots, width), 0)
            new_k = ks[i]
            new_v = vs[i]
            k = keys[i].astype(F32)
            v = values[i].astype(F32)
            for t in range(steps):
                k = jnp.where(slot == base + t, new_k[t : t + 1], k)
                v = jnp.where(slot == base + t, new_v[t : t + 1], v)
            keys[i] = k.astype(BF16)
            values[i] = v.astype(BF16)

        copy_out(i, keys, keys_out, 0).start()
        copy_out(i, values, values_out, 1).start()
        query = qs[i]
        query = jnp.broadcast_to(query[:, None, :], (steps, heads, width)).reshape(across, width)
        query = (query * mask[...]).astype(BF16)
        scores = lax.dot_general(
            query, keys[i], (((1,), (1,)), ((), ())), preferred_element_type=F32
        ) * HEAD ** (-0.5)
        position = seq * slots + lax.broadcasted_iota(jnp.int32, (across, slots), 1)
        step = lax.div(lax.broadcasted_iota(jnp.int32, (across, slots), 0), heads)
        valid = position <= length + step
        masked = jnp.where(valid, scores, -1e30)
        peak = jnp.max(masked, axis=-1, keepdims=True)
        expo = jnp.where(valid, jnp.exp(masked - peak), 0.0)
        total = jnp.sum(expo, axis=-1, keepdims=True)
        mixed = dot(expo.astype(BF16), values[i]) * mask[...]
        part[i] = jnp.sum(mixed.reshape(steps, heads, width), axis=1)
        lane = lax.broadcasted_iota(jnp.int32, (across, LANES), 1)
        head = lax.rem(lax.broadcasted_iota(jnp.int32, (across, LANES), 0), heads)
        pieces = split_three(peak) + split_three(total)[:2]
        tile = jnp.zeros((across, LANES), F32)
        for k, piece in enumerate(pieces):
            tile = jnp.where(lane == head + k * heads, piece, tile)
        stats[i] = jnp.sum(tile.reshape(steps, heads, LANES), axis=1)
        return carry

    lax.fori_loop(0, group, one, 0)
    for i in range(group):
        flat[i * steps : (i + 1) * steps, :] = part[i]
        flat_stats[i * steps : (i + 1) * steps, :] = stats[i]
    share = width // nx
    for dx in range(nx):
        to = place.x_after(dx)
        messages[dx][:, :share] = flat[:, at(to, share)].astype(BF16)
        messages[dx][:, share:] = pltpu.roll(
            flat_stats[...], lax.rem(LANES - to * (heads // nx), LANES), 1
        ).astype(BF16)
    for i in range(group):
        copy_out(i, keys, keys_out, 0).wait()
        copy_out(i, values, values_out, 1).wait()


def expand(factor, count):
    rows = factor.shape[0]
    return jnp.concatenate(
        [jnp.broadcast_to(factor[:, h : h + 1], (rows, HEAD)) for h in range(count)], axis=1
    )


def merge(messages, heads, share):
    peaks, totals = [], []
    for message in messages:
        stats = message[:, share:].astype(F32)
        peaks.append(stats + turn(stats, -heads) + turn(stats, -2 * heads))
        totals.append(turn(stats, -3 * heads) + turn(stats, -4 * heads))
    peak = functools.reduce(jnp.maximum, peaks)
    scales = [jnp.exp(p - peak) for p in peaks]
    total = sum(t * s for t, s in zip(totals, scales))
    return peak, total, scales


def merge_x_kernel(place, heads, *refs):
    share = refs[0].shape[1] - LANES
    count = share // HEAD
    out = refs[-1]
    messages = [r[...] for r in refs[:-1]]
    peak, total, scales = merge(messages, heads, share)
    out[:, :share] = sum(
        m[:, :share].astype(F32) * expand(s, count) for m, s in zip(messages, scales)
    ).astype(BF16)
    lane = lax.broadcasted_iota(jnp.int32, peak.shape, 1)
    tile = jnp.zeros_like(peak)
    for k, piece in enumerate(split_three(peak) + split_three(total)[:2]):
        tile = tile + turn(jnp.where(lane < count, piece, 0.0), k * heads)
    out[:, share:] = tile.astype(BF16)


def merge_z_kernel(place, heads, *refs):
    share = refs[0].shape[1] - LANES
    count = share // HEAD
    out = refs[-1]
    messages = [r[...] for r in refs[:-1]]
    _, total, scales = merge(messages, heads, share)
    out[...] = sum(
        m[:, :share].astype(F32) * expand(s / total, count) for m, s in zip(messages, scales)
    ).astype(BF16)


def out_kernel(place, *refs):
    nx, ny = place.nx, place.ny
    parts = refs[: nx * ny]
    own, sibling, bias, out, full = refs[nx * ny :]
    rows, share = parts[0].shape
    for dx in range(nx):
        for dy in range(ny):
            full[at(place.y_before(dy), rows), at(place.x_before(dx), share)] = parts[dx * ny + dy][...]
    first = (place.y() == 0).astype(F32)
    out[...] = (two_halves(full, own, sibling) + bias[...] * first).astype(BF16)


def up_kernel(place, *refs):
    ny, nz = place.ny, place.nz
    toks = refs[:ny]
    gathered = refs[ny : ny + nz]
    gain, shift, own, sibling, bias, out, mid_out, proj, normed, flat = refs[ny + nz :]
    group, steps, _ = toks[0].shape
    rows = group * steps
    cols = gathered[0].shape[2]
    for dz in range(nz):
        proj[:, at(place.z_before(dz), place.nx * cols)] = side_by_side(gathered[dz], 0, cols)
    for j in range(ny):
        here = at(place.y_before(j), rows)
        for i in range(group):
            flat[i * steps : (i + 1) * steps, :] = toks[j][i].astype(F32)
        mid = flat[...] + proj[here, :]
        if j == 0:
            mid_out[...] = mid
        normed[here, :] = layer_norm(mid, gain[...], shift[...]).astype(BF16)
    first = (place.y() == 0).astype(F32)
    out[...] = (two_halves(normed, own, sibling) + bias[...] * first).astype(BF16)


def down_kernel(place, *refs):
    nx, ny = place.nx, place.ny
    parts = refs[:ny]
    own, sibling = refs[ny : ny + 2]
    outs = refs[ny + 2 : ny + 2 + nx]
    feed = refs[-1]
    total = sum(p[...].astype(F32) for p in parts)
    hidden = (0.5 * total * (1.0 + lax.erf(total * 0.5**0.5))).astype(BF16)
    ncols = own.shape[1]
    feed[:, at(place.core(), ncols)] = dot(hidden, own[...])
    feed[:, at(1 - place.core(), ncols)] = dot(hidden, sibling[...])
    width = outs[0].shape[1]
    for dx in range(nx):
        outs[dx][...] = feed[:, at(place.x_after(dx), width)].astype(BF16)


def add_x_kernel(place, *refs):
    refs[-1][...] = sum(r[...].astype(F32) for r in refs[:-1]).astype(BF16)


def add_z_kernel(place, *refs):
    outs, total = refs[place.nz : -1], refs[-1]
    total[...] = sum(r[...].astype(F32) for r in refs[: place.nz])
    rows = outs[0].shape[0]
    for dy in range(place.ny):
        outs[dy][...] = total[at(lax.rem(place.y() + dy, place.ny), rows), :].astype(BF16)


def last_kernel(place, *refs):
    nx, ny = place.nx, place.ny
    parts = refs[: nx * ny]
    mid, bias, out, full = refs[nx * ny :]
    group, steps, _ = out.shape
    width = parts[0].shape[1]
    for dx in range(nx):
        for dy in range(ny):
            block = place.y_before(dy) * nx + place.x_before(dx)
            full[:, at(block, width)] = parts[dx * ny + dy][...].astype(F32)
    result = mid[...] + full[...] + bias[...]
    for i in range(group):
        out[i] = result[i * steps : (i + 1) * steps].astype(BF16)


def shape(sizes, kind=BF16):
    return jax.ShapeDtypeStruct(tuple(sizes), kind)


def body(
    tokens,
    lengths,
    cache_keys,
    cache_values,
    norm1_gain,
    norm1_bias,
    w_query,
    b_query,
    w_key,
    b_key,
    w_value,
    b_value,
    w_out,
    b_out,
    norm2_gain,
    norm2_bias,
    w_up,
    b_up,
    w_down,
    b_down,
):
    place = Place(lax.axis_size("seq"), lax.axis_size("req"))
    nx, ny = place.nx, place.ny
    group, steps, width = tokens.shape
    slots = cache_keys.shape[1]
    rows = group * steps
    heads = width // HEAD
    share = width // nx
    bind = functools.partial

    def row(vector):
        return vector.reshape(1, -1)

    def spread(by_dy):
        return [
            by_dy[dy] if dx == 0 and dy == 0 else place.move(by_dy[dy], dx, dy)
            for dx in range(nx)
            for dy in range(ny)
        ]

    toks = [tokens] + [place.move(tokens, dy=dy) for dy in range(1, ny)]
    w_qkv = jnp.concatenate([w_query, w_key, w_value], axis=1)
    w_qkv_sibling = place.move(w_qkv, dc=1)
    b_qkv = jnp.concatenate([b_query, b_key, b_value])
    parts = call(
        bind(qkv_kernel, place),
        "norm_qkv",
        [*toks, row(norm1_gain), row(norm1_bias), w_qkv, w_qkv_sibling, row(b_qkv)],
        [shape((rows, w_qkv.shape[1]))] * ny,
        scratch=[pltpu.VMEM((ny * rows, width), F32), pltpu.VMEM((ny * rows, width), BF16)],
    )
    w_out_sibling = place.move(w_out, dc=1)
    w_up_sibling = place.move(w_up, dc=1)
    w_down_sibling = place.move(w_down, dc=1)
    qkv = call(
        bind(add_columns_kernel, place), "add_qkv", spread(parts), shape((nx, rows, w_qkv.shape[1]))
    )
    new_keys, new_values, *messages = call(
        bind(attention_kernel, place, heads),
        "attention",
        [*place.gather_z(qkv), lengths, cache_keys, cache_values],
        [shape(cache_keys.shape), shape(cache_values.shape)] + [shape((rows, share + LANES))] * nx,
        in_specs=[VMEM] * place.nz + [SMEM, ANY, ANY],
        out_specs=[ANY, ANY] + [VMEM] * nx,
        scratch=[
            pltpu.VMEM((group, steps, width), F32),
            pltpu.VMEM((group, steps, width), F32),
            pltpu.VMEM((group, steps, width), F32),
            pltpu.VMEM((group, steps, width), F32),
            pltpu.VMEM((group, steps, LANES), F32),
            pltpu.VMEM((rows, width), F32),
            pltpu.VMEM((rows, LANES), F32),
            pltpu.VMEM((steps * heads, width), F32),
            pltpu.VMEM((group, slots, width), BF16),
            pltpu.VMEM((group, slots, width), BF16),
            pltpu.SemaphoreType.DMA((2, group)),
            pltpu.SemaphoreType.DMA((2, group)),
        ],
    )
    messages = [messages[0]] + [place.move(messages[dx], dx=dx) for dx in range(1, nx)]
    merged = call(
        bind(merge_x_kernel, place, heads), "merge_x", messages, shape((rows, share + LANES))
    )
    attn = call(
        bind(merge_z_kernel, place, heads), "merge_z", place.gather_z(merged), shape((rows, share))
    )
    out_part = call(
        bind(out_kernel, place),
        "out",
        [*spread([attn] * ny), w_out, w_out_sibling, row(b_out)],
        shape((ny * rows, w_out.shape[1])),
        scratch=[pltpu.VMEM((ny * rows, width), BF16)],
    )
    projected = call(
        bind(add_columns_kernel, place),
        "add_out",
        spread([out_part] * ny),
        shape((nx, ny * rows, w_out.shape[1])),
    )
    up_part, mid = call(
        bind(up_kernel, place),
        "norm_up",
        [
            *toks,
            *place.gather_z(projected),
            row(norm2_gain),
            row(norm2_bias),
            w_up,
            w_up_sibling,
            row(b_up),
        ],
        [shape((ny * rows, w_up.shape[1])), shape((rows, width), F32)],
        scratch=[
            pltpu.VMEM((ny * rows, width), F32),
            pltpu.VMEM((ny * rows, width), BF16),
            pltpu.VMEM((rows, width), F32),
        ],
    )
    up_parts = [up_part] + [place.move(up_part, dy=dy) for dy in range(1, ny)]
    piece = CORES * w_down.shape[1] // nx
    feeds = call(
        bind(down_kernel, place),
        "gelu_down",
        [*up_parts, w_down, w_down_sibling],
        [shape((ny * rows, piece))] * nx,
        scratch=[pltpu.VMEM((ny * rows, CORES * w_down.shape[1]), F32)],
    )
    feeds = [feeds[0]] + [place.move(feeds[dx], dx=dx) for dx in range(1, nx)]
    feed = call(bind(add_x_kernel, place), "add_x", feeds, shape((ny * rows, piece)))
    summed = call(
        bind(add_z_kernel, place),
        "add_z",
        place.gather_z(feed),
        [shape((rows, piece))] * ny,
        scratch=[pltpu.VMEM((ny * rows, piece), F32)],
    )
    hidden_out = call(
        bind(last_kernel, place),
        "last",
        [*spread(summed), mid, row(b_down)],
        shape(tokens.shape),
        scratch=[pltpu.VMEM((rows, width), F32)],
    )
    return (hidden_out, new_keys, new_values)


def solution(mesh):
    in_specs = (
        P("req", None, None),
        P("req"),
        P("req", "seq", None),
        P("req", "seq", None),
        P(),
        P(),
        P("req", "seq"),
        P("seq"),
        P("req", "seq"),
        P("seq"),
        P("req", "seq"),
        P("seq"),
        P("req", "seq"),
        P("seq"),
        P(),
        P(),
        P("req", "seq"),
        P("seq"),
        P("seq", "req"),
        P(),
    )
    out_specs = (P("req", None, None), P("req", "seq", None), P("req", "seq", None))
    return jax.shard_map(body, mesh=mesh, in_specs=in_specs, out_specs=out_specs, check_vma=False)
```

```python
import functools

import jax
import jax.numpy as jnp
from jax import lax
from jax.experimental import pallas as pl
from jax.experimental.pallas import tpu as pltpu
from jax.sharding import PartitionSpec as P

HEAD = 128
LANES = 128
CORES = 2
BF16 = jnp.bfloat16
F32 = jnp.float32
VMEM = pl.BlockSpec(memory_space=pltpu.VMEM)
SMEM = pl.BlockSpec(memory_space=pltpu.SMEM)
HBM = pl.BlockSpec(memory_space=pltpu.HBM)


class Place:
    def __init__(self, seqs, reqs):
        self.ny = reqs // CORES
        self.nx = self.ny
        self.nz = seqs // self.nx
        self.seqs = seqs

    def x(self):
        return lax.rem(lax.axis_index("seq"), self.nx)

    def y(self):
        return lax.div(lax.axis_index("req"), CORES)

    def core(self):
        return lax.rem(lax.axis_index("req"), CORES)

    def x_before(self, dx):
        return lax.rem(self.x() + self.nx - dx, self.nx)

    def x_after(self, dx):
        return lax.rem(self.x() + dx, self.nx)

    def y_before(self, dy):
        return lax.rem(self.y() + self.ny - dy, self.ny)

    def z_before(self, dz):
        return lax.rem(lax.div(lax.axis_index("seq"), self.nx) + self.nz - dz, self.nz)

    def move(self, value, dx=0, dy=0, dc=0, dz=0):
        pairs = []
        for z in range(self.nz):
            for x in range(self.nx):
                for y in range(self.ny):
                    for c in range(CORES):
                        to_x, to_y, to_c = (x + dx) % self.nx, (y + dy) % self.ny, (c + dc) % CORES
                        to_z = (z + dz) % self.nz
                        pairs.append(
                            (
                                ((z * self.nx + x) * self.ny + y) * CORES + c,
                                ((to_z * self.nx + to_x) * self.ny + to_y) * CORES + to_c,
                            )
                        )
        return lax.ppermute(value, ("seq", "req"), pairs)

    def transpose(self, value, k):
        n = self.nx
        pairs = []
        for z in range(self.nz):
            for x in range(n):
                for y in range(n):
                    for c in range(CORES):
                        pairs.append(
                            (
                                ((z * n + x) * n + y) * CORES + c,
                                ((z * n + y) * n + (x - k) % n) * CORES + c,
                            )
                        )
        return lax.ppermute(value, ("seq", "req"), pairs)

    def gather_z(self, value):
        return [value] + [self.move(value, dz=dz) for dz in range(1, self.nz)]


def layer_norm(values, gain, shift):
    center = values - jnp.mean(values, axis=-1, keepdims=True)
    spread = jnp.mean(center * center, axis=-1, keepdims=True)
    return center * lax.rsqrt(spread + 1e-05) * gain + shift


def dot(a, b):
    return jnp.dot(a, b, preferred_element_type=F32)


def at(index, size):
    return pl.ds(pl.multiple_of(index * size, size), size)


def call(kernel, name, ins, outs, in_specs=None, out_specs=None, scratch=()):
    single = not isinstance(outs, (list, tuple))
    specs = out_specs or (VMEM if single else [VMEM] * len(outs))
    return pl.pallas_call(
        kernel,
        name=name,
        out_shape=outs,
        in_specs=in_specs or [VMEM] * len(ins),
        out_specs=specs,
        scratch_shapes=list(scratch),
        compiler_params=pltpu.CompilerParams(vmem_limit_bytes=20 * 1024 * 1024),
    )(*ins)


def side_by_side(blocks, start, size):
    return jnp.concatenate(
        [blocks[x, :, start : start + size].astype(F32) for x in range(blocks.shape[0])], axis=1
    )


def two_halves(rows_by_k, own, sibling):
    depth = own.shape[0]
    req = lax.axis_index("req")
    other = req + 1 - 2 * lax.rem(req, CORES)
    return dot(rows_by_k[:, at(req, depth)], own[...]) + dot(
        rows_by_k[:, at(other, depth)], sibling[...]
    )


def flatten(block, flat, start):
    group, steps, _ = block.shape
    for i in range(group):
        flat[start + i * steps : start + (i + 1) * steps, :] = block[i].astype(F32)


def norm_kernel(tokens, gain, shift, out, flat):
    flatten(tokens, flat, 0)
    out[...] = layer_norm(flat[...], gain[...], shift[...]).astype(BF16)


def qkv_kernel(place, *refs):
    ny = place.ny
    mine = refs[0]
    toks = refs[1:ny]
    gain, shift = refs[ny : ny + 2]
    weights = refs[ny + 2 : ny + 8]
    biases = refs[ny + 8 : ny + 11]
    outs = refs[ny + 11 : 2 * ny + 11]
    flat, normed = refs[2 * ny + 11 :]
    rows = mine.shape[0]
    normed[:rows, :] = mine[...]
    for j, tok in enumerate(toks):
        flatten(tok, flat, j * rows)
    normed[rows:, :] = layer_norm(flat[...], gain[...], shift[...]).astype(BF16)
    cols = weights[0].shape[1]
    for k in range(3):
        acc = two_halves(normed, weights[2 * k], weights[2 * k + 1])
        for j in range(ny):
            part = acc[j * rows : (j + 1) * rows]
            if j == 0:
                part = part + biases[k][...]
            outs[(ny - j) % ny][:, k * cols : (k + 1) * cols] = part.astype(BF16)


def add_columns_kernel(place, *refs):
    out = refs[-1]
    for dx in range(place.nx):
        total = refs[dx * place.ny][...].astype(F32)
        for dy in range(1, place.ny):
            total = total + refs[dx * place.ny + dy][...].astype(F32)
        out[place.x_before(dx)] = total.astype(BF16)


def split_three(value):
    first = value.astype(BF16).astype(F32)
    rest = value - first
    second = rest.astype(BF16).astype(F32)
    return first, second, rest - second


def turn(value, by):
    return pltpu.roll(value, by % LANES, 1)


def attention_kernel(place, heads, steps, *refs):
    nx, nz = place.nx, place.nz
    gathered = refs[:nz]
    lengths, keys_in, values_in, keys_out, values_out = refs[nz : nz + 5]
    messages = refs[nz + 5 : nz + 5 + nx]
    qs, ks, vs, scores, part, stats, keys, values, in_sems, out_sems = refs[nz + 5 + nx :]
    group, slots, width = keys.shape
    cols = width // place.seqs
    seq = lax.axis_index("seq")

    def copies(sources, targets, sems, i):
        return [
            pltpu.make_async_copy(source.at[i], target.at[i], sems.at[k, i])
            for k, (source, target) in enumerate(zip(sources, targets))
        ]

    def coming(i):
        return copies((keys_in, values_in), (keys, values), in_sems, i)

    def going(i):
        return copies((keys, values), (keys_out, values_out), out_sems, i)

    for i in range(group):
        for copy in coming(i):
            copy.start()
    for dz in range(nz):
        span = at(place.z_before(dz), nx * cols)
        for k, target in enumerate((qs, ks, vs)):
            target[:, span] = side_by_side(gathered[dz], k * cols, cols)
    window = min(32, slots)
    for i in range(group):
        base = lengths[i] - seq * slots
        for copy in coming(i):
            copy.wait()

        @pl.when((base > -steps) & (base < slots))
        def _():
            start = jnp.clip(lax.div(jnp.maximum(base, 0), 16) * 16, 0, slots - window)
            here = pl.ds(pl.multiple_of(start, 16), window)
            slot = start + lax.broadcasted_iota(jnp.int32, (window, width), 0)
            for target, fresh in ((keys, ks), (values, vs)):
                block = target[i, here, :].astype(F32)
                for t in range(steps):
                    at_row = fresh[i * steps + t : i * steps + t + 1, :]
                    block = jnp.where(slot == base + t, at_row, block)
                target[i, here, :] = block.astype(BF16)

        for copy in going(i):
            copy.start()

    pack = max(1, min(group, 256 // slots))
    rows = pack * steps
    tile = 2 * HEAD
    side = lax.rem(lax.div(lax.broadcasted_iota(jnp.int32, (rows, width), 1), HEAD), 2)
    left = lax.broadcasted_iota(jnp.int32, (rows, tile), 1) < HEAD
    many = heads * rows
    row = lax.broadcasted_iota(jnp.int32, (many, pack * slots), 0)
    column = lax.broadcasted_iota(jnp.int32, (many, pack * slots), 1)
    owner = lax.div(lax.rem(row, rows), steps)
    step = lax.rem(row, steps)
    position = seq * slots + lax.rem(column, slots)
    same = owner == lax.div(column, slots)
    lane = lax.broadcasted_iota(jnp.int32, (rows, LANES), 1)
    for g in range(group // pack):
        mine = slice(g * rows, (g + 1) * rows)
        query = qs[mine, :]
        pair = jnp.concatenate(
            [jnp.where(side == 0, query, 0.0), jnp.where(side == 1, query, 0.0)], axis=0
        ).astype(BF16)
        these = slice(g * pack, (g + 1) * pack)
        key = keys[these].reshape(pack * slots, width)
        value = values[these].reshape(pack * slots, width)
        for j in range(heads // 2):
            span = slice(j * tile, (j + 1) * tile)
            scores[j * 2 * rows : (j + 1) * 2 * rows, :] = lax.dot_general(
                pair[:, span], key[:, span], (((1,), (1,)), ((), ())), preferred_element_type=F32
            )
        limit = step
        for k in range(pack):
            limit = jnp.where(owner == k, step + lengths[g * pack + k], limit)
        valid = same & (position <= limit)
        masked = jnp.where(valid, scores[...] * HEAD ** (-0.5), -1e30)
        peak = jnp.max(masked, axis=-1, keepdims=True)
        expo = jnp.where(valid, jnp.exp(masked - peak), 0.0)
        total = jnp.sum(expo, axis=-1, keepdims=True)
        probs = expo.astype(BF16)
        for j in range(heads // 2):
            span = slice(j * tile, (j + 1) * tile)
            mixed = dot(probs[j * 2 * rows : (j + 1) * 2 * rows], value[:, span])
            part[mine, span] = jnp.where(left, mixed[:rows], mixed[rows:])
        line = jnp.zeros((rows, LANES), F32)
        for k, piece in enumerate(split_three(peak) + split_three(total)[:2]):
            for h in range(heads):
                line = jnp.where(lane == k * heads + h, piece[h * rows : (h + 1) * rows], line)
        stats[mine, :] = line
    share = width // nx
    for dx in range(nx):
        to = place.x_after(dx)
        messages[dx][:, :share] = part[:, at(to, share)].astype(BF16)
        messages[dx][:, share:] = pltpu.roll(
            stats[...], lax.rem(LANES - to * (heads // nx), LANES), 1
        ).astype(BF16)
    for i in range(group):
        for copy in going(i):
            copy.wait()


def expand(factor, count):
    rows = factor.shape[0]
    return jnp.concatenate(
        [jnp.broadcast_to(factor[:, h : h + 1], (rows, HEAD)) for h in range(count)], axis=1
    )


def merge(messages, heads, share):
    peaks, totals = [], []
    for message in messages:
        stats = message[:, share:].astype(F32)
        peaks.append(stats + turn(stats, -heads) + turn(stats, -2 * heads))
        totals.append(turn(stats, -3 * heads) + turn(stats, -4 * heads))
    peak = functools.reduce(jnp.maximum, peaks)
    scales = [jnp.exp(p - peak) for p in peaks]
    total = sum(t * s for t, s in zip(totals, scales))
    return peak, total, scales


def merge_x_kernel(place, heads, *refs):
    share = refs[0].shape[1] - LANES
    count = share // HEAD
    out = refs[-1]
    messages = [r[...] for r in refs[:-1]]
    peak, total, scales = merge(messages, heads, share)
    out[:, :share] = sum(
        m[:, :share].astype(F32) * expand(s, count) for m, s in zip(messages, scales)
    ).astype(BF16)
    lane = lax.broadcasted_iota(jnp.int32, peak.shape, 1)
    tile = jnp.zeros_like(peak)
    for k, piece in enumerate(split_three(peak) + split_three(total)[:2]):
        tile = tile + turn(jnp.where(lane < count, piece, 0.0), k * heads)
    out[:, share:] = tile.astype(BF16)


def merge_z_kernel(place, heads, *refs):
    share = refs[0].shape[1] - LANES
    count = share // HEAD
    out = refs[-1]
    messages = [r[...] for r in refs[:-1]]
    _, total, scales = merge(messages, heads, share)
    out[...] = sum(
        m[:, :share].astype(F32) * expand(s / total, count) for m, s in zip(messages, scales)
    ).astype(BF16)


def out_kernel(place, attn, *refs):
    nx = place.nx
    weights = refs[: 2 * nx]
    bias, out, total = refs[2 * nx :]
    depth = weights[0].shape[0]
    core = place.core()
    for k in range(nx):
        block = lax.rem(place.y() + k, nx)
        total[block] = dot(attn[:, at(core, depth)], weights[2 * k][...]) + dot(
            attn[:, at(1 - core, depth)], weights[2 * k + 1][...]
        )
    total[place.x()] = total[place.x()] + bias[...]
    out[...] = total[...].astype(BF16)


def add_out_kernel(place, *refs):
    out = refs[-1]
    for dy in range(place.ny):
        total = refs[dy][...].astype(F32)
        for dx in range(1, place.nx):
            total = total + refs[dx * place.ny + dy][...].astype(F32)
        out[place.y_before(dy)] = total.astype(BF16)


def up_kernel(place, *refs):
    ny, nz = place.ny, place.nz
    toks = refs[:ny]
    gathered = refs[ny : ny + nz]
    gain, shift, own, sibling, bias, out, mid_out, proj, normed, flat = refs[ny + nz :]
    group, steps, _ = toks[0].shape
    rows = group * steps
    cols = gathered[0].shape[3]
    for dz in range(nz):
        span = at(place.z_before(dz), place.nx * cols)
        for y in range(ny):
            proj[y * rows : (y + 1) * rows, span] = side_by_side(gathered[dz].at[y], 0, cols)
    for j in range(ny):
        here = at(place.y_before(j), rows)
        flatten(toks[j], flat, 0)
        mid = flat[...] + proj[here, :]
        if j == 0:
            mid_out[...] = mid
        normed[here, :] = layer_norm(mid, gain[...], shift[...]).astype(BF16)
    first = (place.y() == 0).astype(F32)
    out[...] = (two_halves(normed, own, sibling) + bias[...] * first).astype(BF16)


def down_kernel(place, *refs):
    nx, ny = place.nx, place.ny
    parts = refs[:ny]
    own, sibling = refs[ny : ny + 2]
    outs = refs[ny + 2 : ny + 2 + nx]
    feed = refs[-1]
    total = sum(p[...].astype(F32) for p in parts)
    hidden = (0.5 * total * (1.0 + lax.erf(total * 0.5**0.5))).astype(BF16)
    ncols = own.shape[1]
    feed[:, at(place.core(), ncols)] = dot(hidden, own[...])
    feed[:, at(1 - place.core(), ncols)] = dot(hidden, sibling[...])
    width = outs[0].shape[1]
    for dx in range(nx):
        outs[dx][...] = feed[:, at(place.x_after(dx), width)].astype(BF16)


def add_x_kernel(place, *refs):
    refs[-1][...] = sum(r[...].astype(F32) for r in refs[:-1]).astype(BF16)


def add_z_kernel(place, *refs):
    outs, total = refs[place.nz : -1], refs[-1]
    total[...] = sum(r[...].astype(F32) for r in refs[: place.nz])
    rows = outs[0].shape[0]
    for dy in range(place.ny):
        outs[dy][...] = total[at(lax.rem(place.y() + dy, place.ny), rows), :].astype(BF16)


def last_kernel(place, *refs):
    nx, ny = place.nx, place.ny
    parts = refs[: nx * ny]
    mid, bias, out, full = refs[nx * ny :]
    group, steps, _ = out.shape
    width = parts[0].shape[1]
    for dx in range(nx):
        for dy in range(ny):
            block = place.y_before(dy) * nx + place.x_before(dx)
            full[:, at(block, width)] = parts[dx * ny + dy][...].astype(F32)
    result = mid[...] + full[...] + bias[...]
    for i in range(group):
        out[i] = result[i * steps : (i + 1) * steps].astype(BF16)


def shape(sizes, kind=BF16):
    return jax.ShapeDtypeStruct(tuple(sizes), kind)


def body(
    tokens,
    lengths,
    cache_keys,
    cache_values,
    norm1_gain,
    norm1_bias,
    w_query,
    b_query,
    w_key,
    b_key,
    w_value,
    b_value,
    w_out,
    b_out,
    norm2_gain,
    norm2_bias,
    w_up,
    b_up,
    w_down,
    b_down,
):
    place = Place(lax.axis_size("seq"), lax.axis_size("req"))
    nx, ny = place.nx, place.ny
    group, steps, width = tokens.shape
    slots = cache_keys.shape[1]
    rows = group * steps
    heads = width // HEAD
    share = width // nx
    bind = functools.partial

    def row(vector):
        return vector.reshape(1, -1)

    def spread(by_dy):
        return [
            by_dy[dy] if dx == 0 and dy == 0 else place.move(by_dy[dy], dx, dy)
            for dx in range(nx)
            for dy in range(ny)
        ]

    toks = [tokens] + [place.move(tokens, dy=dy) for dy in range(1, ny)]
    cols = w_query.shape[1]
    weights = []
    for weight in (w_query, w_key, w_value):
        weights += [weight, place.move(weight, dc=1)]
    gain, shift = row(norm1_gain), row(norm1_bias)
    normed = call(
        norm_kernel,
        "norm",
        [tokens, gain, shift],
        shape((rows, width)),
        scratch=[pltpu.VMEM((rows, width), F32)],
    )
    parts = call(
        bind(qkv_kernel, place),
        "norm_qkv",
        [normed, *toks[1:], gain, shift, *weights, row(b_query), row(b_key), row(b_value)],
        [shape((rows, 3 * cols))] * ny,
        scratch=[pltpu.VMEM(((ny - 1) * rows, width), F32), pltpu.VMEM((ny * rows, width), BF16)],
    )
    w_outs = []
    for k in range(nx):
        block = place.transpose(w_out, k)
        w_outs += [block, place.move(block, dc=1)]
    w_up_sibling = place.move(w_up, dc=1)
    w_down_sibling = place.move(w_down, dc=1)
    qkv = call(
        bind(add_columns_kernel, place), "add_qkv", spread(parts), shape((nx, rows, 3 * cols))
    )

    pack = max(1, min(group, 256 // slots))
    new_keys, new_values, *messages = call(
        bind(attention_kernel, place, heads, steps),
        "attention",
        [*place.gather_z(qkv), lengths, cache_keys, cache_values],
        [shape(cache_keys.shape), shape(cache_values.shape)] + [shape((rows, share + LANES))] * nx,
        in_specs=[VMEM] * place.nz + [SMEM, HBM, HBM],
        out_specs=[HBM, HBM] + [VMEM] * nx,
        scratch=[
            pltpu.VMEM((rows, width), F32),
            pltpu.VMEM((rows, width), F32),
            pltpu.VMEM((rows, width), F32),
            pltpu.VMEM((heads * pack * steps, pack * slots), F32),
            pltpu.VMEM((rows, width), F32),
            pltpu.VMEM((rows, LANES), F32),
            pltpu.VMEM(cache_keys.shape, BF16),
            pltpu.VMEM(cache_keys.shape, BF16),
            pltpu.SemaphoreType.DMA((2, group)),
            pltpu.SemaphoreType.DMA((2, group)),
        ],
    )
    messages = [messages[0]] + [place.move(messages[dx], dx=dx) for dx in range(1, nx)]
    merged = call(
        bind(merge_x_kernel, place, heads), "merge_x", messages, shape((rows, share + LANES))
    )
    attn = call(
        bind(merge_z_kernel, place, heads), "merge_z", place.gather_z(merged), shape((rows, share))
    )
    out_part = call(
        bind(out_kernel, place),
        "out",
        [attn, *w_outs, row(b_out)],
        shape((nx, rows, cols)),
        scratch=[pltpu.VMEM((nx, rows, cols), F32)],
    )
    projected = call(
        bind(add_out_kernel, place),
        "add_out",
        spread([out_part] * ny),
        shape((ny, nx, rows, cols)),
    )
    up_part, mid = call(
        bind(up_kernel, place),
        "norm_up",
        [
            *toks,
            *place.gather_z(projected),
            row(norm2_gain),
            row(norm2_bias),
            w_up,
            w_up_sibling,
            row(b_up),
        ],
        [shape((ny * rows, w_up.shape[1])), shape((rows, width), F32)],
        scratch=[
            pltpu.VMEM((ny * rows, width), F32),
            pltpu.VMEM((ny * rows, width), BF16),
            pltpu.VMEM((rows, width), F32),
        ],
    )
    up_parts = [up_part] + [place.move(up_part, dy=dy) for dy in range(1, ny)]
    piece = CORES * w_down.shape[1] // nx
    feeds = call(
        bind(down_kernel, place),
        "gelu_down",
        [*up_parts, w_down, w_down_sibling],
        [shape((ny * rows, piece))] * nx,
        scratch=[pltpu.VMEM((ny * rows, CORES * w_down.shape[1]), F32)],
    )
    feeds = [feeds[0]] + [place.move(feeds[dx], dx=dx) for dx in range(1, nx)]
    feed = call(bind(add_x_kernel, place), "add_x", feeds, shape((ny * rows, piece)))
    summed = call(
        bind(add_z_kernel, place),
        "add_z",
        place.gather_z(feed),
        [shape((rows, piece))] * ny,
        scratch=[pltpu.VMEM((ny * rows, piece), F32)],
    )
    hidden_out = call(
        bind(last_kernel, place),
        "last",
        [*spread(summed), mid, row(b_down)],
        shape(tokens.shape),
        scratch=[pltpu.VMEM((rows, width), F32)],
    )
    return (hidden_out, new_keys, new_values)


def solution(mesh):
    in_specs = (
        P("req", None, None),
        P("req"),
        P("req", "seq", None),
        P("req", "seq", None),
        P(),
        P(),
        P("req", "seq"),
        P("seq"),
        P("req", "seq"),
        P("seq"),
        P("req", "seq"),
        P("seq"),
        P("req", "seq"),
        P("seq"),
        P(),
        P(),
        P("req", "seq"),
        P("seq"),
        P("seq", "req"),
        P(),
    )
    out_specs = (P("req", None, None), P("req", "seq", None), P("req", "seq", None))
    return jax.shard_map(body, mesh=mesh, in_specs=in_specs, out_specs=out_specs, check_vma=False)
```

```python
import functools

import jax
import jax.numpy as jnp
from jax import lax
from jax.experimental import pallas as pl
from jax.experimental.pallas import tpu as pltpu
from jax.sharding import PartitionSpec as P

HEAD = 128
LANES = 128
CORES = 2
BF16 = jnp.bfloat16
F32 = jnp.float32
VMEM = pl.BlockSpec(memory_space=pltpu.VMEM)
SMEM = pl.BlockSpec(memory_space=pltpu.SMEM)
HBM = pl.BlockSpec(memory_space=pltpu.HBM)


class Place:
    def __init__(self, seqs, reqs):
        self.ny = reqs // CORES
        self.nx = self.ny
        self.nz = seqs // self.nx
        self.seqs = seqs

    def x(self):
        return lax.rem(lax.axis_index("seq"), self.nx)

    def y(self):
        return lax.div(lax.axis_index("req"), CORES)

    def core(self):
        return lax.rem(lax.axis_index("req"), CORES)

    def x_before(self, dx):
        return lax.rem(self.x() + self.nx - dx, self.nx)

    def x_after(self, dx):
        return lax.rem(self.x() + dx, self.nx)

    def y_before(self, dy):
        return lax.rem(self.y() + self.ny - dy, self.ny)

    def z_partner(self, dz):
        return lax.bitwise_xor(lax.div(lax.axis_index("seq"), self.nx), dz)

    def move(self, value, dx=0, dy=0, dc=0, dz=0):
        pairs = []
        for z in range(self.nz):
            for x in range(self.nx):
                for y in range(self.ny):
                    for c in range(CORES):
                        to_x, to_y, to_c = (x + dx) % self.nx, (y + dy) % self.ny, (c + dc) % CORES
                        to_z = z ^ dz
                        pairs.append(
                            (
                                ((z * self.nx + x) * self.ny + y) * CORES + c,
                                ((to_z * self.nx + to_x) * self.ny + to_y) * CORES + to_c,
                            )
                        )
        return lax.ppermute(value, ("seq", "req"), pairs)

    def transpose(self, value, k):
        n = self.nx
        pairs = []
        for z in range(self.nz):
            for x in range(n):
                for y in range(n):
                    for c in range(CORES):
                        pairs.append(
                            (
                                ((z * n + x) * n + y) * CORES + c,
                                ((z * n + y) * n + (x - k) % n) * CORES + c,
                            )
                        )
        return lax.ppermute(value, ("seq", "req"), pairs)

    def gather_z(self, value):
        return [value] + [self.move(value, dz=dz) for dz in range(1, self.nz)]


def layer_norm(values, gain, shift):
    center = values - jnp.mean(values, axis=-1, keepdims=True)
    spread = jnp.mean(center * center, axis=-1, keepdims=True)
    return center * lax.rsqrt(spread + 1e-05) * gain + shift


def dot(a, b):
    return jnp.dot(a, b, preferred_element_type=F32)


def at(index, size):
    return pl.ds(pl.multiple_of(index * size, size), size)


def call(kernel, name, ins, outs, in_specs=None, out_specs=None, scratch=(), moved=2**20, limit=20):
    single = not isinstance(outs, (list, tuple))
    specs = out_specs or (VMEM if single else [VMEM] * len(outs))
    return pl.pallas_call(
        kernel,
        name=name,
        out_shape=outs,
        in_specs=in_specs or [VMEM] * len(ins),
        out_specs=specs,
        scratch_shapes=list(scratch),
        cost_estimate=pl.CostEstimate(flops=0, bytes_accessed=moved, transcendentals=0),
        compiler_params=pltpu.CompilerParams(vmem_limit_bytes=limit * 1024 * 1024),
    )(*ins)


def side_by_side(blocks, start, size):
    return jnp.concatenate(
        [blocks[x, :, start : start + size].astype(F32) for x in range(blocks.shape[0])], axis=1
    )


def two_halves(rows_by_k, own, sibling):
    depth = own.shape[0]
    req = lax.axis_index("req")
    other = req + 1 - 2 * lax.rem(req, CORES)
    return dot(rows_by_k[:, at(req, depth)], own[...]) + dot(
        rows_by_k[:, at(other, depth)], sibling[...]
    )


def flatten(block, flat, start):
    group, steps, _ = block.shape
    for i in range(group):
        flat[start + i * steps : start + (i + 1) * steps, :] = block[i].astype(F32)


def norm_kernel(tokens, scales, *refs):
    count = (len(refs) - 3) // 2
    weights, out, kept = refs[:count], refs[count], refs[count + 1 : 2 * count + 1]
    flat, sems = refs[-2:]
    copies = [
        pltpu.make_async_copy(source, target, sems.at[k])
        for k, (source, target) in enumerate(zip(weights, kept))
    ]
    for copy in copies:
        copy.start()
    width = out.shape[1]
    flatten(tokens, flat, 0)
    out[...] = layer_norm(flat[...], scales[:, :width], scales[:, width:]).astype(BF16)
    for copy in copies:
        copy.wait()


def qkv_kernel(place, *refs):
    ny = place.ny
    mine = refs[0]
    toks = refs[1:ny]
    scales, biases = refs[ny : ny + 2]
    weights = refs[ny + 2 : ny + 8]
    outs = refs[ny + 8 : 2 * ny + 8]
    flat, normed = refs[2 * ny + 8 :]
    rows, width = mine.shape
    normed[:rows, :] = mine[...]
    for j, tok in enumerate(toks):
        flatten(tok, flat, j * rows)
    normed[rows:, :] = layer_norm(flat[...], scales[:, :width], scales[:, width:]).astype(BF16)
    cols = weights[0].shape[1]
    for k in range(3):
        acc = two_halves(normed, weights[k], weights[3 + k])
        for j in range(ny):
            part = acc[j * rows : (j + 1) * rows]
            if j == 0:
                part = part + biases[:, k * cols : (k + 1) * cols]
            outs[(ny - j) % ny][:, k * cols : (k + 1) * cols] = part.astype(BF16)


def add_columns_kernel(place, *refs):
    out = refs[-1]
    for dx in range(place.nx):
        total = refs[dx * place.ny][...].astype(F32)
        for dy in range(1, place.ny):
            total = total + refs[dx * place.ny + dy][...].astype(F32)
        out[place.x_before(dx)] = total.astype(BF16)


def split_three(value):
    first = value.astype(BF16).astype(F32)
    rest = value - first
    second = rest.astype(BF16).astype(F32)
    return first, second, rest - second


def turn(value, by):
    return pltpu.roll(value, by % LANES, 1)


def attention_kernel(place, heads, steps, *refs):
    nx, nz = place.nx, place.nz
    gathered = refs[:nz]
    lengths, keys_in, values_in, keys_out, values_out = refs[nz : nz + 5]
    messages = refs[nz + 5 : nz + 5 + nx]
    qs, ks, vs, scores, part, stats, keys, values, in_sems, out_sems = refs[nz + 5 + nx :]
    group, slots, width = keys.shape
    cols = width // place.seqs
    seq = lax.axis_index("seq")

    def copies(sources, targets, sems, i):
        return [
            pltpu.make_async_copy(source.at[i], target.at[i], sems.at[k, i])
            for k, (source, target) in enumerate(zip(sources, targets))
        ]

    def coming(i):
        return copies((keys_in, values_in), (keys, values), in_sems, i)

    def going(i):
        return copies((keys, values), (keys_out, values_out), out_sems, i)

    for i in range(group):
        for copy in coming(i):
            copy.start()
    for dz in range(nz):
        span = at(place.z_partner(dz), nx * cols)
        for k, target in enumerate((qs, ks, vs)):
            target[:, span] = side_by_side(gathered[dz], k * cols, cols)
    window = min(32, slots)
    for i in range(group):
        base = lengths[i] - seq * slots
        for copy in coming(i):
            copy.wait()

        @pl.when((base > -steps) & (base < slots))
        def _():
            start = jnp.clip(lax.div(jnp.maximum(base, 0), 16) * 16, 0, slots - window)
            here = pl.ds(pl.multiple_of(start, 16), window)
            slot = start + lax.broadcasted_iota(jnp.int32, (window, width), 0)
            for target, fresh in ((keys, ks), (values, vs)):
                block = target[i, here, :].astype(F32)
                for t in range(steps):
                    at_row = fresh[i * steps + t : i * steps + t + 1, :]
                    block = jnp.where(slot == base + t, at_row, block)
                target[i, here, :] = block.astype(BF16)

        for copy in going(i):
            copy.start()

    pack = max(1, min(group, 256 // slots))
    rows = pack * steps
    tile = 2 * HEAD
    side = lax.rem(lax.div(lax.broadcasted_iota(jnp.int32, (rows, width), 1), HEAD), 2)
    left = lax.broadcasted_iota(jnp.int32, (rows, tile), 1) < HEAD
    many = heads * rows
    row = lax.broadcasted_iota(jnp.int32, (many, pack * slots), 0)
    column = lax.broadcasted_iota(jnp.int32, (many, pack * slots), 1)
    owner = lax.div(lax.rem(row, rows), steps)
    step = lax.rem(row, steps)
    position = seq * slots + lax.rem(column, slots)
    same = owner == lax.div(column, slots)
    lane = lax.broadcasted_iota(jnp.int32, (rows, LANES), 1)
    for g in range(group // pack):
        mine = slice(g * rows, (g + 1) * rows)
        query = qs[mine, :]
        pair = jnp.concatenate(
            [jnp.where(side == 0, query, 0.0), jnp.where(side == 1, query, 0.0)], axis=0
        ).astype(BF16)
        these = slice(g * pack, (g + 1) * pack)
        key = keys[these].reshape(pack * slots, width)
        value = values[these].reshape(pack * slots, width)
        for j in range(heads // 2):
            span = slice(j * tile, (j + 1) * tile)
            scores[j * 2 * rows : (j + 1) * 2 * rows, :] = lax.dot_general(
                pair[:, span], key[:, span], (((1,), (1,)), ((), ())), preferred_element_type=F32
            )
        limit = step
        for k in range(pack):
            limit = jnp.where(owner == k, step + lengths[g * pack + k], limit)
        valid = same & (position <= limit)
        masked = jnp.where(valid, scores[...] * HEAD ** (-0.5), -1e30)
        peak = jnp.max(masked, axis=-1, keepdims=True)
        expo = jnp.where(valid, jnp.exp(masked - peak), 0.0)
        total = jnp.sum(expo, axis=-1, keepdims=True)
        probs = expo.astype(BF16)
        for j in range(heads // 2):
            span = slice(j * tile, (j + 1) * tile)
            mixed = dot(probs[j * 2 * rows : (j + 1) * 2 * rows], value[:, span])
            part[mine, span] = jnp.where(left, mixed[:rows], mixed[rows:])
        line = jnp.zeros((rows, LANES), F32)
        for k, piece in enumerate(split_three(peak) + split_three(total)[:2]):
            for h in range(heads):
                line = jnp.where(lane == k * heads + h, piece[h * rows : (h + 1) * rows], line)
        stats[mine, :] = line
    share = width // nx
    for dx in range(nx):
        to = place.x_after(dx)
        messages[dx][:, :share] = part[:, at(to, share)].astype(BF16)
        messages[dx][:, share:] = pltpu.roll(
            stats[...], lax.rem(LANES - to * (heads // nx), LANES), 1
        ).astype(BF16)
    for i in range(group):
        for copy in going(i):
            copy.wait()


def expand(factor, count):
    rows = factor.shape[0]
    return jnp.concatenate(
        [jnp.broadcast_to(factor[:, h : h + 1], (rows, HEAD)) for h in range(count)], axis=1
    )


def merge(messages, heads, share):
    peaks, totals = [], []
    for message in messages:
        stats = message[:, share:].astype(F32)
        peaks.append(stats + turn(stats, -heads) + turn(stats, -2 * heads))
        totals.append(turn(stats, -3 * heads) + turn(stats, -4 * heads))
    peak = functools.reduce(jnp.maximum, peaks)
    scales = [jnp.exp(p - peak) for p in peaks]
    total = sum(t * s for t, s in zip(totals, scales))
    return peak, total, scales


def merge_x_kernel(place, heads, *refs):
    share = refs[0].shape[1] - LANES
    count = share // HEAD
    out = refs[-1]
    messages = [r[...] for r in refs[:-1]]
    peak, total, scales = merge(messages, heads, share)
    out[:, :share] = sum(
        m[:, :share].astype(F32) * expand(s, count) for m, s in zip(messages, scales)
    ).astype(BF16)
    lane = lax.broadcasted_iota(jnp.int32, peak.shape, 1)
    tile = jnp.zeros_like(peak)
    for k, piece in enumerate(split_three(peak) + split_three(total)[:2]):
        tile = tile + turn(jnp.where(lane < count, piece, 0.0), k * heads)
    out[:, share:] = tile.astype(BF16)


def merge_z_kernel(place, heads, *refs):
    share = refs[0].shape[1] - LANES
    count = share // HEAD
    out = refs[-1]
    messages = [r[...] for r in refs[:-1]]
    _, total, scales = merge(messages, heads, share)
    out[...] = sum(
        m[:, :share].astype(F32) * expand(s / total, count) for m, s in zip(messages, scales)
    ).astype(BF16)


def out_kernel(place, attn, *refs):
    nx = place.nx
    weights = refs[: 2 * nx]
    bias, out, total = refs[2 * nx :]
    depth = weights[0].shape[0]
    core = place.core()
    for k in range(nx):
        block = lax.rem(place.y() + k, nx)
        total[block] = dot(attn[:, at(core, depth)], weights[2 * k][...]) + dot(
            attn[:, at(1 - core, depth)], weights[2 * k + 1][...]
        )
    total[place.x()] = total[place.x()] + bias[...]
    out[...] = total[...].astype(BF16)


def add_out_kernel(place, *refs):
    out = refs[-1]
    for dy in range(place.ny):
        total = refs[dy][...].astype(F32)
        for dx in range(1, place.nx):
            total = total + refs[dx * place.ny + dy][...].astype(F32)
        out[place.y_before(dy)] = total.astype(BF16)


def up_kernel(place, *refs):
    ny, nz = place.ny, place.nz
    toks = refs[:ny]
    gathered = refs[ny : ny + nz]
    gain, shift, own, sibling, bias, out, mid_out, proj, normed, flat = refs[ny + nz :]
    group, steps, _ = toks[0].shape
    rows = group * steps
    cols = gathered[0].shape[3]
    for dz in range(nz):
        span = at(place.z_partner(dz), place.nx * cols)
        for y in range(ny):
            proj[y * rows : (y + 1) * rows, span] = side_by_side(gathered[dz].at[y], 0, cols)
    for j in range(ny):
        here = at(place.y_before(j), rows)
        flatten(toks[j], flat, 0)
        mid = flat[...] + proj[here, :]
        if j == 0:
            mid_out[...] = mid
        normed[here, :] = layer_norm(mid, gain[...], shift[...]).astype(BF16)
    first = (place.y() == 0).astype(F32)
    out[...] = (two_halves(normed, own, sibling) + bias[...] * first).astype(BF16)


def down_kernel(place, *refs):
    nx, ny = place.nx, place.ny
    parts = refs[:ny]
    own, sibling = refs[ny : ny + 2]
    outs = refs[ny + 2 : ny + 2 + nx]
    feed = refs[-1]
    total = sum(p[...].astype(F32) for p in parts)
    hidden = (0.5 * total * (1.0 + lax.erf(total * 0.5**0.5))).astype(BF16)
    ncols = own.shape[1]
    feed[:, at(place.core(), ncols)] = dot(hidden, own[...])
    feed[:, at(1 - place.core(), ncols)] = dot(hidden, sibling[...])
    width = outs[0].shape[1]
    for dx in range(nx):
        outs[dx][...] = feed[:, at(place.x_after(dx), width)].astype(BF16)


def add_x_kernel(place, *refs):
    refs[-1][...] = sum(r[...].astype(F32) for r in refs[:-1]).astype(BF16)


def add_z_kernel(place, *refs):
    outs, total = refs[place.nz : -1], refs[-1]
    total[...] = sum(r[...].astype(F32) for r in refs[: place.nz])
    rows = outs[0].shape[0]
    for dy in range(place.ny):
        outs[dy][...] = total[at(lax.rem(place.y() + dy, place.ny), rows), :].astype(BF16)


def last_kernel(place, *refs):
    nx, ny = place.nx, place.ny
    parts = refs[: nx * ny]
    mid, bias, out, full = refs[nx * ny :]
    group, steps, _ = out.shape
    width = parts[0].shape[1]
    for dx in range(nx):
        for dy in range(ny):
            block = place.y_before(dy) * nx + place.x_before(dx)
            full[:, at(block, width)] = parts[dx * ny + dy][...].astype(F32)
    result = mid[...] + full[...] + bias[...]
    for i in range(group):
        out[i] = result[i * steps : (i + 1) * steps].astype(BF16)


def shape(sizes, kind=BF16):
    return jax.ShapeDtypeStruct(tuple(sizes), kind)


def body(
    tokens,
    lengths,
    cache_keys,
    cache_values,
    norm1_gain,
    norm1_bias,
    w_query,
    b_query,
    w_key,
    b_key,
    w_value,
    b_value,
    w_out,
    b_out,
    norm2_gain,
    norm2_bias,
    w_up,
    b_up,
    w_down,
    b_down,
):
    place = Place(lax.axis_size("seq"), lax.axis_size("req"))
    nx, ny = place.nx, place.ny
    group, steps, width = tokens.shape
    slots = cache_keys.shape[1]
    rows = group * steps
    heads = width // HEAD
    share = width // nx
    bind = functools.partial

    def row(vector):
        return vector.reshape(1, -1)

    def spread(by_dy):
        return [
            by_dy[dy] if dx == 0 and dy == 0 else place.move(by_dy[dy], dx, dy)
            for dx in range(nx)
            for dy in range(ny)
        ]

    toks = [tokens] + [place.move(tokens, dy=dy) for dy in range(1, ny)]
    cols = w_query.shape[1]
    own = [w_query, w_key, w_value]
    siblings = [place.move(weight, dc=1) for weight in own]
    scales = row(jnp.concatenate([norm1_gain, norm1_bias]))
    biases = row(jnp.concatenate([b_query, b_key, b_value]))
    normed, *own = call(
        norm_kernel,
        "norm",
        [tokens, scales, *own],
        [shape((rows, width))] + [shape(w.shape) for w in own],
        in_specs=[VMEM] * 2 + [HBM] * 3,
        scratch=[pltpu.VMEM((rows, width), F32), pltpu.SemaphoreType.DMA((3,))],
    )
    parts = call(
        bind(qkv_kernel, place),
        "norm_qkv",
        [normed, *toks[1:], scales, biases, *own, *siblings],
        [shape((rows, 3 * cols))] * ny,
        scratch=[pltpu.VMEM(((ny - 1) * rows, width), F32), pltpu.VMEM((ny * rows, width), BF16)],
    )
    *parts, tied_up, tied_down = lax.optimization_barrier((*parts, w_up, w_down))
    w_up_sibling = place.move(tied_up, dc=1)
    w_down_sibling = place.move(tied_down, dc=1)
    qkv = call(
        bind(add_columns_kernel, place), "add_qkv", spread(parts), shape((nx, rows, 3 * cols))
    )

    qkv, w_up_sibling, w_down_sibling = lax.optimization_barrier(
        (qkv, w_up_sibling, w_down_sibling)
    )
    qkv, tied_w_out = lax.optimization_barrier((qkv, w_out))
    blocks = [place.transpose(tied_w_out, k) for k in range(nx)]
    pack = max(1, min(group, 256 // slots))
    new_keys, new_values, *messages = call(
        bind(attention_kernel, place, heads, steps),
        "attention",
        [*place.gather_z(qkv), lengths, cache_keys, cache_values],
        [shape(cache_keys.shape), shape(cache_values.shape)] + [shape((rows, share + LANES))] * nx,
        in_specs=[VMEM] * place.nz + [SMEM, HBM, HBM],
        out_specs=[HBM, HBM] + [VMEM] * nx,
        scratch=[
            pltpu.VMEM((rows, width), F32),
            pltpu.VMEM((rows, width), F32),
            pltpu.VMEM((rows, width), F32),
            pltpu.VMEM((heads * pack * steps, pack * slots), F32),
            pltpu.VMEM((rows, width), F32),
            pltpu.VMEM((rows, LANES), F32),
            pltpu.VMEM(cache_keys.shape, BF16),
            pltpu.VMEM(cache_keys.shape, BF16),
            pltpu.SemaphoreType.DMA((2, group)),
            pltpu.SemaphoreType.DMA((2, group)),
        ],
        limit=52,
    )
    *messages, blocks = lax.optimization_barrier((*messages, blocks))
    w_outs = []
    for block in blocks:
        w_outs += [block, place.move(block, dc=1)]
    messages = [messages[0]] + [place.move(messages[dx], dx=dx) for dx in range(1, nx)]
    merged = call(
        bind(merge_x_kernel, place, heads), "merge_x", messages, shape((rows, share + LANES))
    )
    merged, *w_outs = lax.optimization_barrier((merged, *w_outs))
    attn = call(
        bind(merge_z_kernel, place, heads), "merge_z", place.gather_z(merged), shape((rows, share))
    )
    out_part = call(
        bind(out_kernel, place),
        "out",
        [attn, *w_outs, row(b_out)],
        shape((nx, rows, cols)),
        scratch=[pltpu.VMEM((nx, rows, cols), F32)],
    )
    projected = call(
        bind(add_out_kernel, place),
        "add_out",
        spread([out_part] * ny),
        shape((ny, nx, rows, cols)),
    )
    up_part, mid = call(
        bind(up_kernel, place),
        "norm_up",
        [
            *toks,
            *place.gather_z(projected),
            row(norm2_gain),
            row(norm2_bias),
            w_up,
            w_up_sibling,
            row(b_up),
        ],
        [shape((ny * rows, w_up.shape[1])), shape((rows, width), F32)],
        scratch=[
            pltpu.VMEM((ny * rows, width), F32),
            pltpu.VMEM((ny * rows, width), BF16),
            pltpu.VMEM((rows, width), F32),
        ],
    )
    up_parts = [up_part] + [place.move(up_part, dy=dy) for dy in range(1, ny)]
    piece = CORES * w_down.shape[1] // nx
    feeds = call(
        bind(down_kernel, place),
        "gelu_down",
        [*up_parts, w_down, w_down_sibling],
        [shape((ny * rows, piece))] * nx,
        scratch=[pltpu.VMEM((ny * rows, CORES * w_down.shape[1]), F32)],
    )
    feeds = [feeds[0]] + [place.move(feeds[dx], dx=dx) for dx in range(1, nx)]
    feed = call(bind(add_x_kernel, place), "add_x", feeds, shape((ny * rows, piece)))
    summed = call(
        bind(add_z_kernel, place),
        "add_z",
        place.gather_z(feed),
        [shape((rows, piece))] * ny,
        scratch=[pltpu.VMEM((ny * rows, piece), F32)],
    )
    hidden_out = call(
        bind(last_kernel, place),
        "last",
        [*spread(summed), mid, row(b_down)],
        shape(tokens.shape),
        scratch=[pltpu.VMEM((rows, width), F32)],
    )
    return (hidden_out, new_keys, new_values)


def solution(mesh):
    in_specs = (
        P("req", None, None),
        P("req"),
        P("req", "seq", None),
        P("req", "seq", None),
        P(),
        P(),
        P("req", "seq"),
        P("seq"),
        P("req", "seq"),
        P("seq"),
        P("req", "seq"),
        P("seq"),
        P("req", "seq"),
        P("seq"),
        P(),
        P(),
        P("req", "seq"),
        P("seq"),
        P("seq", "req"),
        P(),
    )
    out_specs = (P("req", None, None), P("req", "seq", None), P("req", "seq", None))
    return jax.shard_map(body, mesh=mesh, in_specs=in_specs, out_specs=out_specs, check_vma=False)
```

```python
import functools

import jax
import jax.numpy as jnp
from jax import lax
from jax.experimental import pallas as pl
from jax.experimental.pallas import tpu as pltpu
from jax.sharding import PartitionSpec as P

HEAD = 128
LANES = 128
CORES = 2
BF16 = jnp.bfloat16
F32 = jnp.float32
VMEM = pl.BlockSpec(memory_space=pltpu.VMEM)
SMEM = pl.BlockSpec(memory_space=pltpu.SMEM)
HBM = pl.BlockSpec(memory_space=pltpu.HBM)


class Place:
    def __init__(self, seqs, reqs):
        self.ny = reqs // CORES
        self.nx = self.ny
        self.nz = seqs // self.nx
        self.seqs = seqs

    def x(self):
        return lax.rem(lax.axis_index("seq"), self.nx)

    def y(self):
        return lax.div(lax.axis_index("req"), CORES)

    def core(self):
        return lax.rem(lax.axis_index("req"), CORES)

    def x_before(self, dx):
        return lax.rem(self.x() + self.nx - dx, self.nx)

    def x_after(self, dx):
        return lax.rem(self.x() + dx, self.nx)

    def y_before(self, dy):
        return lax.rem(self.y() + self.ny - dy, self.ny)

    def z_partner(self, dz):
        return lax.bitwise_xor(lax.div(lax.axis_index("seq"), self.nx), dz)

    def move(self, value, dx=0, dy=0, dc=0, dz=0):
        pairs = []
        for z in range(self.nz):
            for x in range(self.nx):
                for y in range(self.ny):
                    for c in range(CORES):
                        to_x, to_y, to_c = (x + dx) % self.nx, (y + dy) % self.ny, (c + dc) % CORES
                        to_z = z ^ dz
                        pairs.append(
                            (
                                ((z * self.nx + x) * self.ny + y) * CORES + c,
                                ((to_z * self.nx + to_x) * self.ny + to_y) * CORES + to_c,
                            )
                        )
        return lax.ppermute(value, ("seq", "req"), pairs)

    def transpose(self, value, k):
        n = self.nx
        pairs = []
        for z in range(self.nz):
            for x in range(n):
                for y in range(n):
                    for c in range(CORES):
                        pairs.append(
                            (
                                ((z * n + x) * n + y) * CORES + c,
                                ((z * n + y) * n + (x - k) % n) * CORES + c,
                            )
                        )
        return lax.ppermute(value, ("seq", "req"), pairs)

    def gather_z(self, value):
        return [value] + [self.move(value, dz=dz) for dz in range(1, self.nz)]


def layer_norm(values, gain, shift):
    center = values - jnp.mean(values, axis=-1, keepdims=True)
    spread = jnp.mean(center * center, axis=-1, keepdims=True)
    return center * lax.rsqrt(spread + 1e-05) * gain + shift


def dot(a, b):
    return jnp.dot(a, b, preferred_element_type=F32)


def at(index, size):
    return pl.ds(pl.multiple_of(index * size, size), size)


def call(kernel, name, ins, outs, in_specs=None, out_specs=None, scratch=(), moved=2**20, limit=20):
    single = not isinstance(outs, (list, tuple))
    specs = out_specs or (VMEM if single else [VMEM] * len(outs))
    return pl.pallas_call(
        kernel,
        name=name,
        out_shape=outs,
        in_specs=in_specs or [VMEM] * len(ins),
        out_specs=specs,
        scratch_shapes=list(scratch),
        cost_estimate=pl.CostEstimate(flops=0, bytes_accessed=moved, transcendentals=0),
        compiler_params=pltpu.CompilerParams(vmem_limit_bytes=limit * 1024 * 1024),
    )(*ins)


def side_by_side(blocks, start, size):
    return jnp.concatenate(
        [blocks[x, :, start : start + size].astype(F32) for x in range(blocks.shape[0])], axis=1
    )


def two_halves(rows_by_k, own, sibling):
    depth = own.shape[0]
    req = lax.axis_index("req")
    other = req + 1 - 2 * lax.rem(req, CORES)
    return dot(rows_by_k[:, at(req, depth)], own[...]) + dot(
        rows_by_k[:, at(other, depth)], sibling[...]
    )


def flatten(block, flat, start):
    group, steps, _ = block.shape
    for i in range(group):
        flat[start + i * steps : start + (i + 1) * steps, :] = block[i].astype(F32)


def norm_kernel(tokens, scales, *refs):
    count = (len(refs) - 3) // 2
    weights, out, kept = refs[:count], refs[count], refs[count + 1 : 2 * count + 1]
    flat, sems = refs[-2:]
    copies = [
        pltpu.make_async_copy(source, target, sems.at[k])
        for k, (source, target) in enumerate(zip(weights, kept))
    ]
    for copy in copies:
        copy.start()
    width = out.shape[1]
    flatten(tokens, flat, 0)
    out[...] = layer_norm(flat[...], scales[:, :width], scales[:, width:]).astype(BF16)
    for copy in copies:
        copy.wait()


def qkv_kernel(place, *refs):
    ny = place.ny
    mine = refs[0]
    toks = refs[1:ny]
    scales, biases = refs[ny : ny + 2]
    weights = refs[ny + 2 : ny + 8]
    outs = refs[ny + 8 : 2 * ny + 8]
    flat, normed = refs[2 * ny + 8 :]
    rows, width = mine.shape
    normed[:rows, :] = mine[...]
    for j, tok in enumerate(toks):
        flatten(tok, flat, j * rows)
    normed[rows:, :] = layer_norm(flat[...], scales[:, :width], scales[:, width:]).astype(BF16)
    cols = weights[0].shape[1]
    for k in range(3):
        acc = two_halves(normed, weights[k], weights[3 + k])
        for j in range(ny):
            part = acc[j * rows : (j + 1) * rows]
            if j == 0:
                part = part + biases[:, k * cols : (k + 1) * cols]
            outs[(ny - j) % ny][:, k * cols : (k + 1) * cols] = part.astype(BF16)


def add_columns_kernel(place, *refs):
    out = refs[-1]
    for dx in range(place.nx):
        total = refs[dx * place.ny][...].astype(F32)
        for dy in range(1, place.ny):
            total = total + refs[dx * place.ny + dy][...].astype(F32)
        out[place.x_before(dx)] = total.astype(BF16)


def split_three(value):
    first = value.astype(BF16).astype(F32)
    rest = value - first
    second = rest.astype(BF16).astype(F32)
    return first, second, rest - second


def turn(value, by):
    return pltpu.roll(value, by % LANES, 1)


def attention_kernel(place, heads, steps, *refs):
    nx, nz = place.nx, place.nz
    gathered = refs[:nz]
    lengths, keys_in, values_in, keys_out, values_out = refs[nz : nz + 5]
    messages = refs[nz + 5 : nz + 5 + nx]
    qs, ks, vs, scores, part, stats, keys, values, in_sems, out_sems = refs[nz + 5 + nx :]
    group, slots, width = keys.shape
    cols = width // place.seqs
    seq = lax.axis_index("seq")

    def copies(sources, targets, sems, i):
        return [
            pltpu.make_async_copy(source.at[i], target.at[i], sems.at[k, i])
            for k, (source, target) in enumerate(zip(sources, targets))
        ]

    def coming(i):
        return copies((keys_in, values_in), (keys, values), in_sems, i)

    def going(i):
        return copies((keys, values), (keys_out, values_out), out_sems, i)

    for i in range(group):
        for copy in coming(i):
            copy.start()
    for dz in range(nz):
        span = at(place.z_partner(dz), nx * cols)
        for k, target in enumerate((qs, ks, vs)):
            target[:, span] = side_by_side(gathered[dz], k * cols, cols)
    window = min(32, slots)
    for i in range(group):
        base = lengths[i] - seq * slots
        for copy in coming(i):
            copy.wait()

        @pl.when((base > -steps) & (base < slots))
        def _():
            start = jnp.clip(lax.div(jnp.maximum(base, 0), 16) * 16, 0, slots - window)
            here = pl.ds(pl.multiple_of(start, 16), window)
            slot = start + lax.broadcasted_iota(jnp.int32, (window, width), 0)
            for target, fresh in ((keys, ks), (values, vs)):
                block = target[i, here, :].astype(F32)
                for t in range(steps):
                    at_row = fresh[i * steps + t : i * steps + t + 1, :]
                    block = jnp.where(slot == base + t, at_row, block)
                target[i, here, :] = block.astype(BF16)

        for copy in going(i):
            copy.start()

    pack = max(1, min(group, 256 // slots))
    rows = pack * steps
    tile = 2 * HEAD
    side = lax.rem(lax.div(lax.broadcasted_iota(jnp.int32, (rows, width), 1), HEAD), 2)
    left = lax.broadcasted_iota(jnp.int32, (rows, tile), 1) < HEAD
    many = heads * rows
    row = lax.broadcasted_iota(jnp.int32, (many, pack * slots), 0)
    column = lax.broadcasted_iota(jnp.int32, (many, pack * slots), 1)
    owner = lax.div(lax.rem(row, rows), steps)
    step = lax.rem(row, steps)
    position = seq * slots + lax.rem(column, slots)
    same = owner == lax.div(column, slots)
    lane = lax.broadcasted_iota(jnp.int32, (rows, LANES), 1)
    for g in range(group // pack):
        mine = slice(g * rows, (g + 1) * rows)
        query = qs[mine, :]
        pair = jnp.concatenate(
            [jnp.where(side == 0, query, 0.0), jnp.where(side == 1, query, 0.0)], axis=0
        ).astype(BF16)
        these = slice(g * pack, (g + 1) * pack)
        key = keys[these].reshape(pack * slots, width)
        value = values[these].reshape(pack * slots, width)
        for j in range(heads // 2):
            span = slice(j * tile, (j + 1) * tile)
            scores[j * 2 * rows : (j + 1) * 2 * rows, :] = lax.dot_general(
                pair[:, span], key[:, span], (((1,), (1,)), ((), ())), preferred_element_type=F32
            )
        limit = step
        for k in range(pack):
            limit = jnp.where(owner == k, step + lengths[g * pack + k], limit)
        valid = same & (position <= limit)
        masked = jnp.where(valid, scores[...] * HEAD ** (-0.5), -1e30)
        peak = jnp.max(masked, axis=-1, keepdims=True)
        expo = jnp.where(valid, jnp.exp(masked - peak), 0.0)
        total = jnp.sum(expo, axis=-1, keepdims=True)
        probs = expo.astype(BF16)
        for j in range(heads // 2):
            span = slice(j * tile, (j + 1) * tile)
            mixed = dot(probs[j * 2 * rows : (j + 1) * 2 * rows], value[:, span])
            part[mine, span] = jnp.where(left, mixed[:rows], mixed[rows:])
        line = jnp.zeros((rows, LANES), F32)
        for k, piece in enumerate(split_three(peak) + split_three(total)[:2]):
            for h in range(heads):
                line = jnp.where(lane == k * heads + h, piece[h * rows : (h + 1) * rows], line)
        stats[mine, :] = line
    share = width // nx
    for dx in range(nx):
        to = place.x_after(dx)
        messages[dx][:, :share] = part[:, at(to, share)].astype(BF16)
        messages[dx][:, share:] = pltpu.roll(
            stats[...], lax.rem(LANES - to * (heads // nx), LANES), 1
        ).astype(BF16)
    for i in range(group):
        for copy in going(i):
            copy.wait()


def expand(factor, count):
    rows = factor.shape[0]
    return jnp.concatenate(
        [jnp.broadcast_to(factor[:, h : h + 1], (rows, HEAD)) for h in range(count)], axis=1
    )


def merge(messages, heads, share):
    peaks, totals = [], []
    for message in messages:
        stats = message[:, share:].astype(F32)
        peaks.append(stats + turn(stats, -heads) + turn(stats, -2 * heads))
        totals.append(turn(stats, -3 * heads) + turn(stats, -4 * heads))
    peak = functools.reduce(jnp.maximum, peaks)
    scales = [jnp.exp(p - peak) for p in peaks]
    total = sum(t * s for t, s in zip(totals, scales))
    return peak, total, scales


def merge_x_kernel(place, heads, *refs):
    share = refs[0].shape[1] - LANES
    count = share // HEAD
    out = refs[-1]
    messages = [r[...] for r in refs[:-1]]
    peak, total, scales = merge(messages, heads, share)
    out[:, :share] = sum(
        m[:, :share].astype(F32) * expand(s, count) for m, s in zip(messages, scales)
    ).astype(BF16)
    lane = lax.broadcasted_iota(jnp.int32, peak.shape, 1)
    tile = jnp.zeros_like(peak)
    for k, piece in enumerate(split_three(peak) + split_three(total)[:2]):
        tile = tile + turn(jnp.where(lane < count, piece, 0.0), k * heads)
    out[:, share:] = tile.astype(BF16)


def merge_z_kernel(place, heads, *refs):
    share = refs[0].shape[1] - LANES
    count = share // HEAD
    out = refs[-1]
    messages = [r[...] for r in refs[:-1]]
    _, total, scales = merge(messages, heads, share)
    out[...] = sum(
        m[:, :share].astype(F32) * expand(s / total, count) for m, s in zip(messages, scales)
    ).astype(BF16)


def out_kernel(place, attn, *refs):
    nx = place.nx
    weights = refs[: 2 * nx]
    bias, out, total = refs[2 * nx :]
    depth = weights[0].shape[0]
    core = place.core()
    for k in range(nx):
        block = lax.rem(place.y() + k, nx)
        total[block] = dot(attn[:, at(core, depth)], weights[2 * k][...]) + dot(
            attn[:, at(1 - core, depth)], weights[2 * k + 1][...]
        )
    total[place.x()] = total[place.x()] + bias[...]
    out[...] = total[...].astype(BF16)


def feed_kernel(place, *refs):
    nx, nz = place.nx, place.nz
    blocks = CORES * place.ny
    tokens = refs[0]
    gathered = refs[1 : 1 + nz]
    gain, shift, bias = refs[1 + nz : 4 + nz]
    ups = refs[4 + nz : 4 + nz + blocks]
    downs = refs[4 + nz + blocks : 4 + nz + 2 * blocks]
    outs = refs[4 + nz + 2 * blocks : 4 + nz + 2 * blocks + nx]
    mid_out, proj, normed, flat, feed = refs[4 + nz + 2 * blocks + nx :]
    cols = gathered[0].shape[2]
    for dz in range(nz):
        proj[:, at(place.z_partner(dz), nx * cols)] = side_by_side(gathered[dz], 0, cols)
    flatten(tokens, flat, 0)
    mid = flat[...] + proj[...]
    mid_out[...] = mid
    normed[...] = layer_norm(mid, gain[...], shift[...]).astype(BF16)
    depth = ups[0].shape[0]
    owners = [
        place.y_before(dy) * CORES + lax.rem(place.core() + dc, CORES)
        for dy in range(place.ny)
        for dc in range(CORES)
    ]
    total = bias[...]
    for owner, up in zip(owners, ups):
        total = total + dot(normed[:, at(owner, depth)], up[...])
    hidden = (0.5 * total * (1.0 + lax.erf(total * 0.5**0.5))).astype(BF16)
    ncols = downs[0].shape[1]
    for owner, down in zip(owners, downs):
        feed[:, at(owner, ncols)] = dot(hidden, down[...])
    share = outs[0].shape[1]
    for dx in range(nx):
        outs[dx][...] = feed[:, at(place.x_after(dx), share)].astype(BF16)


def add_kernel(*refs):
    refs[-1][...] = sum(r[...].astype(F32) for r in refs[:-1]).astype(BF16)


def last_kernel(place, *refs):
    nx = place.nx
    parts = refs[:nx]
    mid, bias, out, full = refs[nx:]
    group, steps, _ = out.shape
    share = parts[0].shape[1]
    for dx in range(nx):
        full[:, at(place.x_before(dx), share)] = parts[dx][...].astype(F32)
    result = mid[...] + full[...] + bias[...]
    for i in range(group):
        out[i] = result[i * steps : (i + 1) * steps].astype(BF16)


def tie(values):
    return lax.optimization_barrier(values)


def shape(sizes, kind=BF16):
    return jax.ShapeDtypeStruct(tuple(sizes), kind)


def body(
    tokens,
    lengths,
    cache_keys,
    cache_values,
    norm1_gain,
    norm1_bias,
    w_query,
    b_query,
    w_key,
    b_key,
    w_value,
    b_value,
    w_out,
    b_out,
    norm2_gain,
    norm2_bias,
    w_up,
    b_up,
    w_down,
    b_down,
):
    place = Place(lax.axis_size("seq"), lax.axis_size("req"))
    nx, ny = place.nx, place.ny
    group, steps, width = tokens.shape
    slots = cache_keys.shape[1]
    rows = group * steps
    heads = width // HEAD
    share = width // nx
    bind = functools.partial

    def row(vector):
        return vector.reshape(1, -1)

    def spread(by_dy):
        return [
            by_dy[dy] if dx == 0 and dy == 0 else place.move(by_dy[dy], dx, dy)
            for dx in range(nx)
            for dy in range(ny)
        ]

    def over_y(weight):
        return [place.move(weight, dy=dy) for dy in range(1, ny)]

    def over_core(blocks):
        return [place.move(block, dc=1) for block in blocks]

    def over_x(value):
        return [value] + [place.move(value, dx=dx) for dx in range(1, nx)]

    toks = [tokens] + [place.move(tokens, dy=dy) for dy in range(1, ny)]
    cols = w_query.shape[1]
    own = [w_query, w_key, w_value]
    siblings = over_core(own)
    up_ys = over_y(w_up)
    scales = row(jnp.concatenate([norm1_gain, norm1_bias]))
    biases = row(jnp.concatenate([b_query, b_key, b_value]))
    normed, *own = call(
        norm_kernel,
        "norm",
        [tokens, scales, *own],
        [shape((rows, width))] + [shape(w.shape) for w in own],
        in_specs=[VMEM] * 2 + [HBM] * 3,
        scratch=[pltpu.VMEM((rows, width), F32), pltpu.SemaphoreType.DMA((3,))],
    )
    parts = call(
        bind(qkv_kernel, place),
        "norm_qkv",
        [normed, *toks[1:], scales, biases, *own, *siblings],
        [shape((rows, 3 * cols))] * ny,
        scratch=[pltpu.VMEM(((ny - 1) * rows, width), F32), pltpu.VMEM((ny * rows, width), BF16)],
    )
    parts, tied = tie((parts, w_up))
    up_cores = over_core([tied])
    qkv = call(
        bind(add_columns_kernel, place), "add_qkv", spread(parts), shape((nx, rows, 3 * cols))
    )
    qkv, tied, up_cores = tie((qkv, w_out, up_cores))
    blocks = [place.transpose(tied, 0)]
    pack = max(1, min(group, 256 // slots))
    new_keys, new_values, *messages = call(
        bind(attention_kernel, place, heads, steps),
        "attention",
        [*place.gather_z(qkv), lengths, cache_keys, cache_values],
        [shape(cache_keys.shape), shape(cache_values.shape)] + [shape((rows, share + LANES))] * nx,
        in_specs=[VMEM] * place.nz + [SMEM, HBM, HBM],
        out_specs=[HBM, HBM] + [VMEM] * nx,
        scratch=[
            pltpu.VMEM((rows, width), F32),
            pltpu.VMEM((rows, width), F32),
            pltpu.VMEM((rows, width), F32),
            pltpu.VMEM((heads * pack * steps, pack * slots), F32),
            pltpu.VMEM((rows, width), F32),
            pltpu.VMEM((rows, LANES), F32),
            pltpu.VMEM(cache_keys.shape, BF16),
            pltpu.VMEM(cache_keys.shape, BF16),
            pltpu.SemaphoreType.DMA((2, group)),
            pltpu.SemaphoreType.DMA((2, group)),
        ],
        limit=52,
    )
    messages, blocks, up_ys, tied = tie((messages, blocks, up_ys, (w_out, w_down)))
    blocks += [place.transpose(tied[0], k) for k in range(1, nx)]
    down_ys = over_y(tied[1])
    block_cores = over_core(blocks[:1])
    up_cores += over_core(up_ys)
    messages = [messages[0]] + [place.move(messages[dx], dx=dx) for dx in range(1, nx)]
    merged = call(
        bind(merge_x_kernel, place, heads), "merge_x", messages, shape((rows, share + LANES))
    )
    merged, blocks, block_cores, up_cores = tie((merged, blocks, block_cores, up_cores))
    block_cores += over_core(blocks[1:])
    attn = call(
        bind(merge_z_kernel, place, heads), "merge_z", place.gather_z(merged), shape((rows, share))
    )
    attn, block_cores, tied = tie((attn, block_cores, w_down))
    down_cores = over_core([tied])
    out_part = call(
        bind(out_kernel, place),
        "out",
        [attn, *[b for pair in zip(blocks, block_cores) for b in pair], row(b_out)],
        shape((nx, rows, cols)),
        scratch=[pltpu.VMEM((nx, rows, cols), F32)],
    )
    projected = call(add_kernel, "add_out", over_x(out_part), shape((nx, rows, cols)))
    projected, down_ys, down_cores = tie((projected, down_ys, down_cores))
    down_cores += over_core(down_ys)
    *feeds, mid = call(
        bind(feed_kernel, place),
        "feed",
        [
            tokens,
            *place.gather_z(projected),
            row(norm2_gain),
            row(norm2_bias),
            row(b_up),
            *[b for pair in zip([w_up] + up_ys, up_cores) for b in pair],
            *[b for pair in zip([w_down] + down_ys, down_cores) for b in pair],
        ],
        [shape((rows, share))] * nx + [shape((rows, width), F32)],
        scratch=[
            pltpu.VMEM((rows, width), F32),
            pltpu.VMEM((rows, width), BF16),
            pltpu.VMEM((rows, width), F32),
            pltpu.VMEM((rows, width), F32),
        ],
    )
    feeds = [feeds[0]] + [place.move(feeds[dx], dx=dx) for dx in range(1, nx)]
    feed = call(add_kernel, "add_x", feeds, shape((rows, share)))
    summed = call(add_kernel, "add_z", place.gather_z(feed), shape((rows, share)))
    hidden_out = call(
        bind(last_kernel, place),
        "last",
        [*over_x(summed), mid, row(b_down)],
        shape(tokens.shape),
        scratch=[pltpu.VMEM((rows, width), F32)],
    )
    return (hidden_out, new_keys, new_values)


def solution(mesh):
    in_specs = (
        P("req", None, None),
        P("req"),
        P("req", "seq", None),
        P("req", "seq", None),
        P(),
        P(),
        P("req", "seq"),
        P("seq"),
        P("req", "seq"),
        P("seq"),
        P("req", "seq"),
        P("seq"),
        P("req", "seq"),
        P("seq"),
        P(),
        P(),
        P("req", "seq"),
        P("seq"),
        P("seq", "req"),
        P(),
    )
    out_specs = (P("req", None, None), P("req", "seq", None), P("req", "seq", None))
    return jax.shard_map(body, mesh=mesh, in_specs=in_specs, out_specs=out_specs, check_vma=False)
```

```python
import functools

import jax
import jax.numpy as jnp
from jax import lax
from jax.experimental import pallas as pl
from jax.experimental.pallas import tpu as pltpu
from jax.sharding import PartitionSpec as P

HEAD = 128
LANES = 128
CORES = 2
BF16 = jnp.bfloat16
F32 = jnp.float32
VMEM = pl.BlockSpec(memory_space=pltpu.VMEM)
SMEM = pl.BlockSpec(memory_space=pltpu.SMEM)
HBM = pl.BlockSpec(memory_space=pltpu.HBM)


class Place:
    def __init__(self, seqs, reqs):
        self.ny = reqs // CORES
        self.nx = self.ny
        self.nz = seqs // self.nx
        self.seqs = seqs

    def x(self):
        return lax.rem(lax.axis_index("seq"), self.nx)

    def y(self):
        return lax.div(lax.axis_index("req"), CORES)

    def core(self):
        return lax.rem(lax.axis_index("req"), CORES)

    def x_before(self, dx):
        return lax.rem(self.x() + self.nx - dx, self.nx)

    def x_after(self, dx):
        return lax.rem(self.x() + dx, self.nx)

    def y_before(self, dy):
        return lax.rem(self.y() + self.ny - dy, self.ny)

    def z_partner(self, dz):
        return lax.bitwise_xor(lax.div(lax.axis_index("seq"), self.nx), dz)

    def move(self, value, dx=0, dy=0, dc=0, dz=0):
        pairs = []
        for z in range(self.nz):
            for x in range(self.nx):
                for y in range(self.ny):
                    for c in range(CORES):
                        to_x, to_y, to_c = (x + dx) % self.nx, (y + dy) % self.ny, (c + dc) % CORES
                        to_z = z ^ dz
                        pairs.append(
                            (
                                ((z * self.nx + x) * self.ny + y) * CORES + c,
                                ((to_z * self.nx + to_x) * self.ny + to_y) * CORES + to_c,
                            )
                        )
        return lax.ppermute(value, ("seq", "req"), pairs)

    def transpose(self, value, k):
        n = self.nx
        pairs = []
        for z in range(self.nz):
            for x in range(n):
                for y in range(n):
                    for c in range(CORES):
                        pairs.append(
                            (
                                ((z * n + x) * n + y) * CORES + c,
                                ((z * n + y) * n + (x - k) % n) * CORES + c,
                            )
                        )
        return lax.ppermute(value, ("seq", "req"), pairs)

    def gather_z(self, value):
        return [value] + [self.move(value, dz=dz) for dz in range(1, self.nz)]


def layer_norm(values, gain, shift):
    center = values - jnp.mean(values, axis=-1, keepdims=True)
    spread = jnp.mean(center * center, axis=-1, keepdims=True)
    return center * lax.rsqrt(spread + 1e-05) * gain + shift


def dot(a, b):
    return jnp.dot(a, b, preferred_element_type=F32)


def across(a, b):
    return lax.dot_general(a, b, (((1,), (1,)), ((), ())), preferred_element_type=F32)


def at(index, size):
    return pl.ds(pl.multiple_of(index * size, size), size)


def call(kernel, name, ins, outs, in_specs=None, out_specs=None, scratch=(), moved=2**20, limit=20, aliases=None):
    single = not isinstance(outs, (list, tuple))
    specs = out_specs or (VMEM if single else [VMEM] * len(outs))
    return pl.pallas_call(
        kernel,
        name=name,
        out_shape=outs,
        in_specs=in_specs or [VMEM] * len(ins),
        out_specs=specs,
        scratch_shapes=list(scratch),
        input_output_aliases=aliases or {},
        cost_estimate=pl.CostEstimate(flops=0, bytes_accessed=moved, transcendentals=0),
        compiler_params=pltpu.CompilerParams(vmem_limit_bytes=limit * 1024 * 1024),
    )(*ins)


def side_by_side(blocks, start, size):
    return jnp.concatenate(
        [blocks[x, :, start : start + size].astype(F32) for x in range(blocks.shape[0])], axis=1
    )


def two_halves(rows_by_k, own, sibling):
    depth = own.shape[0]
    req = lax.axis_index("req")
    other = req + 1 - 2 * lax.rem(req, CORES)
    return dot(rows_by_k[:, at(req, depth)], own[...]) + dot(
        rows_by_k[:, at(other, depth)], sibling[...]
    )


def flatten(block, flat, start):
    group, steps, _ = block.shape
    for i in range(group):
        flat[start + i * steps : start + (i + 1) * steps, :] = block[i].astype(F32)


def norm_kernel(mark, tokens, scales, *refs):
    count = (len(refs) - 3) // 2
    weights, out, kept = refs[:count], refs[count], refs[count + 1 : 2 * count + 1]
    flat, sems = refs[-2:]
    copies = [
        pltpu.make_async_copy(source, target, sems.at[k])
        for k, (source, target) in enumerate(zip(weights, kept))
    ]
    for copy in copies:
        copy.start()
    width = out.shape[1]
    flatten(tokens, flat, 0)
    out[...] = layer_norm(flat[...], scales[:, :width], scales[:, width:]).astype(BF16)
    for copy in copies:
        copy.wait()


def qkv_kernel(place, *refs):
    ny = place.ny
    mine = refs[0]
    toks = refs[1:ny]
    scales, biases = refs[ny : ny + 2]
    weights = refs[ny + 2 : ny + 8]
    outs = refs[ny + 8 : 2 * ny + 8]
    flat, normed = refs[2 * ny + 8 :]
    rows, width = mine.shape
    normed[:rows, :] = mine[...]
    for j, tok in enumerate(toks):
        flatten(tok, flat, j * rows)
    normed[rows:, :] = layer_norm(flat[...], scales[:, :width], scales[:, width:]).astype(BF16)
    cols = weights[0].shape[1]
    for k in range(3):
        acc = two_halves(normed, weights[k], weights[3 + k])
        for j in range(ny):
            part = acc[j * rows : (j + 1) * rows]
            if j == 0:
                part = part + biases[:, k * cols : (k + 1) * cols]
            outs[(ny - j) % ny][:, k * cols : (k + 1) * cols] = part.astype(BF16)


def add_qkv_kernel(place, *refs):
    query, fresh = refs[-2:]
    cols = query.shape[2]
    for dx in range(place.nx):
        total = refs[dx * place.ny][...].astype(F32)
        for dy in range(1, place.ny):
            total = total + refs[dx * place.ny + dy][...].astype(F32)
        total = total.astype(BF16)
        query[place.x_before(dx)] = total[:, :cols]
        fresh[place.x_before(dx)] = total[:, cols:]


def cache_kernel(keys_in, values_in, keys_out, values_out, keys, values, mark, in_sems, out_sems):
    group = keys.shape[0]
    arrays = ((keys_in, keys, keys_out), (values_in, values, values_out))
    coming = [
        pltpu.make_async_copy(source.at[i], here.at[i], in_sems.at[k, i])
        for i in range(group)
        for k, (source, here, _) in enumerate(arrays)
    ]
    going = [
        pltpu.make_async_copy(here.at[i], target.at[i], out_sems.at[k, i])
        for i in range(group)
        for k, (_, here, target) in enumerate(arrays)
    ]
    for copy in coming:
        copy.start()
    mark[...] = jnp.zeros_like(mark)
    for arrived, copy in zip(coming, going):
        arrived.wait()
        copy.start()
    for copy in going:
        copy.wait()


def insert_kernel(place, steps, *refs):
    nx, nz = place.nx, place.nz
    gathered = refs[:nz]
    lengths, keys, values, _, _, keys_out, values_out, ks, vs, k_rows, v_rows, sems = refs[nz:]
    group, slots, width = keys.shape
    cols = width // place.seqs
    base_of = lax.axis_index("seq") * slots
    for dz in range(nz):
        span = at(place.z_partner(dz), nx * cols)
        for k, target in enumerate((ks, vs)):
            target[:, span] = side_by_side(gathered[dz], k * cols, cols)
    window = k_rows.shape[1]

    def place_of(i):
        base = lengths[i] - base_of
        start = jnp.clip(lax.div(jnp.maximum(base, 0), 16) * 16, 0, slots - window)
        return base, pl.multiple_of(start, 16)

    def copies(i):
        _, start = place_of(i)
        return [
            pltpu.make_async_copy(
                rows.at[i], target.at[i, pl.ds(start, window), :], sems.at[k, i]
            )
            for k, (rows, target) in enumerate(((k_rows, keys_out), (v_rows, values_out)))
        ]

    for i in range(group):
        base, start = place_of(i)

        @pl.when((base > -steps) & (base < slots))
        def _():
            slot = start + lax.broadcasted_iota(jnp.int32, (window, width), 0)
            for source, fresh, rows in ((keys, ks, k_rows), (values, vs, v_rows)):
                block = source[i, pl.ds(start, window), :].astype(F32)
                for t in range(steps):
                    at_row = fresh[i * steps + t : i * steps + t + 1, :]
                    block = jnp.where(slot == base + t, at_row, block)
                rows[i] = block.astype(BF16)
            for copy in copies(i):
                copy.start()

    for i in range(group):
        base, _ = place_of(i)

        @pl.when((base > -steps) & (base < slots))
        def _():
            for copy in copies(i):
                copy.wait()


def split_three(value):
    first = value.astype(BF16).astype(F32)
    rest = value - first
    second = rest.astype(BF16).astype(F32)
    return first, second, rest - second


def turn(value, by):
    return pltpu.roll(value, by % LANES, 1)


def pairs_of(query):
    side = lax.rem(lax.div(lax.broadcasted_iota(jnp.int32, query.shape, 1), HEAD), 2)
    return jnp.concatenate(
        [jnp.where(side == 0, query, 0.0), jnp.where(side == 1, query, 0.0)], axis=0
    ).astype(BF16)


def attention_kernel(place, heads, steps, *refs):
    nx, nz = place.nx, place.nz
    gathered = refs[:nz]
    fresh, lengths, keys, values = refs[nz : nz + 4]
    messages = refs[nz + 4 : nz + 4 + nx]
    qs, scores, part, stats = refs[nz + 4 + nx :]
    group, slots, width = keys.shape
    cols = width // place.seqs
    seq = lax.axis_index("seq")
    for dz in range(nz):
        qs[:, at(place.z_partner(dz), nx * cols)] = side_by_side(gathered[dz], 0, cols)
    pack = max(1, min(group, 256 // slots))
    rows = pack * steps
    tile = 2 * HEAD
    tiles = nx * cols // tile
    first = place.z_partner(0) * tiles
    own_query = side_by_side(gathered[0], 0, cols)
    own_key = side_by_side(fresh, 0, cols)
    own_value = side_by_side(fresh, cols, cols)
    left = lax.broadcasted_iota(jnp.int32, (rows, tile), 1) < HEAD
    many, cached = heads * rows, pack * slots
    row = lax.broadcasted_iota(jnp.int32, (many, cached + LANES), 0)
    column = lax.broadcasted_iota(jnp.int32, (many, cached + LANES), 1)
    owner = lax.div(lax.rem(row, rows), steps)
    position = seq * slots + lax.rem(column, slots)
    same = (column < cached) & (owner == lax.div(column, slots))
    mine_tile = lax.div(row, 2 * rows) - first
    new = column - cached
    own = (
        (new >= 0)
        & (new < rows)
        & (lax.div(new, steps) == owner)
        & (lax.rem(new, steps) <= lax.rem(row, steps))
        & (mine_tile >= 0)
        & (mine_tile < tiles)
        & (place.x() == 0)
    )
    lane = lax.broadcasted_iota(jnp.int32, (rows, LANES), 1)
    blank = jnp.zeros((LANES - rows, nx * cols), BF16)
    for g in range(group // pack):
        mine = slice(g * rows, (g + 1) * rows)
        these = slice(g * pack, (g + 1) * pack)
        pair = pairs_of(qs[mine, :])
        key = keys[these].reshape(cached, width)
        value = values[these].reshape(cached, width)
        new_key = jnp.concatenate([own_key[mine].astype(BF16), blank], axis=0)
        new_value = jnp.concatenate([own_value[mine].astype(BF16), blank], axis=0)
        own_pair = pairs_of(own_query[mine])
        for j in range(heads // 2):
            span = slice(j * tile, (j + 1) * tile)
            scores[j * 2 * rows : (j + 1) * 2 * rows, :cached] = across(pair[:, span], key[:, span])
        scores[:, cached:] = jnp.zeros((many, LANES), F32)
        for j in range(tiles):
            span = slice(j * tile, (j + 1) * tile)
            scores[at(first + j, 2 * rows), cached:] = across(own_pair[:, span], new_key[:, span])
        limit = jnp.zeros_like(owner)
        for k in range(pack):
            limit = jnp.where(owner == k, lengths[g * pack + k], limit)
        valid = (same & (position < limit)) | own
        masked = jnp.where(valid, scores[...] * HEAD ** (-0.5), -1e30)
        peak = jnp.max(masked, axis=-1, keepdims=True)
        expo = jnp.where(valid, jnp.exp(masked - peak), 0.0)
        total = jnp.sum(expo, axis=-1, keepdims=True)
        scores[...] = expo
        for j in range(heads // 2):
            span = slice(j * tile, (j + 1) * tile)
            probs = scores[j * 2 * rows : (j + 1) * 2 * rows, :cached].astype(BF16)
            mixed = dot(probs, value[:, span])
            part[mine, span] = jnp.where(left, mixed[:rows], mixed[rows:])
        for j in range(tiles):
            span = slice(j * tile, (j + 1) * tile)
            probs = scores[at(first + j, 2 * rows), cached:].astype(BF16)
            mixed = dot(probs, new_value[:, span])
            here = at(first + j, tile)
            part[mine, here] = part[mine, here] + jnp.where(left, mixed[:rows], mixed[rows:])
        line = jnp.zeros((rows, LANES), F32)
        for k, piece in enumerate(split_three(peak) + split_three(total)[:2]):
            for h in range(heads):
                line = jnp.where(lane == k * heads + h, piece[h * rows : (h + 1) * rows], line)
        stats[mine, :] = line
    share = width // nx
    for dx in range(nx):
        to = place.x_after(dx)
        messages[dx][:, :share] = part[:, at(to, share)].astype(BF16)
        messages[dx][:, share:] = pltpu.roll(
            stats[...], lax.rem(LANES - to * (heads // nx), LANES), 1
        ).astype(BF16)


def expand(factor, count):
    rows = factor.shape[0]
    return jnp.concatenate(
        [jnp.broadcast_to(factor[:, h : h + 1], (rows, HEAD)) for h in range(count)], axis=1
    )


def merge(messages, heads, share):
    peaks, totals = [], []
    for message in messages:
        stats = message[:, share:].astype(F32)
        peaks.append(stats + turn(stats, -heads) + turn(stats, -2 * heads))
        totals.append(turn(stats, -3 * heads) + turn(stats, -4 * heads))
    peak = functools.reduce(jnp.maximum, peaks)
    scales = [jnp.exp(p - peak) for p in peaks]
    total = sum(t * s for t, s in zip(totals, scales))
    return peak, total, scales


def merge_x_kernel(place, heads, *refs):
    share = refs[0].shape[1] - LANES
    count = share // HEAD
    out = refs[-1]
    messages = [r[...] for r in refs[:-1]]
    peak, total, scales = merge(messages, heads, share)
    out[:, :share] = sum(
        m[:, :share].astype(F32) * expand(s, count) for m, s in zip(messages, scales)
    ).astype(BF16)
    lane = lax.broadcasted_iota(jnp.int32, peak.shape, 1)
    tile = jnp.zeros_like(peak)
    for k, piece in enumerate(split_three(peak) + split_three(total)[:2]):
        tile = tile + turn(jnp.where(lane < count, piece, 0.0), k * heads)
    out[:, share:] = tile.astype(BF16)


def merge_z_kernel(place, heads, *refs):
    share = refs[0].shape[1] - LANES
    count = share // HEAD
    out = refs[-1]
    messages = [r[...] for r in refs[:-1]]
    _, total, scales = merge(messages, heads, share)
    out[...] = sum(
        m[:, :share].astype(F32) * expand(s / total, count) for m, s in zip(messages, scales)
    ).astype(BF16)


def out_kernel(place, attn, *refs):
    nx = place.nx
    weights = refs[: 2 * nx]
    bias, out, total = refs[2 * nx :]
    depth = weights[0].shape[0]
    core = place.core()
    for k in range(nx):
        block = lax.rem(place.y() + k, nx)
        total[block] = dot(attn[:, at(core, depth)], weights[2 * k][...]) + dot(
            attn[:, at(1 - core, depth)], weights[2 * k + 1][...]
        )
    total[place.x()] = total[place.x()] + bias[...]
    out[...] = total[...].astype(BF16)


def add_out_kernel(place, *refs):
    out = refs[-1]
    for dy in range(place.ny):
        total = refs[dy][...].astype(F32)
        for dx in range(1, place.nx):
            total = total + refs[dx * place.ny + dy][...].astype(F32)
        out[place.y_before(dy)] = total.astype(BF16)


def up_kernel(place, *refs):
    ny, nz = place.ny, place.nz
    toks = refs[:ny]
    gathered = refs[ny : ny + nz]
    gain, shift, own, sibling, bias, out, mid_out, proj, normed, flat = refs[ny + nz :]
    group, steps, _ = toks[0].shape
    rows = group * steps
    cols = gathered[0].shape[3]
    for dz in range(nz):
        span = at(place.z_partner(dz), place.nx * cols)
        for y in range(ny):
            proj[y * rows : (y + 1) * rows, span] = side_by_side(gathered[dz].at[y], 0, cols)
    for j in range(ny):
        here = at(place.y_before(j), rows)
        flatten(toks[j], flat, 0)
        mid = flat[...] + proj[here, :]
        if j == 0:
            mid_out[...] = mid
        normed[here, :] = layer_norm(mid, gain[...], shift[...]).astype(BF16)
    first = (place.y() == 0).astype(F32)
    out[...] = (two_halves(normed, own, sibling) + bias[...] * first).astype(BF16)


def down_kernel(place, *refs):
    nx, ny = place.nx, place.ny
    parts = refs[:ny]
    own, sibling = refs[ny : ny + 2]
    outs = refs[ny + 2 : ny + 2 + nx]
    feed = refs[-1]
    total = sum(p[...].astype(F32) for p in parts)
    hidden = (0.5 * total * (1.0 + lax.erf(total * 0.5**0.5))).astype(BF16)
    ncols = own.shape[1]
    feed[:, at(place.core(), ncols)] = dot(hidden, own[...])
    feed[:, at(1 - place.core(), ncols)] = dot(hidden, sibling[...])
    width = outs[0].shape[1]
    for dx in range(nx):
        outs[dx][...] = feed[:, at(place.x_after(dx), width)].astype(BF16)


def add_x_kernel(place, *refs):
    refs[-1][...] = sum(r[...].astype(F32) for r in refs[:-1]).astype(BF16)


def add_z_kernel(place, *refs):
    outs, total = refs[place.nz : -1], refs[-1]
    total[...] = sum(r[...].astype(F32) for r in refs[: place.nz])
    rows = outs[0].shape[0]
    for dy in range(place.ny):
        outs[dy][...] = total[at(lax.rem(place.y() + dy, place.ny), rows), :].astype(BF16)


def last_kernel(place, *refs):
    nx, ny = place.nx, place.ny
    parts = refs[: nx * ny]
    mid, bias, out, full = refs[nx * ny :]
    group, steps, _ = out.shape
    width = parts[0].shape[1]
    for dx in range(nx):
        for dy in range(ny):
            block = place.y_before(dy) * nx + place.x_before(dx)
            full[:, at(block, width)] = parts[dx * ny + dy][...].astype(F32)
    result = mid[...] + full[...] + bias[...]
    for i in range(group):
        out[i] = result[i * steps : (i + 1) * steps].astype(BF16)


def shape(sizes, kind=BF16):
    return jax.ShapeDtypeStruct(tuple(sizes), kind)


def body(
    tokens,
    lengths,
    cache_keys,
    cache_values,
    norm1_gain,
    norm1_bias,
    w_query,
    b_query,
    w_key,
    b_key,
    w_value,
    b_value,
    w_out,
    b_out,
    norm2_gain,
    norm2_bias,
    w_up,
    b_up,
    w_down,
    b_down,
):
    place = Place(lax.axis_size("seq"), lax.axis_size("req"))
    nx, ny = place.nx, place.ny
    group, steps, width = tokens.shape
    slots = cache_keys.shape[1]
    rows = group * steps
    heads = width // HEAD
    share = width // nx
    bind = functools.partial

    def row(vector):
        return vector.reshape(1, -1)

    def spread(by_dy):
        return [
            by_dy[dy] if dx == 0 and dy == 0 else place.move(by_dy[dy], dx, dy)
            for dx in range(nx)
            for dy in range(ny)
        ]

    toks = [tokens] + [place.move(tokens, dy=dy) for dy in range(1, ny)]
    cols = w_query.shape[1]
    own = [w_query, w_key, w_value]
    siblings = [place.move(weight, dc=1) for weight in own]
    new_keys, new_values, keys, values, mark = call(
        cache_kernel,
        "caches",
        [cache_keys, cache_values],
        [shape(cache_keys.shape)] * 4 + [shape((8, LANES), F32)],
        in_specs=[HBM, HBM],
        out_specs=[HBM, HBM, VMEM, VMEM, VMEM],
        scratch=[pltpu.SemaphoreType.DMA((2, group)), pltpu.SemaphoreType.DMA((2, group))],
        moved=16 * 1024 * 1024,
        limit=46,
    )
    scales = row(jnp.concatenate([norm1_gain, norm1_bias]))
    biases = row(jnp.concatenate([b_query, b_key, b_value]))
    normed, *own = call(
        norm_kernel,
        "norm",
        [mark, tokens, scales, *own],
        [shape((rows, width))] + [shape(w.shape) for w in own],
        in_specs=[VMEM] * 3 + [HBM] * 3,
        scratch=[pltpu.VMEM((rows, width), F32), pltpu.SemaphoreType.DMA((3,))],
    )
    parts = call(
        bind(qkv_kernel, place),
        "norm_qkv",
        [normed, *toks[1:], scales, biases, *own, *siblings],
        [shape((rows, 3 * cols))] * ny,
        scratch=[pltpu.VMEM(((ny - 1) * rows, width), F32), pltpu.VMEM((ny * rows, width), BF16)],
    )
    *parts, tied_up, tied_down = lax.optimization_barrier((*parts, w_up, w_down))
    w_up_sibling = place.move(tied_up, dc=1)
    w_down_sibling = place.move(tied_down, dc=1)
    query, fresh = call(
        bind(add_qkv_kernel, place),
        "add_qkv",
        spread(parts),
        [shape((nx, rows, cols)), shape((nx, rows, 2 * cols))],
    )
    query, fresh, w_up_sibling, w_down_sibling, tied = lax.optimization_barrier(
        (query, fresh, w_up_sibling, w_down_sibling, w_out)
    )
    blocks = [place.transpose(tied, k) for k in range(nx)]
    queries, fresh = lax.optimization_barrier((place.gather_z(query), fresh))
    messages = call(
        bind(attention_kernel, place, heads, steps),
        "attention",
        [*queries, fresh, lengths, keys, values],
        [shape((rows, share + LANES))] * nx,
        in_specs=[VMEM] * (place.nz + 1) + [SMEM, VMEM, VMEM],
        scratch=[
            pltpu.VMEM((rows, width), F32),
            pltpu.VMEM(
                (
                    heads * max(1, min(group, 256 // slots)) * steps,
                    max(1, min(group, 256 // slots)) * slots + LANES,
                ),
                F32,
            ),
            pltpu.VMEM((rows, width), F32),
            pltpu.VMEM((rows, LANES), F32),
        ],
    )
    fresh = place.gather_z(fresh)
    messages, blocks = lax.optimization_barrier((messages, blocks))
    messages = [messages[0]] + [place.move(messages[dx], dx=dx) for dx in range(1, nx)]
    merged = call(
        bind(merge_x_kernel, place, heads), "merge_x", messages, shape((rows, share + LANES))
    )
    merged, blocks, fresh = lax.optimization_barrier((merged, blocks, fresh))
    w_outs = []
    for block in blocks:
        w_outs += [block, place.move(block, dc=1)]
    window = min(32, slots)
    new_keys, new_values = call(
        bind(insert_kernel, place, steps),
        "insert",
        [*fresh, lengths, keys, values, new_keys, new_values],
        [shape(cache_keys.shape)] * 2,
        in_specs=[VMEM] * place.nz + [SMEM, VMEM, VMEM, HBM, HBM],
        out_specs=[HBM, HBM],
        scratch=[
            pltpu.VMEM((rows, width), F32),
            pltpu.VMEM((rows, width), F32),
            pltpu.VMEM((group, window, width), BF16),
            pltpu.VMEM((group, window, width), BF16),
            pltpu.SemaphoreType.DMA((2, group)),
        ],
        aliases={place.nz + 3: 0, place.nz + 4: 1},
    )
    attn = call(
        bind(merge_z_kernel, place, heads), "merge_z", place.gather_z(merged), shape((rows, share))
    )
    out_part = call(
        bind(out_kernel, place),
        "out",
        [attn, *w_outs, row(b_out)],
        shape((nx, rows, cols)),
        scratch=[pltpu.VMEM((nx, rows, cols), F32)],
    )
    projected = call(
        bind(add_out_kernel, place),
        "add_out",
        spread([out_part] * ny),
        shape((ny, nx, rows, cols)),
    )
    up_part, mid = call(
        bind(up_kernel, place),
        "norm_up",
        [
            *toks,
            *place.gather_z(projected),
            row(norm2_gain),
            row(norm2_bias),
            w_up,
            w_up_sibling,
            row(b_up),
        ],
        [shape((ny * rows, w_up.shape[1])), shape((rows, width), F32)],
        scratch=[
            pltpu.VMEM((ny * rows, width), F32),
            pltpu.VMEM((ny * rows, width), BF16),
            pltpu.VMEM((rows, width), F32),
        ],
    )
    up_parts = [up_part] + [place.move(up_part, dy=dy) for dy in range(1, ny)]
    piece = CORES * w_down.shape[1] // nx
    feeds = call(
        bind(down_kernel, place),
        "gelu_down",
        [*up_parts, w_down, w_down_sibling],
        [shape((ny * rows, piece))] * nx,
        scratch=[pltpu.VMEM((ny * rows, CORES * w_down.shape[1]), F32)],
    )
    feeds = [feeds[0]] + [place.move(feeds[dx], dx=dx) for dx in range(1, nx)]
    feed = call(bind(add_x_kernel, place), "add_x", feeds, shape((ny * rows, piece)))
    summed = call(
        bind(add_z_kernel, place),
        "add_z",
        place.gather_z(feed),
        [shape((rows, piece))] * ny,
        scratch=[pltpu.VMEM((ny * rows, piece), F32)],
    )
    hidden_out = call(
        bind(last_kernel, place),
        "last",
        [*spread(summed), mid, row(b_down)],
        shape(tokens.shape),
        scratch=[pltpu.VMEM((rows, width), F32)],
    )
    return (hidden_out, new_keys, new_values)


def solution(mesh):
    in_specs = (
        P("req", None, None),
        P("req"),
        P("req", "seq", None),
        P("req", "seq", None),
        P(),
        P(),
        P("req", "seq"),
        P("seq"),
        P("req", "seq"),
        P("seq"),
        P("req", "seq"),
        P("seq"),
        P("req", "seq"),
        P("seq"),
        P(),
        P(),
        P("req", "seq"),
        P("seq"),
        P("seq", "req"),
        P(),
    )
    out_specs = (P("req", None, None), P("req", "seq", None), P("req", "seq", None))
    return jax.shard_map(body, mesh=mesh, in_specs=in_specs, out_specs=out_specs, check_vma=False)
```

```python
import functools

import jax
import jax.numpy as jnp
from jax import lax
from jax.experimental import pallas as pl
from jax.experimental.pallas import tpu as pltpu
from jax.sharding import PartitionSpec as P

HEAD = 128
LANES = 128
CORES = 2
BF16 = jnp.bfloat16
F32 = jnp.float32
VMEM = pl.BlockSpec(memory_space=pltpu.VMEM)
SMEM = pl.BlockSpec(memory_space=pltpu.SMEM)
HBM = pl.BlockSpec(memory_space=pltpu.HBM)


class Place:
    def __init__(self, seqs, reqs):
        self.ny = reqs // CORES
        self.nx = self.ny
        self.nz = seqs // self.nx
        self.seqs = seqs

    def x(self):
        return lax.rem(lax.axis_index("seq"), self.nx)

    def y(self):
        return lax.div(lax.axis_index("req"), CORES)

    def core(self):
        return lax.rem(lax.axis_index("req"), CORES)

    def x_before(self, dx):
        return lax.rem(self.x() + self.nx - dx, self.nx)

    def x_after(self, dx):
        return lax.rem(self.x() + dx, self.nx)

    def y_before(self, dy):
        return lax.rem(self.y() + self.ny - dy, self.ny)

    def z_partner(self, dz):
        return lax.bitwise_xor(lax.div(lax.axis_index("seq"), self.nx), dz)

    def move(self, value, dx=0, dy=0, dc=0, dz=0):
        pairs = []
        for z in range(self.nz):
            for x in range(self.nx):
                for y in range(self.ny):
                    for c in range(CORES):
                        to_x, to_y, to_c = (x + dx) % self.nx, (y + dy) % self.ny, (c + dc) % CORES
                        to_z = z ^ dz
                        pairs.append(
                            (
                                ((z * self.nx + x) * self.ny + y) * CORES + c,
                                ((to_z * self.nx + to_x) * self.ny + to_y) * CORES + to_c,
                            )
                        )
        return lax.ppermute(value, ("seq", "req"), pairs)

    def transpose(self, value, k):
        n = self.nx
        pairs = []
        for z in range(self.nz):
            for x in range(n):
                for y in range(n):
                    for c in range(CORES):
                        pairs.append(
                            (
                                ((z * n + x) * n + y) * CORES + c,
                                ((z * n + y) * n + (x - k) % n) * CORES + c,
                            )
                        )
        return lax.ppermute(value, ("seq", "req"), pairs)

    def gather_z(self, value):
        return [value] + [self.move(value, dz=dz) for dz in range(1, self.nz)]


def layer_norm(values, gain, shift):
    center = values - jnp.mean(values, axis=-1, keepdims=True)
    spread = jnp.mean(center * center, axis=-1, keepdims=True)
    return center * lax.rsqrt(spread + 1e-05) * gain + shift


def dot(a, b):
    return jnp.dot(a, b, preferred_element_type=F32)


def across(a, b):
    return lax.dot_general(a, b, (((1,), (1,)), ((), ())), preferred_element_type=F32)


def at(index, size):
    return pl.ds(pl.multiple_of(index * size, size), size)


def call(kernel, name, ins, outs, in_specs=None, out_specs=None, scratch=(), moved=2**20, limit=20, aliases=None):
    single = not isinstance(outs, (list, tuple))
    specs = out_specs or (VMEM if single else [VMEM] * len(outs))
    return pl.pallas_call(
        kernel,
        name=name,
        out_shape=outs,
        in_specs=in_specs or [VMEM] * len(ins),
        out_specs=specs,
        scratch_shapes=list(scratch),
        input_output_aliases=aliases or {},
        cost_estimate=pl.CostEstimate(flops=0, bytes_accessed=moved, transcendentals=0),
        compiler_params=pltpu.CompilerParams(vmem_limit_bytes=int(limit * 1024 * 1024)),
    )(*ins)


def side_by_side(blocks, start, size):
    return jnp.concatenate(
        [blocks[x, :, start : start + size].astype(F32) for x in range(blocks.shape[0])], axis=1
    )


def two_halves(rows_by_k, own, sibling):
    depth = own.shape[0]
    req = lax.axis_index("req")
    other = req + 1 - 2 * lax.rem(req, CORES)
    return dot(rows_by_k[:, at(req, depth)], own[...]) + dot(
        rows_by_k[:, at(other, depth)], sibling[...]
    )


def flatten(block, flat, start):
    group, steps, _ = block.shape
    for i in range(group):
        flat[start + i * steps : start + (i + 1) * steps, :] = block[i].astype(F32)


def norm_kernel(tokens, scales, *refs):
    count = (len(refs) - 3) // 2
    weights, out, kept = refs[:count], refs[count], refs[count + 1 : 2 * count + 1]
    flat, sems = refs[-2:]
    copies = [
        pltpu.make_async_copy(source, target, sems.at[k])
        for k, (source, target) in enumerate(zip(weights, kept))
    ]
    for copy in copies:
        copy.start()
    width = out.shape[1]
    flatten(tokens, flat, 0)
    out[...] = layer_norm(flat[...], scales[:, :width], scales[:, width:]).astype(BF16)
    for copy in copies:
        copy.wait()


def qkv_kernel(place, *refs):
    ny = place.ny
    mine = refs[0]
    toks = refs[1:ny]
    scales, biases = refs[ny : ny + 2]
    weights = refs[ny + 2 : ny + 8]
    outs = refs[ny + 8 : 2 * ny + 8]
    flat, normed = refs[2 * ny + 8 :]
    rows, width = mine.shape
    normed[:rows, :] = mine[...]
    for j, tok in enumerate(toks):
        flatten(tok, flat, j * rows)
    normed[rows:, :] = layer_norm(flat[...], scales[:, :width], scales[:, width:]).astype(BF16)
    cols = weights[0].shape[1]
    for k in range(3):
        acc = two_halves(normed, weights[k], weights[3 + k])
        for j in range(ny):
            part = acc[j * rows : (j + 1) * rows]
            if j == 0:
                part = part + biases[:, k * cols : (k + 1) * cols]
            outs[(ny - j) % ny][:, k * cols : (k + 1) * cols] = part.astype(BF16)


def add_columns_kernel(place, *refs):
    out = refs[-1]
    for dx in range(place.nx):
        total = refs[dx * place.ny][...].astype(F32)
        for dy in range(1, place.ny):
            total = total + refs[dx * place.ny + dy][...].astype(F32)
        out[place.x_before(dx)] = total.astype(BF16)


def cache_kernel(keys_in, values_in, keys_out, values_out, keys, values, mark, in_sems, out_sems):
    group = keys.shape[0]
    arrays = ((keys_in, keys, keys_out), (values_in, values, values_out))
    coming = [
        pltpu.make_async_copy(source.at[i], here.at[i], in_sems.at[k, i])
        for i in range(group)
        for k, (source, here, _) in enumerate(arrays)
    ]
    going = [
        pltpu.make_async_copy(here.at[i], target.at[i], out_sems.at[k, i])
        for i in range(group)
        for k, (_, here, target) in enumerate(arrays)
    ]
    for copy in coming:
        copy.start()
    mark[...] = jnp.zeros_like(mark)
    for arrived, copy in zip(coming, going):
        arrived.wait()
        copy.start()
    for copy in going:
        copy.wait()


def split_three(value):
    first = value.astype(BF16).astype(F32)
    rest = value - first
    second = rest.astype(BF16).astype(F32)
    return first, second, rest - second


def turn(value, by):
    return pltpu.roll(value, by % LANES, 1)


def pairs_of(query):
    side = lax.rem(lax.div(lax.broadcasted_iota(jnp.int32, query.shape, 1), HEAD), 2)
    return jnp.concatenate(
        [jnp.where(side == 0, query, 0.0), jnp.where(side == 1, query, 0.0)], axis=0
    ).astype(BF16)


def attention_kernel(place, heads, steps, *refs):
    nx, nz = place.nx, place.nz
    gathered = refs[:nz]
    lengths, keys, values = refs[nz : nz + 3]
    keys_out, values_out = refs[nz + 5 : nz + 7]
    messages = refs[nz + 7 : nz + 7 + nx]
    qs, ks, vs, scores, part, stats, k_rows, v_rows, sems = refs[nz + 7 + nx :]
    group, slots, width = keys.shape
    cols = width // place.seqs
    seq = lax.axis_index("seq")
    for dz in range(nz):
        span = at(place.z_partner(dz), nx * cols)
        for k, target in enumerate((qs, ks, vs)):
            target[:, span] = side_by_side(gathered[dz], k * cols, cols)

    window = k_rows.shape[1]

    def place_of(i):
        base = lengths[i] - seq * slots
        start = jnp.clip(lax.div(jnp.maximum(base, 0), 16) * 16, 0, slots - window)
        return base, pl.multiple_of(start, 16)

    def copies(i):
        _, start = place_of(i)
        return [
            pltpu.make_async_copy(
                rows.at[i], target.at[i, pl.ds(start, window), :], sems.at[k, i]
            )
            for k, (rows, target) in enumerate(((k_rows, keys_out), (v_rows, values_out)))
        ]

    for i in range(group):
        base, start = place_of(i)

        @pl.when((base > -steps) & (base < slots))
        def _():
            slot = start + lax.broadcasted_iota(jnp.int32, (window, width), 0)
            for source, fresh, rows in ((keys, ks, k_rows), (values, vs, v_rows)):
                block = source[i, pl.ds(start, window), :].astype(F32)
                for t in range(steps):
                    at_row = fresh[i * steps + t : i * steps + t + 1, :]
                    block = jnp.where(slot == base + t, at_row, block)
                rows[i] = block.astype(BF16)
            for copy in copies(i):
                copy.start()

    pack = max(1, min(group, 256 // slots))
    rows = pack * steps
    tile = 2 * HEAD
    left = lax.broadcasted_iota(jnp.int32, (rows, tile), 1) < HEAD
    many, cached = heads * rows, pack * slots
    row = lax.broadcasted_iota(jnp.int32, (many, cached + LANES), 0)
    column = lax.broadcasted_iota(jnp.int32, (many, cached + LANES), 1)
    owner = lax.div(lax.rem(row, rows), steps)
    position = lax.rem(column, slots)
    old = (column < cached) & (owner == lax.div(column, slots))
    new = column - cached
    later = lax.rem(new, steps)
    fresh = (
        (new >= 0)
        & (new < rows)
        & (lax.div(new, steps) == owner)
        & (later <= lax.rem(row, steps))
    )
    lane = lax.broadcasted_iota(jnp.int32, (rows, LANES), 1)
    blank = jnp.zeros((LANES - rows, width), BF16)
    for g in range(group // pack):
        mine = slice(g * rows, (g + 1) * rows)
        these = slice(g * pack, (g + 1) * pack)
        pair = pairs_of(qs[mine, :])
        key = keys[these].reshape(cached, width)
        value = values[these].reshape(cached, width)
        new_key = jnp.concatenate([ks[mine, :].astype(BF16), blank], axis=0)
        new_value = jnp.concatenate([vs[mine, :].astype(BF16), blank], axis=0)
        for j in range(heads // 2):
            span = slice(j * tile, (j + 1) * tile)
            these_rows = slice(j * 2 * rows, (j + 1) * 2 * rows)
            scores[these_rows, :cached] = across(pair[:, span], key[:, span])
            scores[these_rows, cached:] = across(pair[:, span], new_key[:, span])
        base = jnp.zeros_like(owner)
        for k in range(pack):
            base = jnp.where(owner == k, lengths[g * pack + k] - seq * slots, base)
        at_new = base + later
        valid = (old & (position < base)) | (fresh & (at_new >= 0) & (at_new < slots))
        masked = jnp.where(valid, scores[...] * HEAD ** (-0.5), -1e30)
        peak = jnp.max(masked, axis=-1, keepdims=True)
        expo = jnp.where(valid, jnp.exp(masked - peak), 0.0)
        total = jnp.sum(expo, axis=-1, keepdims=True)
        probs = expo.astype(BF16)
        for j in range(heads // 2):
            span = slice(j * tile, (j + 1) * tile)
            these_rows = slice(j * 2 * rows, (j + 1) * 2 * rows)
            mixed = dot(probs[these_rows, :cached], value[:, span])
            mixed = mixed + dot(probs[these_rows, cached:], new_value[:, span])
            part[mine, span] = jnp.where(left, mixed[:rows], mixed[rows:])
        line = jnp.zeros((rows, LANES), F32)
        for k, piece in enumerate(split_three(peak) + split_three(total)[:2]):
            for h in range(heads):
                line = jnp.where(lane == k * heads + h, piece[h * rows : (h + 1) * rows], line)
        stats[mine, :] = line
    share = width // nx
    for dx in range(nx):
        to = place.x_after(dx)
        messages[dx][:, :share] = part[:, at(to, share)].astype(BF16)
        messages[dx][:, share:] = pltpu.roll(
            stats[...], lax.rem(LANES - to * (heads // nx), LANES), 1
        ).astype(BF16)
    for i in range(group):
        base, _ = place_of(i)

        @pl.when((base > -steps) & (base < slots))
        def _():
            for copy in copies(i):
                copy.wait()


def expand(factor, count):
    rows = factor.shape[0]
    return jnp.concatenate(
        [jnp.broadcast_to(factor[:, h : h + 1], (rows, HEAD)) for h in range(count)], axis=1
    )


def merge(messages, heads, share):
    peaks, totals = [], []
    for message in messages:
        stats = message[:, share:].astype(F32)
        peaks.append(stats + turn(stats, -heads) + turn(stats, -2 * heads))
        totals.append(turn(stats, -3 * heads) + turn(stats, -4 * heads))
    peak = functools.reduce(jnp.maximum, peaks)
    scales = [jnp.exp(p - peak) for p in peaks]
    total = sum(t * s for t, s in zip(totals, scales))
    return peak, total, scales


def merge_x_kernel(place, heads, *refs):
    share = refs[0].shape[1] - LANES
    count = share // HEAD
    out = refs[-1]
    messages = [r[...] for r in refs[:-1]]
    peak, total, scales = merge(messages, heads, share)
    out[:, :share] = sum(
        m[:, :share].astype(F32) * expand(s, count) for m, s in zip(messages, scales)
    ).astype(BF16)
    lane = lax.broadcasted_iota(jnp.int32, peak.shape, 1)
    tile = jnp.zeros_like(peak)
    for k, piece in enumerate(split_three(peak) + split_three(total)[:2]):
        tile = tile + turn(jnp.where(lane < count, piece, 0.0), k * heads)
    out[:, share:] = tile.astype(BF16)


def merge_z_kernel(place, heads, *refs):
    share = refs[0].shape[1] - LANES
    count = share // HEAD
    out = refs[-1]
    messages = [r[...] for r in refs[:-1]]
    _, total, scales = merge(messages, heads, share)
    out[...] = sum(
        m[:, :share].astype(F32) * expand(s / total, count) for m, s in zip(messages, scales)
    ).astype(BF16)


def out_kernel(place, attn, *refs):
    nx = place.nx
    weights = refs[: 2 * nx]
    bias, out, total = refs[2 * nx :]
    depth = weights[0].shape[0]
    core = place.core()
    for k in range(nx):
        block = lax.rem(place.y() + k, nx)
        total[block] = dot(attn[:, at(core, depth)], weights[2 * k][...]) + dot(
            attn[:, at(1 - core, depth)], weights[2 * k + 1][...]
        )
    total[place.x()] = total[place.x()] + bias[...]
    out[...] = total[...].astype(BF16)


def add_out_kernel(place, *refs):
    out = refs[-1]
    for dy in range(place.ny):
        total = refs[dy][...].astype(F32)
        for dx in range(1, place.nx):
            total = total + refs[dx * place.ny + dy][...].astype(F32)
        out[place.y_before(dy)] = total.astype(BF16)


def up_kernel(place, *refs):
    ny, nz = place.ny, place.nz
    toks = refs[:ny]
    gathered = refs[ny : ny + nz]
    gain, shift, own, sibling, bias, out, mid_out, proj, normed, flat = refs[ny + nz :]
    group, steps, _ = toks[0].shape
    rows = group * steps
    cols = gathered[0].shape[3]
    for dz in range(nz):
        span = at(place.z_partner(dz), place.nx * cols)
        for y in range(ny):
            proj[y * rows : (y + 1) * rows, span] = side_by_side(gathered[dz].at[y], 0, cols)
    for j in range(ny):
        here = at(place.y_before(j), rows)
        flatten(toks[j], flat, 0)
        mid = flat[...] + proj[here, :]
        if j == 0:
            mid_out[...] = mid
        normed[here, :] = layer_norm(mid, gain[...], shift[...]).astype(BF16)
    first = (place.y() == 0).astype(F32)
    out[...] = (two_halves(normed, own, sibling) + bias[...] * first).astype(BF16)


def down_kernel(place, *refs):
    nx, ny = place.nx, place.ny
    parts = refs[:ny]
    own, sibling = refs[ny : ny + 2]
    outs = refs[ny + 2 : ny + 2 + nx]
    feed = refs[-1]
    total = sum(p[...].astype(F32) for p in parts)
    hidden = (0.5 * total * (1.0 + lax.erf(total * 0.5**0.5))).astype(BF16)
    ncols = own.shape[1]
    feed[:, at(place.core(), ncols)] = dot(hidden, own[...])
    feed[:, at(1 - place.core(), ncols)] = dot(hidden, sibling[...])
    width = outs[0].shape[1]
    for dx in range(nx):
        outs[dx][...] = feed[:, at(place.x_after(dx), width)].astype(BF16)


def add_x_kernel(place, *refs):
    refs[-1][...] = sum(r[...].astype(F32) for r in refs[:-1]).astype(BF16)


def add_z_kernel(place, *refs):
    outs, total = refs[place.nz : -1], refs[-1]
    total[...] = sum(r[...].astype(F32) for r in refs[: place.nz])
    rows = outs[0].shape[0]
    for dy in range(place.ny):
        outs[dy][...] = total[at(lax.rem(place.y() + dy, place.ny), rows), :].astype(BF16)


def last_kernel(place, *refs):
    nx, ny = place.nx, place.ny
    parts = refs[: nx * ny]
    mid, bias, out, full = refs[nx * ny :]
    group, steps, _ = out.shape
    width = parts[0].shape[1]
    for dx in range(nx):
        for dy in range(ny):
            block = place.y_before(dy) * nx + place.x_before(dx)
            full[:, at(block, width)] = parts[dx * ny + dy][...].astype(F32)
    result = mid[...] + full[...] + bias[...]
    for i in range(group):
        out[i] = result[i * steps : (i + 1) * steps].astype(BF16)


def shape(sizes, kind=BF16):
    return jax.ShapeDtypeStruct(tuple(sizes), kind)


def body(
    tokens,
    lengths,
    cache_keys,
    cache_values,
    norm1_gain,
    norm1_bias,
    w_query,
    b_query,
    w_key,
    b_key,
    w_value,
    b_value,
    w_out,
    b_out,
    norm2_gain,
    norm2_bias,
    w_up,
    b_up,
    w_down,
    b_down,
):
    place = Place(lax.axis_size("seq"), lax.axis_size("req"))
    nx, ny = place.nx, place.ny
    group, steps, width = tokens.shape
    slots = cache_keys.shape[1]
    rows = group * steps
    heads = width // HEAD
    share = width // nx
    bind = functools.partial

    def row(vector):
        return vector.reshape(1, -1)

    def spread(by_dy):
        return [
            by_dy[dy] if dx == 0 and dy == 0 else place.move(by_dy[dy], dx, dy)
            for dx in range(nx)
            for dy in range(ny)
        ]

    toks = [tokens] + [place.move(tokens, dy=dy) for dy in range(1, ny)]
    cols = w_query.shape[1]
    own = [w_query, w_key, w_value]
    siblings = [place.move(weight, dc=1) for weight in own]
    scales = row(jnp.concatenate([norm1_gain, norm1_bias]))
    biases = row(jnp.concatenate([b_query, b_key, b_value]))
    normed, *own = call(
        norm_kernel,
        "norm",
        [tokens, scales, *own],
        [shape((rows, width))] + [shape(w.shape) for w in own],
        in_specs=[VMEM] * 2 + [HBM] * 3,
        scratch=[pltpu.VMEM((rows, width), F32), pltpu.SemaphoreType.DMA((3,))],
        limit=52.75,
    )
    parts = call(
        bind(qkv_kernel, place),
        "norm_qkv",
        [normed, *toks[1:], scales, biases, *own, *siblings],
        [shape((rows, 3 * cols))] * ny,
        scratch=[pltpu.VMEM(((ny - 1) * rows, width), F32), pltpu.VMEM((ny * rows, width), BF16)],
    )
    *parts, tied_up, tied_down = lax.optimization_barrier((*parts, w_up, w_down))
    w_up_sibling = place.move(tied_up, dc=1)
    w_down_sibling = place.move(tied_down, dc=1)
    parts, tied_keys, tied_values = lax.optimization_barrier((parts, cache_keys, cache_values))
    new_keys, new_values, keys, values, mark = call(
        cache_kernel,
        "caches",
        [tied_keys, tied_values],
        [shape(cache_keys.shape)] * 4 + [shape((8, LANES), F32)],
        in_specs=[HBM, HBM],
        out_specs=[HBM, HBM, VMEM, VMEM, VMEM],
        scratch=[pltpu.SemaphoreType.DMA((2, group)), pltpu.SemaphoreType.DMA((2, group))],
        moved=16 * 1024 * 1024,
        limit=46,
    )
    qkv = call(
        bind(add_columns_kernel, place),
        "add_qkv",
        [*spread(parts), mark],
        shape((nx, rows, 3 * cols)),
    )
    qkv, w_up_sibling, w_down_sibling, tied = lax.optimization_barrier(
        (qkv, w_up_sibling, w_down_sibling, w_out)
    )
    pieces = place.gather_z(qkv)
    blocks = [place.transpose(tied, k) for k in range(nx)]
    pack = max(1, min(group, 256 // slots))
    window = min(32, slots)
    new_keys, new_values, *messages = call(
        bind(attention_kernel, place, heads, steps),
        "attention",
        [*pieces, lengths, keys, values, new_keys, new_values],
        [shape(cache_keys.shape)] * 2 + [shape((rows, share + LANES))] * nx,
        in_specs=[VMEM] * place.nz + [SMEM, VMEM, VMEM, HBM, HBM],
        out_specs=[HBM, HBM] + [VMEM] * nx,
        scratch=[
            pltpu.VMEM((rows, width), F32),
            pltpu.VMEM((rows, width), F32),
            pltpu.VMEM((rows, width), F32),
            pltpu.VMEM((heads * pack * steps, pack * slots + LANES), F32),
            pltpu.VMEM((rows, width), F32),
            pltpu.VMEM((rows, LANES), F32),
            pltpu.VMEM((group, window, width), BF16),
            pltpu.VMEM((group, window, width), BF16),
            pltpu.SemaphoreType.DMA((2, group)),
        ],
        aliases={place.nz + 3: 0, place.nz + 4: 1},
    )
    messages, blocks = lax.optimization_barrier((messages, blocks))
    w_outs = []
    for block in blocks:
        w_outs += [block, place.move(block, dc=1)]
    messages = [messages[0]] + [place.move(messages[dx], dx=dx) for dx in range(1, nx)]
    merged = call(
        bind(merge_x_kernel, place, heads), "merge_x", messages, shape((rows, share + LANES))
    )
    merged, *w_outs = lax.optimization_barrier((merged, *w_outs))
    pieces = place.gather_z(merged)
    attn = call(bind(merge_z_kernel, place, heads), "merge_z", pieces, shape((rows, share)))
    out_part = call(
        bind(out_kernel, place),
        "out",
        [attn, *w_outs, row(b_out)],
        shape((nx, rows, cols)),
        scratch=[pltpu.VMEM((nx, rows, cols), F32)],
    )
    projected = call(
        bind(add_out_kernel, place),
        "add_out",
        spread([out_part] * ny),
        shape((ny, nx, rows, cols)),
    )
    up_part, mid = call(
        bind(up_kernel, place),
        "norm_up",
        [
            *toks,
            *place.gather_z(projected),
            row(norm2_gain),
            row(norm2_bias),
            w_up,
            w_up_sibling,
            row(b_up),
        ],
        [shape((ny * rows, w_up.shape[1])), shape((rows, width), F32)],
        scratch=[
            pltpu.VMEM((ny * rows, width), F32),
            pltpu.VMEM((ny * rows, width), BF16),
            pltpu.VMEM((rows, width), F32),
        ],
    )
    up_parts = [up_part] + [place.move(up_part, dy=dy) for dy in range(1, ny)]
    piece = CORES * w_down.shape[1] // nx
    feeds = call(
        bind(down_kernel, place),
        "gelu_down",
        [*up_parts, w_down, w_down_sibling],
        [shape((ny * rows, piece))] * nx,
        scratch=[pltpu.VMEM((ny * rows, CORES * w_down.shape[1]), F32)],
    )
    feeds = [feeds[0]] + [place.move(feeds[dx], dx=dx) for dx in range(1, nx)]
    feed = call(bind(add_x_kernel, place), "add_x", feeds, shape((ny * rows, piece)))
    summed = call(
        bind(add_z_kernel, place),
        "add_z",
        place.gather_z(feed),
        [shape((rows, piece))] * ny,
        scratch=[pltpu.VMEM((ny * rows, piece), F32)],
    )
    hidden_out = call(
        bind(last_kernel, place),
        "last",
        [*spread(summed), mid, row(b_down)],
        shape(tokens.shape),
        scratch=[pltpu.VMEM((rows, width), F32)],
    )
    return (hidden_out, new_keys, new_values)


def solution(mesh):
    in_specs = (
        P("req", None, None),
        P("req"),
        P("req", "seq", None),
        P("req", "seq", None),
        P(),
        P(),
        P("req", "seq"),
        P("seq"),
        P("req", "seq"),
        P("seq"),
        P("req", "seq"),
        P("seq"),
        P("req", "seq"),
        P("seq"),
        P(),
        P(),
        P("req", "seq"),
        P("seq"),
        P("seq", "req"),
        P(),
    )
    out_specs = (P("req", None, None), P("req", "seq", None), P("req", "seq", None))
    return jax.shard_map(body, mesh=mesh, in_specs=in_specs, out_specs=out_specs, check_vma=False)
```

```python
import functools

import jax
import jax.numpy as jnp
from jax import lax
from jax.experimental import pallas as pl
from jax.experimental.pallas import tpu as pltpu
from jax.sharding import PartitionSpec as P

HEAD = 128
LANES = 128
CORES = 2
BF16 = jnp.bfloat16
F32 = jnp.float32
VMEM = pl.BlockSpec(memory_space=pltpu.VMEM)
SMEM = pl.BlockSpec(memory_space=pltpu.SMEM)
HBM = pl.BlockSpec(memory_space=pltpu.HBM)


class Place:
    def __init__(self, seqs, reqs):
        self.ny = reqs // CORES
        self.nx = self.ny
        self.nz = seqs // self.nx
        self.seqs = seqs

    def x(self):
        return lax.rem(lax.axis_index("seq"), self.nx)

    def y(self):
        return lax.div(lax.axis_index("req"), CORES)

    def core(self):
        return lax.rem(lax.axis_index("req"), CORES)

    def x_before(self, dx):
        return lax.rem(self.x() + self.nx - dx, self.nx)

    def x_after(self, dx):
        return lax.rem(self.x() + dx, self.nx)

    def y_before(self, dy):
        return lax.rem(self.y() + self.ny - dy, self.ny)

    def z_partner(self, dz):
        return lax.bitwise_xor(lax.div(lax.axis_index("seq"), self.nx), dz)

    def move(self, value, dx=0, dy=0, dc=0, dz=0):
        pairs = []
        for z in range(self.nz):
            for x in range(self.nx):
                for y in range(self.ny):
                    for c in range(CORES):
                        to_x, to_y, to_c = (x + dx) % self.nx, (y + dy) % self.ny, (c + dc) % CORES
                        to_z = z ^ dz
                        pairs.append(
                            (
                                ((z * self.nx + x) * self.ny + y) * CORES + c,
                                ((to_z * self.nx + to_x) * self.ny + to_y) * CORES + to_c,
                            )
                        )
        return lax.ppermute(value, ("seq", "req"), pairs)

    def transpose(self, value, k):
        n = self.nx
        pairs = []
        for z in range(self.nz):
            for x in range(n):
                for y in range(n):
                    for c in range(CORES):
                        pairs.append(
                            (
                                ((z * n + x) * n + y) * CORES + c,
                                ((z * n + y) * n + (x - k) % n) * CORES + c,
                            )
                        )
        return lax.ppermute(value, ("seq", "req"), pairs)

    def gather_z(self, value):
        return [value] + [self.move(value, dz=dz) for dz in range(1, self.nz)]


def layer_norm(values, gain, shift):
    center = values - jnp.mean(values, axis=-1, keepdims=True)
    spread = jnp.mean(center * center, axis=-1, keepdims=True)
    return center * lax.rsqrt(spread + 1e-05) * gain + shift


def dot(a, b):
    return jnp.dot(a, b, preferred_element_type=F32)


def across(a, b):
    return lax.dot_general(a, b, (((1,), (1,)), ((), ())), preferred_element_type=F32)


def at(index, size):
    return pl.ds(pl.multiple_of(index * size, size), size)


def call(kernel, name, ins, outs, in_specs=None, out_specs=None, scratch=(), moved=2**20, limit=20, aliases=None):
    single = not isinstance(outs, (list, tuple))
    specs = out_specs or (VMEM if single else [VMEM] * len(outs))
    return pl.pallas_call(
        kernel,
        name=name,
        out_shape=outs,
        in_specs=in_specs or [VMEM] * len(ins),
        out_specs=specs,
        scratch_shapes=list(scratch),
        input_output_aliases=aliases or {},
        cost_estimate=pl.CostEstimate(flops=0, bytes_accessed=moved, transcendentals=0),
        compiler_params=pltpu.CompilerParams(vmem_limit_bytes=int(limit * 1024 * 1024)),
    )(*ins)


def side_by_side(blocks, start, size):
    return jnp.concatenate(
        [blocks[x, :, start : start + size].astype(F32) for x in range(blocks.shape[0])], axis=1
    )


def two_halves(rows_by_k, own, sibling):
    depth = own.shape[0]
    req = lax.axis_index("req")
    other = req + 1 - 2 * lax.rem(req, CORES)
    return dot(rows_by_k[:, at(req, depth)], own[...]) + dot(
        rows_by_k[:, at(other, depth)], sibling[...]
    )


def flatten(block, flat, start):
    group, steps, _ = block.shape
    for i in range(group):
        flat[start + i * steps : start + (i + 1) * steps, :] = block[i].astype(F32)


def norm_kernel(tokens, scales, *refs):
    count = (len(refs) - 3) // 2
    weights, out, kept = refs[:count], refs[count], refs[count + 1 : 2 * count + 1]
    flat, sems = refs[-2:]
    copies = [
        pltpu.make_async_copy(source, target, sems.at[k])
        for k, (source, target) in enumerate(zip(weights, kept))
    ]
    for copy in copies:
        copy.start()
    width = out.shape[1]
    flatten(tokens, flat, 0)
    out[...] = layer_norm(flat[...], scales[:, :width], scales[:, width:]).astype(BF16)
    for copy in copies:
        copy.wait()


def qkv_kernel(place, *refs):
    ny = place.ny
    mine = refs[0]
    toks = refs[1:ny]
    scales, biases = refs[ny : ny + 2]
    weights = refs[ny + 2 : ny + 8]
    outs = refs[ny + 8 : 2 * ny + 8]
    flat, normed = refs[2 * ny + 8 :]
    rows, width = mine.shape
    normed[:rows, :] = mine[...]
    for j, tok in enumerate(toks):
        flatten(tok, flat, j * rows)
    normed[rows:, :] = layer_norm(flat[...], scales[:, :width], scales[:, width:]).astype(BF16)
    cols = weights[0].shape[1]
    for k in range(3):
        acc = two_halves(normed, weights[k], weights[3 + k])
        for j in range(ny):
            part = acc[j * rows : (j + 1) * rows]
            if j == 0:
                part = part + biases[:, k * cols : (k + 1) * cols]
            outs[(ny - j) % ny][:, k * cols : (k + 1) * cols] = part.astype(BF16)


def add_columns_kernel(place, *refs):
    out = refs[-1]
    for dx in range(place.nx):
        total = refs[dx * place.ny][...].astype(F32)
        for dy in range(1, place.ny):
            total = total + refs[dx * place.ny + dy][...].astype(F32)
        out[place.x_before(dx)] = total.astype(BF16)


def cache_kernel(keys_in, values_in, keys_out, values_out, keys, values, mark, in_sems, out_sems):
    group = keys.shape[0]
    arrays = ((keys_in, keys, keys_out), (values_in, values, values_out))
    coming = [
        pltpu.make_async_copy(source.at[i], here.at[i], in_sems.at[k, i])
        for i in range(group)
        for k, (source, here, _) in enumerate(arrays)
    ]
    going = [
        pltpu.make_async_copy(here.at[i], target.at[i], out_sems.at[k, i])
        for i in range(group)
        for k, (_, here, target) in enumerate(arrays)
    ]
    for copy in coming:
        copy.start()
    mark[...] = jnp.zeros_like(mark)
    for arrived, copy in zip(coming, going):
        arrived.wait()
        copy.start()
    for copy in going:
        copy.wait()


def split_three(value):
    first = value.astype(BF16).astype(F32)
    rest = value - first
    second = rest.astype(BF16).astype(F32)
    return first, second, rest - second


def turn(value, by):
    return pltpu.roll(value, by % LANES, 1)


def pairs_of(query):
    side = lax.rem(lax.div(lax.broadcasted_iota(jnp.int32, query.shape, 1), HEAD), 2)
    return jnp.concatenate(
        [jnp.where(side == 0, query, 0.0), jnp.where(side == 1, query, 0.0)], axis=0
    ).astype(BF16)


def attention_kernel(place, heads, steps, *refs):
    nx, nz = place.nx, place.nz
    gathered = refs[:nz]
    lengths, keys, values = refs[nz : nz + 3]
    keys_out, values_out = refs[nz + 5 : nz + 7]
    messages = refs[nz + 7 : nz + 7 + nx]
    qs, ks, vs, scores, part, stats, k_rows, v_rows, sems = refs[nz + 7 + nx :]
    group, slots, width = keys.shape
    cols = width // place.seqs
    seq = lax.axis_index("seq")
    for dz in range(nz):
        span = at(place.z_partner(dz), nx * cols)
        for k, target in enumerate((qs, ks, vs)):
            target[:, span] = side_by_side(gathered[dz], k * cols, cols)

    window = k_rows.shape[1]

    def place_of(i):
        base = lengths[i] - seq * slots
        start = jnp.clip(lax.div(jnp.maximum(base, 0), 16) * 16, 0, slots - window)
        return base, pl.multiple_of(start, 16)

    def copies(i):
        _, start = place_of(i)
        return [
            pltpu.make_async_copy(
                rows.at[i], target.at[i, pl.ds(start, window), :], sems.at[k, i]
            )
            for k, (rows, target) in enumerate(((k_rows, keys_out), (v_rows, values_out)))
        ]

    for i in range(group):
        base, start = place_of(i)

        @pl.when((base > -steps) & (base < slots))
        def _():
            slot = start + lax.broadcasted_iota(jnp.int32, (window, width), 0)
            for source, fresh, rows in ((keys, ks, k_rows), (values, vs, v_rows)):
                block = source[i, pl.ds(start, window), :].astype(F32)
                for t in range(steps):
                    at_row = fresh[i * steps + t : i * steps + t + 1, :]
                    block = jnp.where(slot == base + t, at_row, block)
                rows[i] = block.astype(BF16)
            for copy in copies(i):
                copy.start()

    pack = max(1, min(group, 256 // slots))
    rows = pack * steps
    tile = 2 * HEAD
    left = lax.broadcasted_iota(jnp.int32, (rows, tile), 1) < HEAD
    many, cached = heads * rows, pack * slots
    row = lax.broadcasted_iota(jnp.int32, (many, cached + LANES), 0)
    column = lax.broadcasted_iota(jnp.int32, (many, cached + LANES), 1)
    owner = lax.div(lax.rem(row, rows), steps)
    position = lax.rem(column, slots)
    old = (column < cached) & (owner == lax.div(column, slots))
    new = column - cached
    later = lax.rem(new, steps)
    fresh = (
        (new >= 0)
        & (new < rows)
        & (lax.div(new, steps) == owner)
        & (later <= lax.rem(row, steps))
    )
    lane = lax.broadcasted_iota(jnp.int32, (rows, LANES), 1)
    blank = jnp.zeros((LANES - rows, width), BF16)
    for g in range(group // pack):
        mine = slice(g * rows, (g + 1) * rows)
        these = slice(g * pack, (g + 1) * pack)
        pair = pairs_of(qs[mine, :])
        key = keys[these].reshape(cached, width)
        value = values[these].reshape(cached, width)
        new_key = jnp.concatenate([ks[mine, :].astype(BF16), blank], axis=0)
        new_value = jnp.concatenate([vs[mine, :].astype(BF16), blank], axis=0)
        for j in range(heads // 2):
            span = slice(j * tile, (j + 1) * tile)
            these_rows = slice(j * 2 * rows, (j + 1) * 2 * rows)
            scores[these_rows, :cached] = across(pair[:, span], key[:, span])
            scores[these_rows, cached:] = across(pair[:, span], new_key[:, span])
        base = jnp.zeros_like(owner)
        for k in range(pack):
            base = jnp.where(owner == k, lengths[g * pack + k] - seq * slots, base)
        at_new = base + later
        valid = (old & (position < base)) | (fresh & (at_new >= 0) & (at_new < slots))
        masked = jnp.where(valid, scores[...] * HEAD ** (-0.5), -1e30)
        peak = jnp.max(masked, axis=-1, keepdims=True)
        expo = jnp.where(valid, jnp.exp(masked - peak), 0.0)
        total = jnp.sum(expo, axis=-1, keepdims=True)
        probs = expo.astype(BF16)
        for j in range(heads // 2):
            span = slice(j * tile, (j + 1) * tile)
            these_rows = slice(j * 2 * rows, (j + 1) * 2 * rows)
            mixed = dot(probs[these_rows, :cached], value[:, span])
            mixed = mixed + dot(probs[these_rows, cached:], new_value[:, span])
            part[mine, span] = jnp.where(left, mixed[:rows], mixed[rows:])
        line = jnp.zeros((rows, LANES), F32)
        for k, piece in enumerate(split_three(peak) + split_three(total)[:2]):
            for h in range(heads):
                line = jnp.where(lane == k * heads + h, piece[h * rows : (h + 1) * rows], line)
        stats[mine, :] = line
    share = width // nx
    for dx in range(nx):
        to = place.x_after(dx)
        messages[dx][:, :share] = part[:, at(to, share)].astype(BF16)
        messages[dx][:, share:] = pltpu.roll(
            stats[...], lax.rem(LANES - to * (heads // nx), LANES), 1
        ).astype(BF16)
    for i in range(group):
        base, _ = place_of(i)

        @pl.when((base > -steps) & (base < slots))
        def _():
            for copy in copies(i):
                copy.wait()


def expand(factor, count):
    rows = factor.shape[0]
    return jnp.concatenate(
        [jnp.broadcast_to(factor[:, h : h + 1], (rows, HEAD)) for h in range(count)], axis=1
    )


def merge(messages, heads, share):
    peaks, totals = [], []
    for message in messages:
        stats = message[:, share:].astype(F32)
        peaks.append(stats + turn(stats, -heads) + turn(stats, -2 * heads))
        totals.append(turn(stats, -3 * heads) + turn(stats, -4 * heads))
    peak = functools.reduce(jnp.maximum, peaks)
    scales = [jnp.exp(p - peak) for p in peaks]
    total = sum(t * s for t, s in zip(totals, scales))
    return peak, total, scales


def merge_x_kernel(place, heads, *refs):
    share = refs[0].shape[1] - LANES
    count = share // HEAD
    out = refs[-1]
    messages = [r[...] for r in refs[:-1]]
    peak, total, scales = merge(messages, heads, share)
    out[:, :share] = sum(
        m[:, :share].astype(F32) * expand(s, count) for m, s in zip(messages, scales)
    ).astype(BF16)
    lane = lax.broadcasted_iota(jnp.int32, peak.shape, 1)
    tile = jnp.zeros_like(peak)
    for k, piece in enumerate(split_three(peak) + split_three(total)[:2]):
        tile = tile + turn(jnp.where(lane < count, piece, 0.0), k * heads)
    out[:, share:] = tile.astype(BF16)


def merge_z_kernel(place, heads, *refs):
    share = refs[0].shape[1] - LANES
    count = share // HEAD
    out = refs[-1]
    messages = [r[...] for r in refs[:-1]]
    _, total, scales = merge(messages, heads, share)
    out[...] = sum(
        m[:, :share].astype(F32) * expand(s / total, count) for m, s in zip(messages, scales)
    ).astype(BF16)


def out_kernel(place, attn, *refs):
    nx = place.nx
    weights = refs[: 2 * nx]
    bias, out, total = refs[2 * nx :]
    depth = weights[0].shape[0]
    core = place.core()
    for k in range(nx):
        block = lax.rem(place.y() + k, nx)
        total[block] = dot(attn[:, at(core, depth)], weights[2 * k][...]) + dot(
            attn[:, at(1 - core, depth)], weights[2 * k + 1][...]
        )
    total[place.x()] = total[place.x()] + bias[...]
    out[...] = total[...].astype(BF16)


def add_out_kernel(place, *refs):
    out = refs[-1]
    for dy in range(place.ny):
        total = refs[dy][...].astype(F32)
        for dx in range(1, place.nx):
            total = total + refs[dx * place.ny + dy][...].astype(F32)
        out[place.y_before(dy)] = total.astype(BF16)


def up_kernel(place, *refs):
    ny, nz = place.ny, place.nz
    toks = refs[:ny]
    gathered = refs[ny : ny + nz]
    gain, shift, own, sibling, bias, out, mid_out, proj, normed, flat = refs[ny + nz :]
    group, steps, _ = toks[0].shape
    rows = group * steps
    cols = gathered[0].shape[3]
    for dz in range(nz):
        span = at(place.z_partner(dz), place.nx * cols)
        for y in range(ny):
            proj[y * rows : (y + 1) * rows, span] = side_by_side(gathered[dz].at[y], 0, cols)
    for j in range(ny):
        here = at(place.y_before(j), rows)
        flatten(toks[j], flat, 0)
        mid = flat[...] + proj[here, :]
        if j == 0:
            mid_out[...] = mid
        normed[here, :] = layer_norm(mid, gain[...], shift[...]).astype(BF16)
    first = (place.y() == 0).astype(F32)
    out[...] = (two_halves(normed, own, sibling) + bias[...] * first).astype(BF16)


def down_kernel(place, *refs):
    ny = place.ny
    parts = refs[:ny]
    own, sibling, out, feed = refs[ny:]
    total = sum(p[...].astype(F32) for p in parts)
    hidden = (0.5 * total * (1.0 + lax.erf(total * 0.5**0.5))).astype(BF16)
    ncols = own.shape[1]
    feed[:, at(place.core(), ncols)] = dot(hidden, own[...])
    feed[:, at(1 - place.core(), ncols)] = dot(hidden, sibling[...])
    out[...] = feed[...].astype(BF16)


def add_z_kernel(place, *refs):
    outs, total = refs[place.nz : -1], refs[-1]
    total[...] = sum(r[...].astype(F32) for r in refs[: place.nz])
    rows = outs[0].shape[0]
    for dy in range(place.ny):
        outs[dy][...] = total[at(lax.rem(place.y() + dy, place.ny), rows), :].astype(BF16)


def last_kernel(place, *refs):
    nx, ny = place.nx, place.ny
    parts = refs[: nx * ny]
    mid, bias, out, full = refs[nx * ny :]
    group, steps, _ = out.shape
    width = parts[0].shape[1]
    for dy in range(ny):
        total = parts[dy][...].astype(F32)
        for dx in range(1, nx):
            total = total + parts[dx * ny + dy][...].astype(F32)
        full[:, at(place.y_before(dy), width)] = total
    result = mid[...] + full[...] + bias[...]
    for i in range(group):
        out[i] = result[i * steps : (i + 1) * steps].astype(BF16)


def shape(sizes, kind=BF16):
    return jax.ShapeDtypeStruct(tuple(sizes), kind)


def body(
    tokens,
    lengths,
    cache_keys,
    cache_values,
    norm1_gain,
    norm1_bias,
    w_query,
    b_query,
    w_key,
    b_key,
    w_value,
    b_value,
    w_out,
    b_out,
    norm2_gain,
    norm2_bias,
    w_up,
    b_up,
    w_down,
    b_down,
):
    place = Place(lax.axis_size("seq"), lax.axis_size("req"))
    nx, ny = place.nx, place.ny
    group, steps, width = tokens.shape
    slots = cache_keys.shape[1]
    rows = group * steps
    heads = width // HEAD
    share = width // nx
    bind = functools.partial

    def row(vector):
        return vector.reshape(1, -1)

    def spread(by_dy):
        return [
            by_dy[dy] if dx == 0 and dy == 0 else place.move(by_dy[dy], dx, dy)
            for dx in range(nx)
            for dy in range(ny)
        ]

    toks = [tokens] + [place.move(tokens, dy=dy) for dy in range(1, ny)]
    cols = w_query.shape[1]
    own = [w_query, w_key, w_value]
    siblings = [place.move(weight, dc=1) for weight in own]
    scales = row(jnp.concatenate([norm1_gain, norm1_bias]))
    biases = row(jnp.concatenate([b_query, b_key, b_value]))
    normed, *own = call(
        norm_kernel,
        "norm",
        [tokens, scales, *own],
        [shape((rows, width))] + [shape(w.shape) for w in own],
        in_specs=[VMEM] * 2 + [HBM] * 3,
        scratch=[pltpu.VMEM((rows, width), F32), pltpu.SemaphoreType.DMA((3,))],
        limit=52.75,
    )
    parts = call(
        bind(qkv_kernel, place),
        "norm_qkv",
        [normed, *toks[1:], scales, biases, *own, *siblings],
        [shape((rows, 3 * cols))] * ny,
        scratch=[pltpu.VMEM(((ny - 1) * rows, width), F32), pltpu.VMEM((ny * rows, width), BF16)],
    )
    *parts, tied_up, tied_down = lax.optimization_barrier((*parts, w_up, w_down))
    w_up_sibling = place.move(tied_up, dc=1)
    w_down_sibling = place.move(tied_down, dc=1)
    parts, tied_keys, tied_values = lax.optimization_barrier((parts, cache_keys, cache_values))
    new_keys, new_values, keys, values, mark = call(
        cache_kernel,
        "caches",
        [tied_keys, tied_values],
        [shape(cache_keys.shape)] * 4 + [shape((8, LANES), F32)],
        in_specs=[HBM, HBM],
        out_specs=[HBM, HBM, VMEM, VMEM, VMEM],
        scratch=[pltpu.SemaphoreType.DMA((2, group)), pltpu.SemaphoreType.DMA((2, group))],
        moved=16 * 1024 * 1024,
        limit=46,
    )
    qkv = call(
        bind(add_columns_kernel, place),
        "add_qkv",
        [*spread(parts), mark],
        shape((nx, rows, 3 * cols)),
    )
    qkv, w_up_sibling, w_down_sibling, tied = lax.optimization_barrier(
        (qkv, w_up_sibling, w_down_sibling, w_out)
    )
    pieces = place.gather_z(qkv)
    blocks = [place.transpose(tied, k) for k in range(nx)]
    pack = max(1, min(group, 256 // slots))
    window = min(32, slots)
    new_keys, new_values, *messages = call(
        bind(attention_kernel, place, heads, steps),
        "attention",
        [*pieces, lengths, keys, values, new_keys, new_values],
        [shape(cache_keys.shape)] * 2 + [shape((rows, share + LANES))] * nx,
        in_specs=[VMEM] * place.nz + [SMEM, VMEM, VMEM, HBM, HBM],
        out_specs=[HBM, HBM] + [VMEM] * nx,
        scratch=[
            pltpu.VMEM((rows, width), F32),
            pltpu.VMEM((rows, width), F32),
            pltpu.VMEM((rows, width), F32),
            pltpu.VMEM((heads * pack * steps, pack * slots + LANES), F32),
            pltpu.VMEM((rows, width), F32),
            pltpu.VMEM((rows, LANES), F32),
            pltpu.VMEM((group, window, width), BF16),
            pltpu.VMEM((group, window, width), BF16),
            pltpu.SemaphoreType.DMA((2, group)),
        ],
        aliases={place.nz + 3: 0, place.nz + 4: 1},
    )
    messages, blocks = lax.optimization_barrier((messages, blocks))
    w_outs = []
    for block in blocks:
        w_outs += [block, place.move(block, dc=1)]
    messages = [messages[0]] + [place.move(messages[dx], dx=dx) for dx in range(1, nx)]
    merged = call(
        bind(merge_x_kernel, place, heads), "merge_x", messages, shape((rows, share + LANES))
    )
    merged, *w_outs = lax.optimization_barrier((merged, *w_outs))
    pieces = place.gather_z(merged)
    attn = call(bind(merge_z_kernel, place, heads), "merge_z", pieces, shape((rows, share)))
    out_part = call(
        bind(out_kernel, place),
        "out",
        [attn, *w_outs, row(b_out)],
        shape((nx, rows, cols)),
        scratch=[pltpu.VMEM((nx, rows, cols), F32)],
    )
    projected = call(
        bind(add_out_kernel, place),
        "add_out",
        spread([out_part] * ny),
        shape((ny, nx, rows, cols)),
    )
    up_part, mid = call(
        bind(up_kernel, place),
        "norm_up",
        [
            *toks,
            *place.gather_z(projected),
            row(norm2_gain),
            row(norm2_bias),
            w_up,
            w_up_sibling,
            row(b_up),
        ],
        [shape((ny * rows, w_up.shape[1])), shape((rows, width), F32)],
        scratch=[
            pltpu.VMEM((ny * rows, width), F32),
            pltpu.VMEM((ny * rows, width), BF16),
            pltpu.VMEM((rows, width), F32),
        ],
    )
    up_parts = [up_part] + [place.move(up_part, dy=dy) for dy in range(1, ny)]
    piece = CORES * w_down.shape[1]
    feed = call(
        bind(down_kernel, place),
        "gelu_down",
        [*up_parts, w_down, w_down_sibling],
        shape((ny * rows, piece)),
        scratch=[pltpu.VMEM((ny * rows, piece), F32)],
    )
    summed = call(
        bind(add_z_kernel, place),
        "add_z",
        place.gather_z(feed),
        [shape((rows, piece))] * ny,
        scratch=[pltpu.VMEM((ny * rows, piece), F32)],
    )
    hidden_out = call(
        bind(last_kernel, place),
        "last",
        [*spread(summed), mid, row(b_down)],
        shape(tokens.shape),
        scratch=[pltpu.VMEM((rows, width), F32)],
    )
    return (hidden_out, new_keys, new_values)


def solution(mesh):
    in_specs = (
        P("req", None, None),
        P("req"),
        P("req", "seq", None),
        P("req", "seq", None),
        P(),
        P(),
        P("req", "seq"),
        P("seq"),
        P("req", "seq"),
        P("seq"),
        P("req", "seq"),
        P("seq"),
        P("req", "seq"),
        P("seq"),
        P(),
        P(),
        P("req", "seq"),
        P("seq"),
        P("seq", "req"),
        P(),
    )
    out_specs = (P("req", None, None), P("req", "seq", None), P("req", "seq", None))
    return jax.shard_map(body, mesh=mesh, in_specs=in_specs, out_specs=out_specs, check_vma=False)
```

```python
import functools

import jax
import jax.numpy as jnp
from jax import lax
from jax.experimental import pallas as pl
from jax.experimental.pallas import tpu as pltpu
from jax.sharding import PartitionSpec as P

HEAD = 128
LANES = 128
CORES = 2
BF16 = jnp.bfloat16
F32 = jnp.float32
VMEM = pl.BlockSpec(memory_space=pltpu.VMEM)
SMEM = pl.BlockSpec(memory_space=pltpu.SMEM)
HBM = pl.BlockSpec(memory_space=pltpu.HBM)


class Place:
    def __init__(self, seqs, reqs):
        self.ny = reqs // CORES
        self.nx = self.ny
        self.nz = seqs // self.nx
        self.seqs = seqs

    def x(self):
        return lax.rem(lax.axis_index("seq"), self.nx)

    def y(self):
        return lax.div(lax.axis_index("req"), CORES)

    def core(self):
        return lax.rem(lax.axis_index("req"), CORES)

    def x_before(self, dx):
        return lax.rem(self.x() + self.nx - dx, self.nx)

    def x_after(self, dx):
        return lax.rem(self.x() + dx, self.nx)

    def y_before(self, dy):
        return lax.rem(self.y() + self.ny - dy, self.ny)

    def z_partner(self, dz):
        return lax.bitwise_xor(lax.div(lax.axis_index("seq"), self.nx), dz)

    def move(self, value, dx=0, dy=0, dc=0, dz=0):
        pairs = []
        for z in range(self.nz):
            for x in range(self.nx):
                for y in range(self.ny):
                    for c in range(CORES):
                        to_x, to_y, to_c = (x + dx) % self.nx, (y + dy) % self.ny, (c + dc) % CORES
                        to_z = z ^ dz
                        pairs.append(
                            (
                                ((z * self.nx + x) * self.ny + y) * CORES + c,
                                ((to_z * self.nx + to_x) * self.ny + to_y) * CORES + to_c,
                            )
                        )
        return lax.ppermute(value, ("seq", "req"), pairs)

    def transpose(self, value, k):
        n = self.nx
        pairs = []
        for z in range(self.nz):
            for x in range(n):
                for y in range(n):
                    pairs.append(
                        (
                            ((z * n + x) * n + y) * CORES + 1,
                            ((z * n + y) * n + (x - k) % n) * CORES + 1,
                        )
                    )
        return lax.ppermute(value, ("seq", "req"), pairs)

    def hand(self, value, source):
        chips = self.nz * self.nx * self.ny
        pairs = [(i * CORES + source, i * CORES + 1 - source) for i in range(chips)]
        return lax.ppermute(value, ("seq", "req"), pairs)

    def gather_z(self, value):
        return [value] + [self.move(value, dz=dz) for dz in range(1, self.nz)]


def layer_norm(values, gain, shift):
    center = values - jnp.mean(values, axis=-1, keepdims=True)
    spread = jnp.mean(center * center, axis=-1, keepdims=True)
    return center * lax.rsqrt(spread + 1e-05) * gain + shift


def dot(a, b):
    return jnp.dot(a, b, preferred_element_type=F32)


def across(a, b):
    return lax.dot_general(a, b, (((1,), (1,)), ((), ())), preferred_element_type=F32)


def at(index, size):
    return pl.ds(pl.multiple_of(index * size, size), size)


def call(kernel, name, ins, outs, in_specs=None, out_specs=None, scratch=(), moved=2**20, limit=20, aliases=None):
    single = not isinstance(outs, (list, tuple))
    specs = out_specs or (VMEM if single else [VMEM] * len(outs))
    return pl.pallas_call(
        kernel,
        name=name,
        out_shape=outs,
        in_specs=in_specs or [VMEM] * len(ins),
        out_specs=specs,
        scratch_shapes=list(scratch),
        input_output_aliases=aliases or {},
        cost_estimate=pl.CostEstimate(flops=0, bytes_accessed=moved, transcendentals=0),
        compiler_params=pltpu.CompilerParams(vmem_limit_bytes=int(limit * 1024 * 1024)),
    )(*ins)


def side_by_side(blocks, start, size):
    return jnp.concatenate(
        [blocks[x, :, start : start + size].astype(F32) for x in range(blocks.shape[0])], axis=1
    )


def two_halves(rows_by_k, own, sibling):
    depth = own.shape[0]
    req = lax.axis_index("req")
    other = req + 1 - 2 * lax.rem(req, CORES)
    return dot(rows_by_k[:, at(req, depth)], own[...]) + dot(
        rows_by_k[:, at(other, depth)], sibling[...]
    )


def flatten(block, flat, start):
    group, steps, _ = block.shape
    for i in range(group):
        flat[start + i * steps : start + (i + 1) * steps, :] = block[i].astype(F32)


def norm_kernel(tokens, scales, *refs):
    count = (len(refs) - 3) // 2
    weights, out, kept = refs[:count], refs[count], refs[count + 1 : 2 * count + 1]
    flat, sems = refs[-2:]
    copies = [
        pltpu.make_async_copy(source, target, sems.at[k])
        for k, (source, target) in enumerate(zip(weights, kept))
    ]
    for copy in copies:
        copy.start()
    width = out.shape[1]
    flatten(tokens, flat, 0)
    out[...] = layer_norm(flat[...], scales[:, :width], scales[:, width:]).astype(BF16)
    for copy in copies:
        copy.wait()


def qkv_kernel(place, *refs):
    ny = place.ny
    mine = refs[0]
    toks = refs[1:ny]
    scales, biases = refs[ny : ny + 2]
    weights = refs[ny + 2 : ny + 8]
    outs = refs[ny + 8 : 2 * ny + 8]
    flat, normed = refs[2 * ny + 8 :]
    rows, width = mine.shape
    normed[:rows, :] = mine[...]
    for j, tok in enumerate(toks):
        flatten(tok, flat, j * rows)
    normed[rows:, :] = layer_norm(flat[...], scales[:, :width], scales[:, width:]).astype(BF16)
    cols = weights[0].shape[1]
    for k in range(3):
        acc = two_halves(normed, weights[k], weights[3 + k])
        for j in range(ny):
            part = acc[j * rows : (j + 1) * rows]
            if j == 0:
                part = part + biases[:, k * cols : (k + 1) * cols]
            outs[(ny - j) % ny][:, k * cols : (k + 1) * cols] = part.astype(BF16)


def add_columns_kernel(place, *refs):
    out = refs[-1]
    for dx in range(place.nx):
        total = refs[dx * place.ny][...].astype(F32)
        for dy in range(1, place.ny):
            total = total + refs[dx * place.ny + dy][...].astype(F32)
        out[place.x_before(dx)] = total.astype(BF16)


def cache_kernel(keys_in, values_in, keys_out, values_out, keys, values, in_sems, out_sems):
    group = keys.shape[0]
    arrays = ((keys_in, keys, keys_out), (values_in, values, values_out))
    coming = [
        pltpu.make_async_copy(source.at[i], here.at[i], in_sems.at[k, i])
        for i in range(group)
        for k, (source, here, _) in enumerate(arrays)
    ]
    going = [
        pltpu.make_async_copy(here.at[i], target.at[i], out_sems.at[k, i])
        for i in range(group)
        for k, (_, here, target) in enumerate(arrays)
    ]
    for copy in coming:
        copy.start()
    for arrived, copy in zip(coming, going):
        arrived.wait()
        copy.start()
    for copy in going:
        copy.wait()


def split_three(value):
    first = value.astype(BF16).astype(F32)
    rest = value - first
    second = rest.astype(BF16).astype(F32)
    return first, second, rest - second


def turn(value, by):
    return pltpu.roll(value, by % LANES, 1)


def pairs_of(query):
    side = lax.rem(lax.div(lax.broadcasted_iota(jnp.int32, query.shape, 1), HEAD), 2)
    return jnp.concatenate(
        [jnp.where(side == 0, query, 0.0), jnp.where(side == 1, query, 0.0)], axis=0
    ).astype(BF16)


def attention_kernel(place, heads, steps, *refs):
    nx, nz = place.nx, place.nz
    gathered = refs[:nz]
    lengths, keys, values = refs[nz : nz + 3]
    keys_out, values_out = refs[nz + 5 : nz + 7]
    messages = refs[nz + 7 : nz + 7 + nx]
    qs, ks, vs, scores, part, stats, k_rows, v_rows, sems = refs[nz + 7 + nx :]
    group, slots, width = keys.shape
    cols = width // place.seqs
    seq = lax.axis_index("seq")
    for dz in range(nz):
        span = at(place.z_partner(dz), nx * cols)
        for k, target in enumerate((qs, ks, vs)):
            target[:, span] = side_by_side(gathered[dz], k * cols, cols)

    window = k_rows.shape[1]

    def place_of(i):
        base = lengths[i] - seq * slots
        start = jnp.clip(lax.div(jnp.maximum(base, 0), 16) * 16, 0, slots - window)
        return base, pl.multiple_of(start, 16)

    def copies(i):
        _, start = place_of(i)
        return [
            pltpu.make_async_copy(
                rows.at[i], target.at[i, pl.ds(start, window), :], sems.at[k, i]
            )
            for k, (rows, target) in enumerate(((k_rows, keys_out), (v_rows, values_out)))
        ]

    for i in range(group):
        base, start = place_of(i)

        @pl.when((base > -steps) & (base < slots))
        def _():
            slot = start + lax.broadcasted_iota(jnp.int32, (window, width), 0)
            for source, fresh, rows in ((keys, ks, k_rows), (values, vs, v_rows)):
                block = source[i, pl.ds(start, window), :].astype(F32)
                for t in range(steps):
                    at_row = fresh[i * steps + t : i * steps + t + 1, :]
                    block = jnp.where(slot == base + t, at_row, block)
                rows[i] = block.astype(BF16)
            for copy in copies(i):
                copy.start()

    pack = max(1, min(group, 256 // slots))
    rows = pack * steps
    tile = 2 * HEAD
    left = lax.broadcasted_iota(jnp.int32, (rows, tile), 1) < HEAD
    many, cached = heads * rows, pack * slots
    row = lax.broadcasted_iota(jnp.int32, (many, cached + LANES), 0)
    column = lax.broadcasted_iota(jnp.int32, (many, cached + LANES), 1)
    owner = lax.div(lax.rem(row, rows), steps)
    position = lax.rem(column, slots)
    old = (column < cached) & (owner == lax.div(column, slots))
    new = column - cached
    later = lax.rem(new, steps)
    fresh = (
        (new >= 0)
        & (new < rows)
        & (lax.div(new, steps) == owner)
        & (later <= lax.rem(row, steps))
    )
    lane = lax.broadcasted_iota(jnp.int32, (rows, LANES), 1)
    blank = jnp.zeros((LANES - rows, width), BF16)
    for g in range(group // pack):
        mine = slice(g * rows, (g + 1) * rows)
        these = slice(g * pack, (g + 1) * pack)
        pair = pairs_of(qs[mine, :])
        key = keys[these].reshape(cached, width)
        value = values[these].reshape(cached, width)
        new_key = jnp.concatenate([ks[mine, :].astype(BF16), blank], axis=0)
        new_value = jnp.concatenate([vs[mine, :].astype(BF16), blank], axis=0)
        for j in range(heads // 2):
            span = slice(j * tile, (j + 1) * tile)
            these_rows = slice(j * 2 * rows, (j + 1) * 2 * rows)
            scores[these_rows, :cached] = across(pair[:, span], key[:, span])
            scores[these_rows, cached:] = across(pair[:, span], new_key[:, span])
        base = jnp.zeros_like(owner)
        for k in range(pack):
            base = jnp.where(owner == k, lengths[g * pack + k] - seq * slots, base)
        at_new = base + later
        valid = (old & (position < base)) | (fresh & (at_new >= 0) & (at_new < slots))
        masked = jnp.where(valid, scores[...] * HEAD ** (-0.5), -1e30)
        peak = jnp.max(masked, axis=-1, keepdims=True)
        expo = jnp.where(valid, jnp.exp(masked - peak), 0.0)
        total = jnp.sum(expo, axis=-1, keepdims=True)
        probs = expo.astype(BF16)
        for j in range(heads // 2):
            span = slice(j * tile, (j + 1) * tile)
            these_rows = slice(j * 2 * rows, (j + 1) * 2 * rows)
            mixed = dot(probs[these_rows, :cached], value[:, span])
            mixed = mixed + dot(probs[these_rows, cached:], new_value[:, span])
            part[mine, span] = jnp.where(left, mixed[:rows], mixed[rows:])
        line = jnp.zeros((rows, LANES), F32)
        for k, piece in enumerate(split_three(peak) + split_three(total)[:2]):
            for h in range(heads):
                line = jnp.where(lane == k * heads + h, piece[h * rows : (h + 1) * rows], line)
        stats[mine, :] = line
    share = width // nx
    for dx in range(nx):
        to = place.x_after(dx)
        messages[dx][:, :share] = part[:, at(to, share)].astype(BF16)
        messages[dx][:, share:] = pltpu.roll(
            stats[...], lax.rem(LANES - to * (heads // nx), LANES), 1
        ).astype(BF16)
    for i in range(group):
        base, _ = place_of(i)

        @pl.when((base > -steps) & (base < slots))
        def _():
            for copy in copies(i):
                copy.wait()


def expand(factor, count):
    rows = factor.shape[0]
    return jnp.concatenate(
        [jnp.broadcast_to(factor[:, h : h + 1], (rows, HEAD)) for h in range(count)], axis=1
    )


def merge(messages, heads, share):
    peaks, totals = [], []
    for message in messages:
        stats = message[:, share:].astype(F32)
        peaks.append(stats + turn(stats, -heads) + turn(stats, -2 * heads))
        totals.append(turn(stats, -3 * heads) + turn(stats, -4 * heads))
    peak = functools.reduce(jnp.maximum, peaks)
    scales = [jnp.exp(p - peak) for p in peaks]
    total = sum(t * s for t, s in zip(totals, scales))
    return peak, total, scales


def merge_x_kernel(place, heads, *refs):
    share = refs[0].shape[1] - LANES
    count = share // HEAD
    out = refs[-1]
    messages = [r[...] for r in refs[:-1]]
    peak, total, scales = merge(messages, heads, share)
    out[:, :share] = sum(
        m[:, :share].astype(F32) * expand(s, count) for m, s in zip(messages, scales)
    ).astype(BF16)
    lane = lax.broadcasted_iota(jnp.int32, peak.shape, 1)
    tile = jnp.zeros_like(peak)
    for k, piece in enumerate(split_three(peak) + split_three(total)[:2]):
        tile = tile + turn(jnp.where(lane < count, piece, 0.0), k * heads)
    out[:, share:] = tile.astype(BF16)


def merge_z_kernel(place, heads, *refs):
    share = refs[0].shape[1] - LANES
    count = share // HEAD
    out = refs[-1]
    messages = [r[...] for r in refs[:-1]]
    _, total, scales = merge(messages, heads, share)
    out[...] = sum(
        m[:, :share].astype(F32) * expand(s / total, count) for m, s in zip(messages, scales)
    ).astype(BF16)


def pack_kernel(own, sibling, out, sems):
    copies = [
        pltpu.make_async_copy(sibling, out.at[0], sems.at[0]),
        pltpu.make_async_copy(own, out.at[1], sems.at[1]),
    ]
    for copy in copies:
        copy.start()
    for copy in copies:
        copy.wait()


def out_kernel(place, attn, *refs):
    nx = place.nx
    weights = refs[: 2 * nx]
    bias, out, total = refs[2 * nx :]
    depth = weights[0].shape[1]

    def multiply(mine):
        for k in range(nx):
            block = lax.rem(place.y() + k, nx)
            weight = weights[2 * k + mine]
            total[block] = dot(attn[:, :depth], weight[0]) + dot(attn[:, depth:], weight[1])

    @pl.when(place.core() == 1)
    def _():
        multiply(0)

    @pl.when(place.core() == 0)
    def _():
        multiply(1)

    total[place.x()] = total[place.x()] + bias[...]
    out[...] = total[...].astype(BF16)


def add_out_kernel(place, *refs):
    out = refs[-1]
    for dy in range(place.ny):
        total = refs[dy][...].astype(F32)
        for dx in range(1, place.nx):
            total = total + refs[dx * place.ny + dy][...].astype(F32)
        out[place.y_before(dy)] = total.astype(BF16)


def up_kernel(place, *refs):
    ny, nz = place.ny, place.nz
    toks = refs[:ny]
    gathered = refs[ny : ny + nz]
    gain, shift, own, sibling, bias, out, mid_out, proj, normed, flat = refs[ny + nz :]
    group, steps, _ = toks[0].shape
    rows = group * steps
    cols = gathered[0].shape[3]
    for dz in range(nz):
        span = at(place.z_partner(dz), place.nx * cols)
        for y in range(ny):
            proj[y * rows : (y + 1) * rows, span] = side_by_side(gathered[dz].at[y], 0, cols)
    for j in range(ny):
        here = at(place.y_before(j), rows)
        flatten(toks[j], flat, 0)
        mid = flat[...] + proj[here, :]
        if j == 0:
            mid_out[...] = mid
        normed[here, :] = layer_norm(mid, gain[...], shift[...]).astype(BF16)
    first = (place.y() == 0).astype(F32)
    out[...] = (two_halves(normed, own, sibling) + bias[...] * first).astype(BF16)


def down_kernel(place, *refs):
    nx, ny = place.nx, place.ny
    parts = refs[:ny]
    own, sibling = refs[ny : ny + 2]
    outs = refs[ny + 2 : ny + 2 + nx]
    feed = refs[-1]
    total = sum(p[...].astype(F32) for p in parts)
    hidden = (0.5 * total * (1.0 + lax.erf(total * 0.5**0.5))).astype(BF16)
    ncols = own.shape[1]
    feed[:, at(place.core(), ncols)] = dot(hidden, own[...])
    feed[:, at(1 - place.core(), ncols)] = dot(hidden, sibling[...])
    width = outs[0].shape[1]
    for dx in range(nx):
        outs[dx][...] = feed[:, at(place.x_after(dx), width)].astype(BF16)


def add_x_kernel(place, *refs):
    refs[-1][...] = sum(r[...].astype(F32) for r in refs[:-1]).astype(BF16)


def add_z_kernel(place, *refs):
    outs, total = refs[place.nz : -1], refs[-1]
    total[...] = sum(r[...].astype(F32) for r in refs[: place.nz])
    rows = outs[0].shape[0]
    for dy in range(place.ny):
        outs[dy][...] = total[at(lax.rem(place.y() + dy, place.ny), rows), :].astype(BF16)


def last_kernel(place, *refs):
    nx, ny = place.nx, place.ny
    parts = refs[: nx * ny]
    mid, bias, out, full = refs[nx * ny :]
    group, steps, _ = out.shape
    width = parts[0].shape[1]
    for dx in range(nx):
        for dy in range(ny):
            block = place.y_before(dy) * nx + place.x_before(dx)
            full[:, at(block, width)] = parts[dx * ny + dy][...].astype(F32)
    result = mid[...] + full[...] + bias[...]
    for i in range(group):
        out[i] = result[i * steps : (i + 1) * steps].astype(BF16)


def shape(sizes, kind=BF16):
    return jax.ShapeDtypeStruct(tuple(sizes), kind)


def body(
    tokens,
    lengths,
    cache_keys,
    cache_values,
    norm1_gain,
    norm1_bias,
    w_query,
    b_query,
    w_key,
    b_key,
    w_value,
    b_value,
    w_out,
    b_out,
    norm2_gain,
    norm2_bias,
    w_up,
    b_up,
    w_down,
    b_down,
):
    place = Place(lax.axis_size("seq"), lax.axis_size("req"))
    nx, ny = place.nx, place.ny
    group, steps, width = tokens.shape
    slots = cache_keys.shape[1]
    rows = group * steps
    heads = width // HEAD
    share = width // nx
    bind = functools.partial

    def row(vector):
        return vector.reshape(1, -1)

    def spread(by_dy):
        return [
            by_dy[dy] if dx == 0 and dy == 0 else place.move(by_dy[dy], dx, dy)
            for dx in range(nx)
            for dy in range(ny)
        ]

    toks = [tokens] + [place.move(tokens, dy=dy) for dy in range(1, ny)]
    cols = w_query.shape[1]
    own = [w_query, w_key, w_value]
    siblings = [place.move(weight, dc=1) for weight in own]
    scales = row(jnp.concatenate([norm1_gain, norm1_bias]))
    biases = row(jnp.concatenate([b_query, b_key, b_value]))
    normed, *own = call(
        norm_kernel,
        "norm",
        [tokens, scales, *own],
        [shape((rows, width))] + [shape(w.shape) for w in own],
        in_specs=[VMEM] * 2 + [HBM] * 3,
        scratch=[pltpu.VMEM((rows, width), F32), pltpu.SemaphoreType.DMA((3,))],
        limit=52.75,
    )
    parts = call(
        bind(qkv_kernel, place),
        "norm_qkv",
        [normed, *toks[1:], scales, biases, *own, *siblings],
        [shape((rows, 3 * cols))] * ny,
        scratch=[pltpu.VMEM(((ny - 1) * rows, width), F32), pltpu.VMEM((ny * rows, width), BF16)],
    )
    out_sibling = place.hand(w_out, 0)
    *parts, tied_up, tied_down, out_sibling = lax.optimization_barrier(
        (*parts, w_up, w_down, out_sibling)
    )
    packed = call(
        pack_kernel,
        "pack",
        [w_out, out_sibling],
        shape((CORES, *w_out.shape)),
        in_specs=[HBM, VMEM],
        scratch=[pltpu.SemaphoreType.DMA((2,))],
        moved=4 * 1024 * 1024,
    )
    w_up_sibling = place.move(tied_up, dc=1)
    w_down_sibling = place.move(tied_down, dc=1)
    qkv = call(
        bind(add_columns_kernel, place),
        "add_qkv",
        spread(parts),
        shape((nx, rows, 3 * cols)),
    )
    qkv, w_up_sibling, w_down_sibling, packed = lax.optimization_barrier(
        (qkv, w_up_sibling, w_down_sibling, packed)
    )
    qkv, tied_keys, tied_values = lax.optimization_barrier((qkv, cache_keys, cache_values))
    new_keys, new_values, keys, values = call(
        cache_kernel,
        "caches",
        [tied_keys, tied_values],
        [shape(cache_keys.shape)] * 4,
        in_specs=[HBM, HBM],
        out_specs=[HBM, HBM, VMEM, VMEM],
        scratch=[pltpu.SemaphoreType.DMA((2, group)), pltpu.SemaphoreType.DMA((2, group))],
        moved=16 * 1024 * 1024,
        limit=46,
    )
    pieces = place.gather_z(qkv)
    blocks = [place.transpose(packed, k) for k in range(nx)]
    pack = max(1, min(group, 256 // slots))
    window = min(32, slots)
    new_keys, new_values, *messages = call(
        bind(attention_kernel, place, heads, steps),
        "attention",
        [*pieces, lengths, keys, values, new_keys, new_values],
        [shape(cache_keys.shape)] * 2 + [shape((rows, share + LANES))] * nx,
        in_specs=[VMEM] * place.nz + [SMEM, VMEM, VMEM, HBM, HBM],
        out_specs=[HBM, HBM] + [VMEM] * nx,
        scratch=[
            pltpu.VMEM((rows, width), F32),
            pltpu.VMEM((rows, width), F32),
            pltpu.VMEM((rows, width), F32),
            pltpu.VMEM((heads * pack * steps, pack * slots + LANES), F32),
            pltpu.VMEM((rows, width), F32),
            pltpu.VMEM((rows, LANES), F32),
            pltpu.VMEM((group, window, width), BF16),
            pltpu.VMEM((group, window, width), BF16),
            pltpu.SemaphoreType.DMA((2, group)),
        ],
        aliases={place.nz + 3: 0, place.nz + 4: 1},
    )
    messages, blocks = lax.optimization_barrier((messages, blocks))
    w_outs = []
    for block in blocks:
        w_outs += [block, place.hand(block, 1)]
    messages = [messages[0]] + [place.move(messages[dx], dx=dx) for dx in range(1, nx)]
    merged = call(
        bind(merge_x_kernel, place, heads), "merge_x", messages, shape((rows, share + LANES))
    )
    pieces = place.gather_z(merged)
    attn = call(bind(merge_z_kernel, place, heads), "merge_z", pieces, shape((rows, share)))
    out_part = call(
        bind(out_kernel, place),
        "out",
        [attn, *w_outs, row(b_out)],
        shape((nx, rows, cols)),
        scratch=[pltpu.VMEM((nx, rows, cols), F32)],
    )
    projected = call(
        bind(add_out_kernel, place),
        "add_out",
        spread([out_part] * ny),
        shape((ny, nx, rows, cols)),
    )
    up_part, mid = call(
        bind(up_kernel, place),
        "norm_up",
        [
            *toks,
            *place.gather_z(projected),
            row(norm2_gain),
            row(norm2_bias),
            w_up,
            w_up_sibling,
            row(b_up),
        ],
        [shape((ny * rows, w_up.shape[1])), shape((rows, width), F32)],
        scratch=[
            pltpu.VMEM((ny * rows, width), F32),
            pltpu.VMEM((ny * rows, width), BF16),
            pltpu.VMEM((rows, width), F32),
        ],
    )
    up_parts = [up_part] + [place.move(up_part, dy=dy) for dy in range(1, ny)]
    piece = CORES * w_down.shape[1] // nx
    feeds = call(
        bind(down_kernel, place),
        "gelu_down",
        [*up_parts, w_down, w_down_sibling],
        [shape((ny * rows, piece))] * nx,
        scratch=[pltpu.VMEM((ny * rows, CORES * w_down.shape[1]), F32)],
    )
    feeds = [feeds[0]] + [place.move(feeds[dx], dx=dx) for dx in range(1, nx)]
    feed = call(bind(add_x_kernel, place), "add_x", feeds, shape((ny * rows, piece)))
    summed = call(
        bind(add_z_kernel, place),
        "add_z",
        place.gather_z(feed),
        [shape((rows, piece))] * ny,
        scratch=[pltpu.VMEM((ny * rows, piece), F32)],
    )
    hidden_out = call(
        bind(last_kernel, place),
        "last",
        [*spread(summed), mid, row(b_down)],
        shape(tokens.shape),
        scratch=[pltpu.VMEM((rows, width), F32)],
    )
    return (hidden_out, new_keys, new_values)


def solution(mesh):
    in_specs = (
        P("req", None, None),
        P("req"),
        P("req", "seq", None),
        P("req", "seq", None),
        P(),
        P(),
        P("req", "seq"),
        P("seq"),
        P("req", "seq"),
        P("seq"),
        P("req", "seq"),
        P("seq"),
        P("req", "seq"),
        P("seq"),
        P(),
        P(),
        P("req", "seq"),
        P("seq"),
        P("seq", "req"),
        P(),
    )
    out_specs = (P("req", None, None), P("req", "seq", None), P("req", "seq", None))
    return jax.shard_map(body, mesh=mesh, in_specs=in_specs, out_specs=out_specs, check_vma=False)
```

```python
import functools

import jax
import jax.numpy as jnp
from jax import lax
from jax.experimental import pallas as pl
from jax.experimental.pallas import tpu as pltpu
from jax.sharding import PartitionSpec as P

HEAD = 128
LANES = 128
CORES = 2
BF16 = jnp.bfloat16
F32 = jnp.float32
VMEM = pl.BlockSpec(memory_space=pltpu.VMEM)
SMEM = pl.BlockSpec(memory_space=pltpu.SMEM)
HBM = pl.BlockSpec(memory_space=pltpu.HBM)


class Place:
    def __init__(self, seqs, reqs):
        self.ny = reqs // CORES
        self.nx = self.ny
        self.nz = seqs // self.nx
        self.seqs = seqs

    def x(self):
        return lax.rem(lax.axis_index("seq"), self.nx)

    def y(self):
        return lax.div(lax.axis_index("req"), CORES)

    def core(self):
        return lax.rem(lax.axis_index("req"), CORES)

    def x_before(self, dx):
        return lax.rem(self.x() + self.nx - dx, self.nx)

    def x_after(self, dx):
        return lax.rem(self.x() + dx, self.nx)

    def y_before(self, dy):
        return lax.rem(self.y() + self.ny - dy, self.ny)

    def z_partner(self, dz):
        return lax.bitwise_xor(lax.div(lax.axis_index("seq"), self.nx), dz)

    def move(self, value, dx=0, dy=0, dc=0, dz=0):
        pairs = []
        for z in range(self.nz):
            for x in range(self.nx):
                for y in range(self.ny):
                    for c in range(CORES):
                        to_x, to_y, to_c = (x + dx) % self.nx, (y + dy) % self.ny, (c + dc) % CORES
                        to_z = z ^ dz
                        pairs.append(
                            (
                                ((z * self.nx + x) * self.ny + y) * CORES + c,
                                ((to_z * self.nx + to_x) * self.ny + to_y) * CORES + to_c,
                            )
                        )
        return lax.ppermute(value, ("seq", "req"), pairs)

    def transpose(self, value, k):
        n = self.nx
        pairs = []
        for z in range(self.nz):
            for x in range(n):
                for y in range(n):
                    for c in range(CORES):
                        pairs.append(
                            (
                                ((z * n + x) * n + y) * CORES + c,
                                ((z * n + y) * n + (x - k) % n) * CORES + c,
                            )
                        )
        return lax.ppermute(value, ("seq", "req"), pairs)

    def gather_z(self, value):
        return [value] + [self.move(value, dz=dz) for dz in range(1, self.nz)]


def layer_norm(values, gain, shift):
    center = values - jnp.mean(values, axis=-1, keepdims=True)
    spread = jnp.mean(center * center, axis=-1, keepdims=True)
    return center * lax.rsqrt(spread + 1e-05) * gain + shift


def dot(a, b):
    return jnp.dot(a, b, preferred_element_type=F32)


def across(a, b):
    return lax.dot_general(a, b, (((1,), (1,)), ((), ())), preferred_element_type=F32)


def at(index, size):
    return pl.ds(pl.multiple_of(index * size, size), size)


def call(kernel, name, ins, outs, in_specs=None, out_specs=None, scratch=(), moved=2**20, limit=20, aliases=None):
    single = not isinstance(outs, (list, tuple))
    specs = out_specs or (VMEM if single else [VMEM] * len(outs))
    return pl.pallas_call(
        kernel,
        name=name,
        out_shape=outs,
        in_specs=in_specs or [VMEM] * len(ins),
        out_specs=specs,
        scratch_shapes=list(scratch),
        input_output_aliases=aliases or {},
        cost_estimate=pl.CostEstimate(flops=0, bytes_accessed=moved, transcendentals=0),
        compiler_params=pltpu.CompilerParams(vmem_limit_bytes=int(limit * 1024 * 1024)),
    )(*ins)


def side_by_side(blocks, start, size):
    return jnp.concatenate(
        [blocks[x, :, start : start + size].astype(F32) for x in range(blocks.shape[0])], axis=1
    )


def two_halves(rows_by_k, own, sibling):
    depth = own.shape[0]
    req = lax.axis_index("req")
    other = req + 1 - 2 * lax.rem(req, CORES)
    return dot(rows_by_k[:, at(req, depth)], own[...]) + dot(
        rows_by_k[:, at(other, depth)], sibling[...]
    )


def flatten(block, flat, start):
    group, steps, _ = block.shape
    for i in range(group):
        flat[start + i * steps : start + (i + 1) * steps, :] = block[i].astype(F32)


def norm_kernel(tokens, scales, *refs):
    count = (len(refs) - 3) // 2
    weights, out, kept = refs[:count], refs[count], refs[count + 1 : 2 * count + 1]
    flat, sems = refs[-2:]
    copies = [
        pltpu.make_async_copy(source, target, sems.at[k])
        for k, (source, target) in enumerate(zip(weights, kept))
    ]
    for copy in copies:
        copy.start()
    width = out.shape[1]
    flatten(tokens, flat, 0)
    out[...] = layer_norm(flat[...], scales[:, :width], scales[:, width:]).astype(BF16)
    for copy in copies:
        copy.wait()


def qkv_kernel(place, *refs):
    ny = place.ny
    mine = refs[0]
    toks = refs[1:ny]
    scales, biases = refs[ny : ny + 2]
    weights = refs[ny + 2 : ny + 8]
    outs = refs[ny + 8 : 2 * ny + 8]
    flat, normed = refs[2 * ny + 8 :]
    rows, width = mine.shape
    normed[:rows, :] = mine[...]
    for j, tok in enumerate(toks):
        flatten(tok, flat, j * rows)
    normed[rows:, :] = layer_norm(flat[...], scales[:, :width], scales[:, width:]).astype(BF16)
    cols = weights[0].shape[1]
    for k in range(3):
        acc = two_halves(normed, weights[k], weights[3 + k])
        for j in range(ny):
            part = acc[j * rows : (j + 1) * rows]
            if j == 0:
                part = part + biases[:, k * cols : (k + 1) * cols]
            outs[(ny - j) % ny][:, k * cols : (k + 1) * cols] = part.astype(BF16)


def add_columns_kernel(place, *refs):
    out = refs[-1]
    for dx in range(place.nx):
        total = refs[dx * place.ny][...].astype(F32)
        for dy in range(1, place.ny):
            total = total + refs[dx * place.ny + dy][...].astype(F32)
        out[place.x_before(dx)] = total.astype(BF16)


def cache_kernel(keys_in, values_in, keys_out, values_out, keys, values, mark, in_sems, out_sems):
    group = keys.shape[0]
    arrays = ((keys_in, keys, keys_out), (values_in, values, values_out))
    coming = [
        pltpu.make_async_copy(source.at[i], here.at[i], in_sems.at[k, i])
        for i in range(group)
        for k, (source, here, _) in enumerate(arrays)
    ]
    going = [
        pltpu.make_async_copy(here.at[i], target.at[i], out_sems.at[k, i])
        for i in range(group)
        for k, (_, here, target) in enumerate(arrays)
    ]
    for copy in coming:
        copy.start()
    mark[...] = jnp.zeros_like(mark)
    for arrived, copy in zip(coming, going):
        arrived.wait()
        copy.start()
    for copy in going:
        copy.wait()


def split_three(value):
    first = value.astype(BF16).astype(F32)
    rest = value - first
    second = rest.astype(BF16).astype(F32)
    return first, second, rest - second


def turn(value, by):
    return pltpu.roll(value, by % LANES, 1)


def pairs_of(query):
    side = lax.rem(lax.div(lax.broadcasted_iota(jnp.int32, query.shape, 1), HEAD), 2)
    return jnp.concatenate(
        [jnp.where(side == 0, query, 0.0), jnp.where(side == 1, query, 0.0)], axis=0
    ).astype(BF16)


def attention_kernel(place, heads, steps, *refs):
    nx, nz = place.nx, place.nz
    gathered = refs[:nz]
    lengths, keys, values = refs[nz : nz + 3]
    keys_out, values_out = refs[nz + 5 : nz + 7]
    messages = refs[nz + 7 : nz + 7 + nx]
    qs, ks, vs, scores, part, stats, k_rows, v_rows, sems = refs[nz + 7 + nx :]
    group, slots, width = keys.shape
    cols = width // place.seqs
    seq = lax.axis_index("seq")
    for dz in range(nz):
        span = at(place.z_partner(dz), nx * cols)
        for k, target in enumerate((qs, ks, vs)):
            target[:, span] = side_by_side(gathered[dz], k * cols, cols)

    window = k_rows.shape[1]

    def place_of(i):
        base = lengths[i] - seq * slots
        start = jnp.clip(lax.div(jnp.maximum(base, 0), 16) * 16, 0, slots - window)
        return base, pl.multiple_of(start, 16)

    def copies(i):
        _, start = place_of(i)
        return [
            pltpu.make_async_copy(
                rows.at[i], target.at[i, pl.ds(start, window), :], sems.at[k, i]
            )
            for k, (rows, target) in enumerate(((k_rows, keys_out), (v_rows, values_out)))
        ]

    for i in range(group):
        base, start = place_of(i)

        @pl.when((base > -steps) & (base < slots))
        def _():
            slot = start + lax.broadcasted_iota(jnp.int32, (window, width), 0)
            for source, fresh, rows in ((keys, ks, k_rows), (values, vs, v_rows)):
                block = source[i, pl.ds(start, window), :].astype(F32)
                for t in range(steps):
                    at_row = fresh[i * steps + t : i * steps + t + 1, :]
                    block = jnp.where(slot == base + t, at_row, block)
                rows[i] = block.astype(BF16)
            for copy in copies(i):
                copy.start()

    pack = max(1, min(group, 256 // slots))
    rows = pack * steps
    tile = 2 * HEAD
    left = lax.broadcasted_iota(jnp.int32, (rows, tile), 1) < HEAD
    many, cached = heads * rows, pack * slots
    row = lax.broadcasted_iota(jnp.int32, (many, cached + LANES), 0)
    column = lax.broadcasted_iota(jnp.int32, (many, cached + LANES), 1)
    owner = lax.div(lax.rem(row, rows), steps)
    position = lax.rem(column, slots)
    old = (column < cached) & (owner == lax.div(column, slots))
    new = column - cached
    later = lax.rem(new, steps)
    fresh = (
        (new >= 0)
        & (new < rows)
        & (lax.div(new, steps) == owner)
        & (later <= lax.rem(row, steps))
    )
    lane = lax.broadcasted_iota(jnp.int32, (rows, LANES), 1)
    blank = jnp.zeros((LANES - rows, width), BF16)
    for g in range(group // pack):
        mine = slice(g * rows, (g + 1) * rows)
        these = slice(g * pack, (g + 1) * pack)
        pair = pairs_of(qs[mine, :])
        key = keys[these].reshape(cached, width)
        value = values[these].reshape(cached, width)
        new_key = jnp.concatenate([ks[mine, :].astype(BF16), blank], axis=0)
        new_value = jnp.concatenate([vs[mine, :].astype(BF16), blank], axis=0)
        for j in range(heads // 2):
            span = slice(j * tile, (j + 1) * tile)
            these_rows = slice(j * 2 * rows, (j + 1) * 2 * rows)
            scores[these_rows, :cached] = across(pair[:, span], key[:, span])
            scores[these_rows, cached:] = across(pair[:, span], new_key[:, span])
        base = jnp.zeros_like(owner)
        for k in range(pack):
            base = jnp.where(owner == k, lengths[g * pack + k] - seq * slots, base)
        at_new = base + later
        valid = (old & (position < base)) | (fresh & (at_new >= 0) & (at_new < slots))
        masked = jnp.where(valid, scores[...] * HEAD ** (-0.5), -1e30)
        peak = jnp.max(masked, axis=-1, keepdims=True)
        expo = jnp.where(valid, jnp.exp(masked - peak), 0.0)
        total = jnp.sum(expo, axis=-1, keepdims=True)
        probs = expo.astype(BF16)
        for j in range(heads // 2):
            span = slice(j * tile, (j + 1) * tile)
            these_rows = slice(j * 2 * rows, (j + 1) * 2 * rows)
            mixed = dot(probs[these_rows, :cached], value[:, span])
            mixed = mixed + dot(probs[these_rows, cached:], new_value[:, span])
            part[mine, span] = jnp.where(left, mixed[:rows], mixed[rows:])
        line = jnp.zeros((rows, LANES), F32)
        for k, piece in enumerate(split_three(peak) + split_three(total)[:2]):
            for h in range(heads):
                line = jnp.where(lane == k * heads + h, piece[h * rows : (h + 1) * rows], line)
        stats[mine, :] = line
    share = width // nx
    for dx in range(nx):
        to = place.x_after(dx)
        messages[dx][:, :share] = part[:, at(to, share)].astype(BF16)
        messages[dx][:, share:] = pltpu.roll(
            stats[...], lax.rem(LANES - to * (heads // nx), LANES), 1
        ).astype(BF16)
    for i in range(group):
        base, _ = place_of(i)

        @pl.when((base > -steps) & (base < slots))
        def _():
            for copy in copies(i):
                copy.wait()


def expand(factor, count):
    rows = factor.shape[0]
    return jnp.concatenate(
        [jnp.broadcast_to(factor[:, h : h + 1], (rows, HEAD)) for h in range(count)], axis=1
    )


def merge(messages, heads, share):
    peaks, totals = [], []
    for message in messages:
        stats = message[:, share:].astype(F32)
        peaks.append(stats + turn(stats, -heads) + turn(stats, -2 * heads))
        totals.append(turn(stats, -3 * heads) + turn(stats, -4 * heads))
    peak = functools.reduce(jnp.maximum, peaks)
    scales = [jnp.exp(p - peak) for p in peaks]
    total = sum(t * s for t, s in zip(totals, scales))
    return peak, total, scales


def merge_x_kernel(place, heads, *refs):
    share = refs[0].shape[1] - LANES
    count = share // HEAD
    out = refs[-1]
    messages = [r[...] for r in refs[:-1]]
    peak, total, scales = merge(messages, heads, share)
    out[:, :share] = sum(
        m[:, :share].astype(F32) * expand(s, count) for m, s in zip(messages, scales)
    ).astype(BF16)
    lane = lax.broadcasted_iota(jnp.int32, peak.shape, 1)
    tile = jnp.zeros_like(peak)
    for k, piece in enumerate(split_three(peak) + split_three(total)[:2]):
        tile = tile + turn(jnp.where(lane < count, piece, 0.0), k * heads)
    out[:, share:] = tile.astype(BF16)


def merge_z_kernel(place, heads, *refs):
    share = refs[0].shape[1] - LANES
    count = share // HEAD
    out = refs[-1]
    messages = [r[...] for r in refs[:-1]]
    _, total, scales = merge(messages, heads, share)
    out[...] = sum(
        m[:, :share].astype(F32) * expand(s / total, count) for m, s in zip(messages, scales)
    ).astype(BF16)


def out_kernel(place, attn, *refs):
    nx = place.nx
    weights = refs[: 2 * nx]
    bias, out, total = refs[2 * nx :]
    depth = weights[0].shape[0]
    core = place.core()
    for k in range(nx):
        block = lax.rem(place.y() + k, nx)
        total[block] = dot(attn[:, at(core, depth)], weights[2 * k][...]) + dot(
            attn[:, at(1 - core, depth)], weights[2 * k + 1][...]
        )
    total[place.x()] = total[place.x()] + bias[...]
    out[...] = total[...].astype(BF16)


def add_out_kernel(place, *refs):
    out = refs[-1]
    for dy in range(place.ny):
        total = refs[dy][...].astype(F32)
        for dx in range(1, place.nx):
            total = total + refs[dx * place.ny + dy][...].astype(F32)
        out[place.y_before(dy)] = total.astype(BF16)


def up_kernel(place, *refs):
    ny, nz = place.ny, place.nz
    toks = refs[:ny]
    gathered = refs[ny : ny + nz]
    gain, shift, own, sibling, bias, out, mid_out, proj, normed, flat = refs[ny + nz :]
    group, steps, _ = toks[0].shape
    rows = group * steps
    cols = gathered[0].shape[3]
    for dz in range(nz):
        span = at(place.z_partner(dz), place.nx * cols)
        for y in range(ny):
            proj[y * rows : (y + 1) * rows, span] = side_by_side(gathered[dz].at[y], 0, cols)
    for j in range(ny):
        here = at(place.y_before(j), rows)
        flatten(toks[j], flat, 0)
        mid = flat[...] + proj[here, :]
        if j == 0:
            mid_out[...] = mid
        normed[here, :] = layer_norm(mid, gain[...], shift[...]).astype(BF16)
    first = (place.y() == 0).astype(F32)
    out[...] = (two_halves(normed, own, sibling) + bias[...] * first).astype(BF16)


def down_kernel(place, *refs):
    nx, ny = place.nx, place.ny
    parts = refs[:ny]
    own, sibling = refs[ny : ny + 2]
    outs = refs[ny + 2 : ny + 2 + nx]
    feed = refs[-1]
    total = sum(p[...].astype(F32) for p in parts)
    hidden = (0.5 * total * (1.0 + lax.erf(total * 0.5**0.5))).astype(BF16)
    ncols = own.shape[1]
    feed[:, at(place.core(), ncols)] = dot(hidden, own[...])
    feed[:, at(1 - place.core(), ncols)] = dot(hidden, sibling[...])
    width = outs[0].shape[1]
    for dx in range(nx):
        outs[dx][...] = feed[:, at(place.x_after(dx), width)].astype(BF16)


def add_x_kernel(place, *refs):
    refs[-1][...] = sum(r[...].astype(F32) for r in refs[:-1]).astype(BF16)


def add_z_kernel(place, *refs):
    outs, total = refs[place.nz : -1], refs[-1]
    total[...] = sum(r[...].astype(F32) for r in refs[: place.nz])
    rows = outs[0].shape[0]
    for dy in range(place.ny):
        outs[dy][...] = total[at(lax.rem(place.y() + dy, place.ny), rows), :].astype(BF16)


def last_kernel(place, *refs):
    nx, ny = place.nx, place.ny
    parts = refs[: nx * ny]
    mid, bias, out, full = refs[nx * ny :]
    group, steps, _ = out.shape
    width = parts[0].shape[1]
    for dx in range(nx):
        for dy in range(ny):
            block = place.y_before(dy) * nx + place.x_before(dx)
            full[:, at(block, width)] = parts[dx * ny + dy][...].astype(F32)
    result = mid[...] + full[...] + bias[...]
    for i in range(group):
        out[i] = result[i * steps : (i + 1) * steps].astype(BF16)


def shape(sizes, kind=BF16):
    return jax.ShapeDtypeStruct(tuple(sizes), kind)


def body(
    tokens,
    lengths,
    cache_keys,
    cache_values,
    norm1_gain,
    norm1_bias,
    w_query,
    b_query,
    w_key,
    b_key,
    w_value,
    b_value,
    w_out,
    b_out,
    norm2_gain,
    norm2_bias,
    w_up,
    b_up,
    w_down,
    b_down,
):
    place = Place(lax.axis_size("seq"), lax.axis_size("req"))
    nx, ny = place.nx, place.ny
    group, steps, width = tokens.shape
    slots = cache_keys.shape[1]
    rows = group * steps
    heads = width // HEAD
    share = width // nx
    bind = functools.partial

    def row(vector):
        return vector.reshape(1, -1)

    def spread(by_dy):
        return [
            by_dy[dy] if dx == 0 and dy == 0 else place.move(by_dy[dy], dx, dy)
            for dx in range(nx)
            for dy in range(ny)
        ]

    toks = [tokens] + [place.move(tokens, dy=dy) for dy in range(1, ny)]
    cols = w_query.shape[1]
    own = [w_query, w_key, w_value]
    siblings = [place.move(weight, dc=1) for weight in own]
    scales = row(jnp.concatenate([norm1_gain, norm1_bias]))
    biases = row(jnp.concatenate([b_query, b_key, b_value]))
    normed, *own = call(
        norm_kernel,
        "norm",
        [tokens, scales, *own],
        [shape((rows, width))] + [shape(w.shape) for w in own],
        in_specs=[VMEM] * 2 + [HBM] * 3,
        scratch=[pltpu.VMEM((rows, width), F32), pltpu.SemaphoreType.DMA((3,))],
        limit=52.75,
    )
    parts = call(
        bind(qkv_kernel, place),
        "norm_qkv",
        [normed, *toks[1:], scales, biases, *own, *siblings],
        [shape((rows, 3 * cols))] * ny,
        scratch=[pltpu.VMEM(((ny - 1) * rows, width), F32), pltpu.VMEM((ny * rows, width), BF16)],
    )
    *parts, tied_up, tied_down = lax.optimization_barrier((*parts, w_up, w_down))
    w_up_sibling = place.move(tied_up, dc=1)
    w_down_sibling = place.move(tied_down, dc=1)
    parts, tied_keys, tied_values = lax.optimization_barrier((parts, cache_keys, cache_values))
    new_keys, new_values, keys, values, mark = call(
        cache_kernel,
        "caches",
        [tied_keys, tied_values],
        [shape(cache_keys.shape)] * 4 + [shape((8, LANES), F32)],
        in_specs=[HBM, HBM],
        out_specs=[HBM, HBM, VMEM, VMEM, VMEM],
        scratch=[pltpu.SemaphoreType.DMA((2, group)), pltpu.SemaphoreType.DMA((2, group))],
        moved=16 * 1024 * 1024,
        limit=46,
    )
    qkv = call(
        bind(add_columns_kernel, place),
        "add_qkv",
        [*spread(parts), mark],
        shape((nx, rows, 3 * cols)),
    )
    qkv, w_up_sibling, w_down_sibling, tied = lax.optimization_barrier(
        (qkv, w_up_sibling, w_down_sibling, w_out)
    )
    pieces = place.gather_z(qkv)
    blocks = [place.transpose(tied, k) for k in range(nx)]
    pieces, blocks = lax.optimization_barrier((pieces, blocks))
    w_outs = []
    for block in blocks:
        w_outs += [block, place.move(block, dc=1)]
    pack = max(1, min(group, 256 // slots))
    window = min(32, slots)
    new_keys, new_values, *messages = call(
        bind(attention_kernel, place, heads, steps),
        "attention",
        [*pieces, lengths, keys, values, new_keys, new_values],
        [shape(cache_keys.shape)] * 2 + [shape((rows, share + LANES))] * nx,
        in_specs=[VMEM] * place.nz + [SMEM, VMEM, VMEM, HBM, HBM],
        out_specs=[HBM, HBM] + [VMEM] * nx,
        scratch=[
            pltpu.VMEM((rows, width), F32),
            pltpu.VMEM((rows, width), F32),
            pltpu.VMEM((rows, width), F32),
            pltpu.VMEM((heads * pack * steps, pack * slots + LANES), F32),
            pltpu.VMEM((rows, width), F32),
            pltpu.VMEM((rows, LANES), F32),
            pltpu.VMEM((group, window, width), BF16),
            pltpu.VMEM((group, window, width), BF16),
            pltpu.SemaphoreType.DMA((2, group)),
        ],
        aliases={place.nz + 3: 0, place.nz + 4: 1},
        moved=16 * 1024 * 1024,
    )
    messages, w_outs = lax.optimization_barrier((messages, w_outs))
    messages = [messages[0]] + [place.move(messages[dx], dx=dx) for dx in range(1, nx)]
    merged = call(
        bind(merge_x_kernel, place, heads), "merge_x", messages, shape((rows, share + LANES))
    )
    pieces = place.gather_z(merged)
    attn = call(bind(merge_z_kernel, place, heads), "merge_z", pieces, shape((rows, share)))
    out_part = call(
        bind(out_kernel, place),
        "out",
        [attn, *w_outs, row(b_out)],
        shape((nx, rows, cols)),
        scratch=[pltpu.VMEM((nx, rows, cols), F32)],
    )
    projected = call(
        bind(add_out_kernel, place),
        "add_out",
        spread([out_part] * ny),
        shape((ny, nx, rows, cols)),
    )
    up_part, mid = call(
        bind(up_kernel, place),
        "norm_up",
        [
            *toks,
            *place.gather_z(projected),
            row(norm2_gain),
            row(norm2_bias),
            w_up,
            w_up_sibling,
            row(b_up),
        ],
        [shape((ny * rows, w_up.shape[1])), shape((rows, width), F32)],
        scratch=[
            pltpu.VMEM((ny * rows, width), F32),
            pltpu.VMEM((ny * rows, width), BF16),
            pltpu.VMEM((rows, width), F32),
        ],
    )
    up_parts = [up_part] + [place.move(up_part, dy=dy) for dy in range(1, ny)]
    piece = CORES * w_down.shape[1] // nx
    feeds = call(
        bind(down_kernel, place),
        "gelu_down",
        [*up_parts, w_down, w_down_sibling],
        [shape((ny * rows, piece))] * nx,
        scratch=[pltpu.VMEM((ny * rows, CORES * w_down.shape[1]), F32)],
    )
    feeds = [feeds[0]] + [place.move(feeds[dx], dx=dx) for dx in range(1, nx)]
    feed = call(bind(add_x_kernel, place), "add_x", feeds, shape((ny * rows, piece)))
    summed = call(
        bind(add_z_kernel, place),
        "add_z",
        place.gather_z(feed),
        [shape((rows, piece))] * ny,
        scratch=[pltpu.VMEM((ny * rows, piece), F32)],
    )
    hidden_out = call(
        bind(last_kernel, place),
        "last",
        [*spread(summed), mid, row(b_down)],
        shape(tokens.shape),
        scratch=[pltpu.VMEM((rows, width), F32)],
    )
    return (hidden_out, new_keys, new_values)


def solution(mesh):
    in_specs = (
        P("req", None, None),
        P("req"),
        P("req", "seq", None),
        P("req", "seq", None),
        P(),
        P(),
        P("req", "seq"),
        P("seq"),
        P("req", "seq"),
        P("seq"),
        P("req", "seq"),
        P("seq"),
        P("req", "seq"),
        P("seq"),
        P(),
        P(),
        P("req", "seq"),
        P("seq"),
        P("seq", "req"),
        P(),
    )
    out_specs = (P("req", None, None), P("req", "seq", None), P("req", "seq", None))
    return jax.shard_map(body, mesh=mesh, in_specs=in_specs, out_specs=out_specs, check_vma=False)
```

```python
import functools

import jax
import jax.numpy as jnp
from jax import lax
from jax.experimental import pallas as pl
from jax.experimental.pallas import tpu as pltpu
from jax.sharding import PartitionSpec as P

HEAD = 128
LANES = 128
CORES = 2
BF16 = jnp.bfloat16
F32 = jnp.float32
VMEM = pl.BlockSpec(memory_space=pltpu.VMEM)
SMEM = pl.BlockSpec(memory_space=pltpu.SMEM)
HBM = pl.BlockSpec(memory_space=pltpu.HBM)


class Place:
    def __init__(self, seqs, reqs):
        self.ny = reqs // CORES
        self.nx = self.ny
        self.nz = seqs // self.nx
        self.seqs = seqs

    def x(self):
        return lax.rem(lax.axis_index("seq"), self.nx)

    def y(self):
        return lax.div(lax.axis_index("req"), CORES)

    def core(self):
        return lax.rem(lax.axis_index("req"), CORES)

    def x_before(self, dx):
        return lax.rem(self.x() + self.nx - dx, self.nx)

    def x_after(self, dx):
        return lax.rem(self.x() + dx, self.nx)

    def y_before(self, dy):
        return lax.rem(self.y() + self.ny - dy, self.ny)

    def z_partner(self, dz):
        return lax.bitwise_xor(lax.div(lax.axis_index("seq"), self.nx), dz)

    def move(self, value, dx=0, dy=0, dc=0, dz=0):
        pairs = []
        for z in range(self.nz):
            for x in range(self.nx):
                for y in range(self.ny):
                    for c in range(CORES):
                        to_x, to_y, to_c = (x + dx) % self.nx, (y + dy) % self.ny, (c + dc) % CORES
                        to_z = z ^ dz
                        pairs.append(
                            (
                                ((z * self.nx + x) * self.ny + y) * CORES + c,
                                ((to_z * self.nx + to_x) * self.ny + to_y) * CORES + to_c,
                            )
                        )
        return lax.ppermute(value, ("seq", "req"), pairs)

    def transpose(self, value, k):
        n = self.nx
        pairs = []
        for z in range(self.nz):
            for x in range(n):
                for y in range(n):
                    for c in range(CORES):
                        pairs.append(
                            (
                                ((z * n + x) * n + y) * CORES + c,
                                ((z * n + y) * n + (x - k) % n) * CORES + c,
                            )
                        )
        return lax.ppermute(value, ("seq", "req"), pairs)

    def gather_z(self, value):
        return [value] + [self.move(value, dz=dz) for dz in range(1, self.nz)]


def layer_norm(values, gain, shift):
    center = values - jnp.mean(values, axis=-1, keepdims=True)
    spread = jnp.mean(center * center, axis=-1, keepdims=True)
    return center * lax.rsqrt(spread + 1e-05) * gain + shift


def dot(a, b):
    return jnp.dot(a, b, preferred_element_type=F32)


def across(a, b):
    return lax.dot_general(a, b, (((1,), (1,)), ((), ())), preferred_element_type=F32)


def at(index, size):
    return pl.ds(pl.multiple_of(index * size, size), size)


def call(kernel, name, ins, outs, in_specs=None, out_specs=None, scratch=(), moved=2**20, limit=20, aliases=None):
    single = not isinstance(outs, (list, tuple))
    specs = out_specs or (VMEM if single else [VMEM] * len(outs))
    return pl.pallas_call(
        kernel,
        name=name,
        out_shape=outs,
        in_specs=in_specs or [VMEM] * len(ins),
        out_specs=specs,
        scratch_shapes=list(scratch),
        input_output_aliases=aliases or {},
        cost_estimate=pl.CostEstimate(flops=0, bytes_accessed=moved, transcendentals=0),
        compiler_params=pltpu.CompilerParams(vmem_limit_bytes=int(limit * 1024 * 1024)),
    )(*ins)


def side_by_side(blocks, start, size):
    return jnp.concatenate(
        [blocks[x, :, start : start + size].astype(F32) for x in range(blocks.shape[0])], axis=1
    )


def two_halves(rows_by_k, own, sibling):
    depth = own.shape[0]
    req = lax.axis_index("req")
    other = req + 1 - 2 * lax.rem(req, CORES)
    return dot(rows_by_k[:, at(req, depth)], own[...]) + dot(
        rows_by_k[:, at(other, depth)], sibling[...]
    )


def flatten(block, flat, start):
    group, steps, _ = block.shape
    for i in range(group):
        flat[start + i * steps : start + (i + 1) * steps, :] = block[i].astype(F32)


def norm_kernel(tokens, scales, *refs):
    count = (len(refs) - 3) // 2
    weights, out, kept = refs[:count], refs[count], refs[count + 1 : 2 * count + 1]
    flat, sems = refs[-2:]
    copies = [
        pltpu.make_async_copy(source, target, sems.at[k])
        for k, (source, target) in enumerate(zip(weights, kept))
    ]
    for copy in copies:
        copy.start()
    width = out.shape[1]
    flatten(tokens, flat, 0)
    out[...] = layer_norm(flat[...], scales[:, :width], scales[:, width:]).astype(BF16)
    for copy in copies:
        copy.wait()


def qkv_kernel(place, *refs):
    ny = place.ny
    mine = refs[0]
    toks = refs[1:ny]
    scales, biases = refs[ny : ny + 2]
    weights = refs[ny + 2 : ny + 8]
    outs = refs[ny + 8 : 2 * ny + 8]
    flat, normed = refs[2 * ny + 8 :]
    rows, width = mine.shape
    normed[:rows, :] = mine[...]
    for j, tok in enumerate(toks):
        flatten(tok, flat, j * rows)
    normed[rows:, :] = layer_norm(flat[...], scales[:, :width], scales[:, width:]).astype(BF16)
    cols = weights[0].shape[1]
    for k in range(3):
        acc = two_halves(normed, weights[k], weights[3 + k])
        for j in range(ny):
            part = acc[j * rows : (j + 1) * rows]
            if j == 0:
                part = part + biases[:, k * cols : (k + 1) * cols]
            outs[(ny - j) % ny][:, k * cols : (k + 1) * cols] = part.astype(BF16)


def add_columns_kernel(place, *refs):
    out = refs[-1]
    for dx in range(place.nx):
        total = refs[dx * place.ny][...].astype(F32)
        for dy in range(1, place.ny):
            total = total + refs[dx * place.ny + dy][...].astype(F32)
        out[place.x_before(dx)] = total.astype(BF16)


def cache_kernel(keys_in, values_in, keys_out, values_out, keys, values, mark, in_sems, out_sems):
    group = keys.shape[0]
    arrays = ((keys_in, keys, keys_out), (values_in, values, values_out))
    coming = [
        pltpu.make_async_copy(source.at[i], here.at[i], in_sems.at[k, i])
        for i in range(group)
        for k, (source, here, _) in enumerate(arrays)
    ]
    going = [
        pltpu.make_async_copy(here.at[i], target.at[i], out_sems.at[k, i])
        for i in range(group)
        for k, (_, here, target) in enumerate(arrays)
    ]
    for copy in coming:
        copy.start()
    mark[...] = jnp.zeros_like(mark)
    for arrived, copy in zip(coming, going):
        arrived.wait()
        copy.start()
    for copy in going:
        copy.wait()


def split_three(value):
    first = value.astype(BF16).astype(F32)
    rest = value - first
    second = rest.astype(BF16).astype(F32)
    return first, second, rest - second


def turn(value, by):
    return pltpu.roll(value, by % LANES, 1)


def pairs_of(query):
    side = lax.rem(lax.div(lax.broadcasted_iota(jnp.int32, query.shape, 1), HEAD), 2)
    return jnp.concatenate(
        [jnp.where(side == 0, query, 0.0), jnp.where(side == 1, query, 0.0)], axis=0
    ).astype(BF16)


def attention_kernel(place, heads, steps, *refs):
    nx, nz = place.nx, place.nz
    gathered = refs[:nz]
    lengths, keys, values = refs[nz : nz + 3]
    keys_out, values_out = refs[nz + 5 : nz + 7]
    messages = refs[nz + 7 : nz + 7 + nx]
    qs, ks, vs, scores, part, stats, k_rows, v_rows, sems = refs[nz + 7 + nx :]
    group, slots, width = keys.shape
    cols = width // place.seqs
    seq = lax.axis_index("seq")
    for dz in range(nz):
        span = at(place.z_partner(dz), nx * cols)
        for k, target in enumerate((qs, ks, vs)):
            target[:, span] = side_by_side(gathered[dz], k * cols, cols)

    window = k_rows.shape[1]

    def place_of(i):
        base = lengths[i] - seq * slots
        start = jnp.clip(lax.div(jnp.maximum(base, 0), 16) * 16, 0, slots - window)
        return base, pl.multiple_of(start, 16)

    def copies(i):
        _, start = place_of(i)
        return [
            pltpu.make_async_copy(
                rows.at[i], target.at[i, pl.ds(start, window), :], sems.at[k, i]
            )
            for k, (rows, target) in enumerate(((k_rows, keys_out), (v_rows, values_out)))
        ]

    for i in range(group):
        base, start = place_of(i)

        @pl.when((base > -steps) & (base < slots))
        def _():
            slot = start + lax.broadcasted_iota(jnp.int32, (window, width), 0)
            for source, fresh, rows in ((keys, ks, k_rows), (values, vs, v_rows)):
                block = source[i, pl.ds(start, window), :].astype(F32)
                for t in range(steps):
                    at_row = fresh[i * steps + t : i * steps + t + 1, :]
                    block = jnp.where(slot == base + t, at_row, block)
                rows[i] = block.astype(BF16)
            for copy in copies(i):
                copy.start()

    pack = max(1, min(group, 256 // slots))
    rows = pack * steps
    tile = 2 * HEAD
    left = lax.broadcasted_iota(jnp.int32, (rows, tile), 1) < HEAD
    many, cached = heads * rows, pack * slots
    row = lax.broadcasted_iota(jnp.int32, (many, cached + LANES), 0)
    column = lax.broadcasted_iota(jnp.int32, (many, cached + LANES), 1)
    owner = lax.div(lax.rem(row, rows), steps)
    position = lax.rem(column, slots)
    old = (column < cached) & (owner == lax.div(column, slots))
    new = column - cached
    later = lax.rem(new, steps)
    fresh = (
        (new >= 0)
        & (new < rows)
        & (lax.div(new, steps) == owner)
        & (later <= lax.rem(row, steps))
    )
    lane = lax.broadcasted_iota(jnp.int32, (rows, LANES), 1)
    blank = jnp.zeros((LANES - rows, width), BF16)
    for g in range(group // pack):
        mine = slice(g * rows, (g + 1) * rows)
        these = slice(g * pack, (g + 1) * pack)
        pair = pairs_of(qs[mine, :])
        key = keys[these].reshape(cached, width)
        value = values[these].reshape(cached, width)
        new_key = jnp.concatenate([ks[mine, :].astype(BF16), blank], axis=0)
        new_value = jnp.concatenate([vs[mine, :].astype(BF16), blank], axis=0)
        for j in range(heads // 2):
            span = slice(j * tile, (j + 1) * tile)
            these_rows = slice(j * 2 * rows, (j + 1) * 2 * rows)
            scores[these_rows, :cached] = across(pair[:, span], key[:, span])
            scores[these_rows, cached:] = across(pair[:, span], new_key[:, span])
        base = jnp.zeros_like(owner)
        for k in range(pack):
            base = jnp.where(owner == k, lengths[g * pack + k] - seq * slots, base)
        at_new = base + later
        valid = (old & (position < base)) | (fresh & (at_new >= 0) & (at_new < slots))
        masked = jnp.where(valid, scores[...] * HEAD ** (-0.5), -1e30)
        peak = jnp.max(masked, axis=-1, keepdims=True)
        expo = jnp.where(valid, jnp.exp(masked - peak), 0.0)
        total = jnp.sum(expo, axis=-1, keepdims=True)
        probs = expo.astype(BF16)
        for j in range(heads // 2):
            span = slice(j * tile, (j + 1) * tile)
            these_rows = slice(j * 2 * rows, (j + 1) * 2 * rows)
            mixed = dot(probs[these_rows, :cached], value[:, span])
            mixed = mixed + dot(probs[these_rows, cached:], new_value[:, span])
            part[mine, span] = jnp.where(left, mixed[:rows], mixed[rows:])
        line = jnp.zeros((rows, LANES), F32)
        for k, piece in enumerate(split_three(peak) + split_three(total)[:2]):
            for h in range(heads):
                line = jnp.where(lane == k * heads + h, piece[h * rows : (h + 1) * rows], line)
        stats[mine, :] = line
    share = width // nx
    for dx in range(nx):
        to = place.x_after(dx)
        messages[dx][:, :share] = part[:, at(to, share)].astype(BF16)
        messages[dx][:, share:] = pltpu.roll(
            stats[...], lax.rem(LANES - to * (heads // nx), LANES), 1
        ).astype(BF16)
    for i in range(group):
        base, _ = place_of(i)

        @pl.when((base > -steps) & (base < slots))
        def _():
            for copy in copies(i):
                copy.wait()


def expand(factor, count):
    rows = factor.shape[0]
    return jnp.concatenate(
        [jnp.broadcast_to(factor[:, h : h + 1], (rows, HEAD)) for h in range(count)], axis=1
    )


def merge(messages, heads, share):
    peaks, totals = [], []
    for message in messages:
        stats = message[:, share:].astype(F32)
        peaks.append(stats + turn(stats, -heads) + turn(stats, -2 * heads))
        totals.append(turn(stats, -3 * heads) + turn(stats, -4 * heads))
    peak = functools.reduce(jnp.maximum, peaks)
    scales = [jnp.exp(p - peak) for p in peaks]
    total = sum(t * s for t, s in zip(totals, scales))
    return peak, total, scales


def merge_x_kernel(place, heads, *refs):
    share = refs[0].shape[1] - LANES
    count = share // HEAD
    out = refs[-1]
    messages = [r[...] for r in refs[:-1]]
    peak, total, scales = merge(messages, heads, share)
    out[:, :share] = sum(
        m[:, :share].astype(F32) * expand(s, count) for m, s in zip(messages, scales)
    ).astype(BF16)
    lane = lax.broadcasted_iota(jnp.int32, peak.shape, 1)
    tile = jnp.zeros_like(peak)
    for k, piece in enumerate(split_three(peak) + split_three(total)[:2]):
        tile = tile + turn(jnp.where(lane < count, piece, 0.0), k * heads)
    out[:, share:] = tile.astype(BF16)


def merge_z_kernel(place, heads, *refs):
    share = refs[0].shape[1] - LANES
    count = share // HEAD
    out = refs[-1]
    messages = [r[...] for r in refs[:-1]]
    _, total, scales = merge(messages, heads, share)
    out[...] = sum(
        m[:, :share].astype(F32) * expand(s / total, count) for m, s in zip(messages, scales)
    ).astype(BF16)


def out_kernel(place, attn, *refs):
    nx = place.nx
    weights = refs[: 2 * nx]
    bias, out, total = refs[2 * nx :]
    depth = weights[0].shape[0]
    core = place.core()
    for k in range(nx):
        block = lax.rem(place.y() + nx - 1 - k, nx)
        total[block] = dot(attn[:, at(core, depth)], weights[2 * k][...]) + dot(
            attn[:, at(1 - core, depth)], weights[2 * k + 1][...]
        )
    total[place.x()] = total[place.x()] + bias[...]
    out[...] = total[...].astype(BF16)


def add_out_kernel(place, *refs):
    out = refs[-1]
    for dy in range(place.ny):
        total = refs[dy][...].astype(F32)
        for dx in range(1, place.nx):
            total = total + refs[dx * place.ny + dy][...].astype(F32)
        out[place.y_before(dy)] = total.astype(BF16)


def up_kernel(place, *refs):
    ny, nz = place.ny, place.nz
    toks = refs[:ny]
    gathered = refs[ny : ny + nz]
    gain, shift, own, sibling, bias, out, mid_out, proj, normed, flat = refs[ny + nz :]
    group, steps, _ = toks[0].shape
    rows = group * steps
    cols = gathered[0].shape[3]
    for dz in range(nz):
        span = at(place.z_partner(dz), place.nx * cols)
        for y in range(ny):
            proj[y * rows : (y + 1) * rows, span] = side_by_side(gathered[dz].at[y], 0, cols)
    for j in range(ny):
        here = at(place.y_before(j), rows)
        flatten(toks[j], flat, 0)
        mid = flat[...] + proj[here, :]
        if j == 0:
            mid_out[...] = mid
        normed[here, :] = layer_norm(mid, gain[...], shift[...]).astype(BF16)
    first = (place.y() == 0).astype(F32)
    out[...] = (two_halves(normed, own, sibling) + bias[...] * first).astype(BF16)


def down_kernel(place, *refs):
    nx, ny = place.nx, place.ny
    parts = refs[:ny]
    own, sibling = refs[ny : ny + 2]
    outs = refs[ny + 2 : ny + 2 + nx]
    feed = refs[-1]
    total = sum(p[...].astype(F32) for p in parts)
    hidden = (0.5 * total * (1.0 + lax.erf(total * 0.5**0.5))).astype(BF16)
    ncols = own.shape[1]
    feed[:, at(place.core(), ncols)] = dot(hidden, own[...])
    feed[:, at(1 - place.core(), ncols)] = dot(hidden, sibling[...])
    width = outs[0].shape[1]
    for dx in range(nx):
        outs[dx][...] = feed[:, at(place.x_after(dx), width)].astype(BF16)


def add_x_kernel(place, *refs):
    refs[-1][...] = sum(r[...].astype(F32) for r in refs[:-1]).astype(BF16)


def add_z_kernel(place, *refs):
    outs, total = refs[place.nz : -1], refs[-1]
    total[...] = sum(r[...].astype(F32) for r in refs[: place.nz])
    rows = outs[0].shape[0]
    for dy in range(place.ny):
        outs[dy][...] = total[at(lax.rem(place.y() + dy, place.ny), rows), :].astype(BF16)


def last_kernel(place, *refs):
    nx, ny = place.nx, place.ny
    parts = refs[: nx * ny]
    mid, bias, out, full = refs[nx * ny :]
    group, steps, _ = out.shape
    width = parts[0].shape[1]
    for dx in range(nx):
        for dy in range(ny):
            block = place.y_before(dy) * nx + place.x_before(dx)
            full[:, at(block, width)] = parts[dx * ny + dy][...].astype(F32)
    result = mid[...] + full[...] + bias[...]
    for i in range(group):
        out[i] = result[i * steps : (i + 1) * steps].astype(BF16)


def shape(sizes, kind=BF16):
    return jax.ShapeDtypeStruct(tuple(sizes), kind)


def body(
    tokens,
    lengths,
    cache_keys,
    cache_values,
    norm1_gain,
    norm1_bias,
    w_query,
    b_query,
    w_key,
    b_key,
    w_value,
    b_value,
    w_out,
    b_out,
    norm2_gain,
    norm2_bias,
    w_up,
    b_up,
    w_down,
    b_down,
):
    place = Place(lax.axis_size("seq"), lax.axis_size("req"))
    nx, ny = place.nx, place.ny
    group, steps, width = tokens.shape
    slots = cache_keys.shape[1]
    rows = group * steps
    heads = width // HEAD
    share = width // nx
    bind = functools.partial

    def row(vector):
        return vector.reshape(1, -1)

    def spread(by_dy):
        return [
            by_dy[dy] if dx == 0 and dy == 0 else place.move(by_dy[dy], dx, dy)
            for dx in range(nx)
            for dy in range(ny)
        ]

    toks = [tokens] + [place.move(tokens, dy=dy) for dy in range(1, ny)]
    cols = w_query.shape[1]
    own = [w_query, w_key, w_value]
    siblings = [place.move(weight, dc=1) for weight in own]
    scales = row(jnp.concatenate([norm1_gain, norm1_bias]))
    biases = row(jnp.concatenate([b_query, b_key, b_value]))
    normed, *own = call(
        norm_kernel,
        "norm",
        [tokens, scales, *own],
        [shape((rows, width))] + [shape(w.shape) for w in own],
        in_specs=[VMEM] * 2 + [HBM] * 3,
        scratch=[pltpu.VMEM((rows, width), F32), pltpu.SemaphoreType.DMA((3,))],
        limit=52.75,
    )
    parts = call(
        bind(qkv_kernel, place),
        "norm_qkv",
        [normed, *toks[1:], scales, biases, *own, *siblings],
        [shape((rows, 3 * cols))] * ny,
        scratch=[pltpu.VMEM(((ny - 1) * rows, width), F32), pltpu.VMEM((ny * rows, width), BF16)],
    )
    *parts, tied_up, tied_down = lax.optimization_barrier((*parts, w_up, w_down))
    w_up_sibling = place.move(tied_up, dc=1)
    w_down_sibling = place.move(tied_down, dc=1)
    parts, tied_keys, tied_values = lax.optimization_barrier((parts, cache_keys, cache_values))
    new_keys, new_values, keys, values, mark = call(
        cache_kernel,
        "caches",
        [tied_keys, tied_values],
        [shape(cache_keys.shape)] * 4 + [shape((8, LANES), F32)],
        in_specs=[HBM, HBM],
        out_specs=[HBM, HBM, VMEM, VMEM, VMEM],
        scratch=[pltpu.SemaphoreType.DMA((2, group)), pltpu.SemaphoreType.DMA((2, group))],
        moved=16 * 1024 * 1024,
        limit=46,
    )
    qkv = call(
        bind(add_columns_kernel, place),
        "add_qkv",
        [*spread(parts), mark],
        shape((nx, rows, 3 * cols)),
    )
    qkv, w_up_sibling, w_down_sibling, tied = lax.optimization_barrier(
        (qkv, w_up_sibling, w_down_sibling, w_out)
    )
    pieces = place.gather_z(qkv)
    blocks = [place.transpose(tied, nx - 1 - k) for k in range(nx)]
    pieces, blocks = lax.optimization_barrier((pieces, blocks))
    w_outs = []
    for block in blocks:
        w_outs += [block, place.move(block, dc=1)]
    pack = max(1, min(group, 256 // slots))
    window = min(32, slots)
    new_keys, new_values, *messages = call(
        bind(attention_kernel, place, heads, steps),
        "attention",
        [*pieces, lengths, keys, values, new_keys, new_values],
        [shape(cache_keys.shape)] * 2 + [shape((rows, share + LANES))] * nx,
        in_specs=[VMEM] * place.nz + [SMEM, VMEM, VMEM, HBM, HBM],
        out_specs=[HBM, HBM] + [VMEM] * nx,
        scratch=[
            pltpu.VMEM((rows, width), F32),
            pltpu.VMEM((rows, width), F32),
            pltpu.VMEM((rows, width), F32),
            pltpu.VMEM((heads * pack * steps, pack * slots + LANES), F32),
            pltpu.VMEM((rows, width), F32),
            pltpu.VMEM((rows, LANES), F32),
            pltpu.VMEM((group, window, width), BF16),
            pltpu.VMEM((group, window, width), BF16),
            pltpu.SemaphoreType.DMA((2, group)),
        ],
        aliases={place.nz + 3: 0, place.nz + 4: 1},
        moved=16 * 1024 * 1024,
    )
    messages, w_outs = lax.optimization_barrier((messages, w_outs))
    messages = [messages[0]] + [place.move(messages[dx], dx=dx) for dx in range(1, nx)]
    merged = call(
        bind(merge_x_kernel, place, heads), "merge_x", messages, shape((rows, share + LANES))
    )
    pieces = place.gather_z(merged)
    attn = call(bind(merge_z_kernel, place, heads), "merge_z", pieces, shape((rows, share)))
    out_part = call(
        bind(out_kernel, place),
        "out",
        [attn, *w_outs, row(b_out)],
        shape((nx, rows, cols)),
        scratch=[pltpu.VMEM((nx, rows, cols), F32)],
    )
    projected = call(
        bind(add_out_kernel, place),
        "add_out",
        spread([out_part] * ny),
        shape((ny, nx, rows, cols)),
    )
    up_part, mid = call(
        bind(up_kernel, place),
        "norm_up",
        [
            *toks,
            *place.gather_z(projected),
            row(norm2_gain),
            row(norm2_bias),
            w_up,
            w_up_sibling,
            row(b_up),
        ],
        [shape((ny * rows, w_up.shape[1])), shape((rows, width), F32)],
        scratch=[
            pltpu.VMEM((ny * rows, width), F32),
            pltpu.VMEM((ny * rows, width), BF16),
            pltpu.VMEM((rows, width), F32),
        ],
    )
    up_parts = [up_part] + [place.move(up_part, dy=dy) for dy in range(1, ny)]
    piece = CORES * w_down.shape[1] // nx
    feeds = call(
        bind(down_kernel, place),
        "gelu_down",
        [*up_parts, w_down, w_down_sibling],
        [shape((ny * rows, piece))] * nx,
        scratch=[pltpu.VMEM((ny * rows, CORES * w_down.shape[1]), F32)],
    )
    feeds = [feeds[0]] + [place.move(feeds[dx], dx=dx) for dx in range(1, nx)]
    feed = call(bind(add_x_kernel, place), "add_x", feeds, shape((ny * rows, piece)))
    summed = call(
        bind(add_z_kernel, place),
        "add_z",
        place.gather_z(feed),
        [shape((rows, piece))] * ny,
        scratch=[pltpu.VMEM((ny * rows, piece), F32)],
    )
    hidden_out = call(
        bind(last_kernel, place),
        "last",
        [*spread(summed), mid, row(b_down)],
        shape(tokens.shape),
        scratch=[pltpu.VMEM((rows, width), F32)],
    )
    return (hidden_out, new_keys, new_values)


def solution(mesh):
    in_specs = (
        P("req", None, None),
        P("req"),
        P("req", "seq", None),
        P("req", "seq", None),
        P(),
        P(),
        P("req", "seq"),
        P("seq"),
        P("req", "seq"),
        P("seq"),
        P("req", "seq"),
        P("seq"),
        P("req", "seq"),
        P("seq"),
        P(),
        P(),
        P("req", "seq"),
        P("seq"),
        P("seq", "req"),
        P(),
    )
    out_specs = (P("req", None, None), P("req", "seq", None), P("req", "seq", None))
    return jax.shard_map(body, mesh=mesh, in_specs=in_specs, out_specs=out_specs, check_vma=False)
```

```python
import functools

import jax
import jax.numpy as jnp
from jax import lax
from jax.experimental import pallas as pl
from jax.experimental.pallas import tpu as pltpu
from jax.sharding import PartitionSpec as P

HEAD = 128
LANES = 128
CORES = 2
BF16 = jnp.bfloat16
F32 = jnp.float32
VMEM = pl.BlockSpec(memory_space=pltpu.VMEM)
SMEM = pl.BlockSpec(memory_space=pltpu.SMEM)
HBM = pl.BlockSpec(memory_space=pltpu.HBM)


class Place:
    def __init__(self, seqs, reqs):
        self.ny = reqs // CORES
        self.nx = self.ny
        self.nz = seqs // self.nx
        self.seqs = seqs

    def x(self):
        return lax.rem(lax.axis_index("seq"), self.nx)

    def y(self):
        return lax.div(lax.axis_index("req"), CORES)

    def core(self):
        return lax.rem(lax.axis_index("req"), CORES)

    def x_before(self, dx):
        return lax.rem(self.x() + self.nx - dx, self.nx)

    def x_after(self, dx):
        return lax.rem(self.x() + dx, self.nx)

    def y_before(self, dy):
        return lax.rem(self.y() + self.ny - dy, self.ny)

    def z_partner(self, dz):
        return lax.bitwise_xor(lax.div(lax.axis_index("seq"), self.nx), dz)

    def move(self, value, dx=0, dy=0, dc=0, dz=0):
        pairs = []
        for z in range(self.nz):
            for x in range(self.nx):
                for y in range(self.ny):
                    for c in range(CORES):
                        to_x, to_y, to_c = (x + dx) % self.nx, (y + dy) % self.ny, (c + dc) % CORES
                        to_z = z ^ dz
                        pairs.append(
                            (
                                ((z * self.nx + x) * self.ny + y) * CORES + c,
                                ((to_z * self.nx + to_x) * self.ny + to_y) * CORES + to_c,
                            )
                        )
        return lax.ppermute(value, ("seq", "req"), pairs)

    def transpose(self, value, k):
        n = self.nx
        pairs = []
        for z in range(self.nz):
            for x in range(n):
                for y in range(n):
                    for c in range(CORES):
                        pairs.append(
                            (
                                ((z * n + x) * n + y) * CORES + c,
                                ((z * n + y) * n + (x - k) % n) * CORES + c,
                            )
                        )
        return lax.ppermute(value, ("seq", "req"), pairs)

    def gather_z(self, value):
        return [value] + [self.move(value, dz=dz) for dz in range(1, self.nz)]


def layer_norm(values, gain, shift):
    center = values - jnp.mean(values, axis=-1, keepdims=True)
    spread = jnp.mean(center * center, axis=-1, keepdims=True)
    return center * lax.rsqrt(spread + 1e-05) * gain + shift


def dot(a, b):
    return jnp.dot(a, b, preferred_element_type=F32)


def across(a, b):
    return lax.dot_general(a, b, (((1,), (1,)), ((), ())), preferred_element_type=F32)


def at(index, size):
    return pl.ds(pl.multiple_of(index * size, size), size)


def call(kernel, name, ins, outs, in_specs=None, out_specs=None, scratch=(), moved=2**20, limit=20, aliases=None):
    single = not isinstance(outs, (list, tuple))
    specs = out_specs or (VMEM if single else [VMEM] * len(outs))
    return pl.pallas_call(
        kernel,
        name=name,
        out_shape=outs,
        in_specs=in_specs or [VMEM] * len(ins),
        out_specs=specs,
        scratch_shapes=list(scratch),
        input_output_aliases=aliases or {},
        cost_estimate=pl.CostEstimate(flops=0, bytes_accessed=moved, transcendentals=0),
        compiler_params=pltpu.CompilerParams(vmem_limit_bytes=int(limit * 1024 * 1024)),
    )(*ins)


def side_by_side(blocks, start, size):
    return jnp.concatenate(
        [blocks[x, :, start : start + size].astype(F32) for x in range(blocks.shape[0])], axis=1
    )


def two_halves(rows_by_k, own, sibling):
    depth = own.shape[0]
    req = lax.axis_index("req")
    other = req + 1 - 2 * lax.rem(req, CORES)
    return dot(rows_by_k[:, at(req, depth)], own[...]) + dot(
        rows_by_k[:, at(other, depth)], sibling[...]
    )


def flatten(block, flat, start):
    group, steps, _ = block.shape
    for i in range(group):
        flat[start + i * steps : start + (i + 1) * steps, :] = block[i].astype(F32)


def norm_kernel(tokens, scales, *refs):
    count = (len(refs) - 3) // 2
    weights, out, kept = refs[:count], refs[count], refs[count + 1 : 2 * count + 1]
    flat, sems = refs[-2:]
    copies = [
        pltpu.make_async_copy(source, target, sems.at[k])
        for k, (source, target) in enumerate(zip(weights, kept))
    ]
    for copy in copies:
        copy.start()
    width = out.shape[1]
    flatten(tokens, flat, 0)
    out[...] = layer_norm(flat[...], scales[:, :width], scales[:, width:]).astype(BF16)
    for copy in copies:
        copy.wait()


def qkv_kernel(place, *refs):
    ny = place.ny
    mine = refs[0]
    toks = refs[1:ny]
    scales, biases = refs[ny : ny + 2]
    weights = refs[ny + 2 : ny + 8]
    outs = refs[ny + 8 : 2 * ny + 8]
    flat, normed = refs[2 * ny + 8 :]
    rows, width = mine.shape
    normed[:rows, :] = mine[...]
    for j, tok in enumerate(toks):
        flatten(tok, flat, j * rows)
    normed[rows:, :] = layer_norm(flat[...], scales[:, :width], scales[:, width:]).astype(BF16)
    cols = weights[0].shape[1]
    for k in range(3):
        acc = two_halves(normed, weights[k], weights[3 + k])
        for j in range(ny):
            part = acc[j * rows : (j + 1) * rows]
            if j == 0:
                part = part + biases[:, k * cols : (k + 1) * cols]
            outs[(ny - j) % ny][:, k * cols : (k + 1) * cols] = part.astype(BF16)


def add_columns_kernel(place, *refs):
    out = refs[-1]
    for dx in range(place.nx):
        total = refs[dx * place.ny][...].astype(F32)
        for dy in range(1, place.ny):
            total = total + refs[dx * place.ny + dy][...].astype(F32)
        out[place.x_before(dx)] = total.astype(BF16)


def cache_kernel(keys_in, values_in, keys_out, values_out, keys, values, mark, in_sems, out_sems):
    group = keys.shape[0]
    arrays = ((keys_in, keys, keys_out), (values_in, values, values_out))
    coming = [
        pltpu.make_async_copy(source.at[i], here.at[i], in_sems.at[k, i])
        for i in range(group)
        for k, (source, here, _) in enumerate(arrays)
    ]
    going = [
        pltpu.make_async_copy(here.at[i], target.at[i], out_sems.at[k, i])
        for i in range(group)
        for k, (_, here, target) in enumerate(arrays)
    ]
    for copy in coming:
        copy.start()
    mark[...] = jnp.zeros_like(mark)
    for arrived, copy in zip(coming, going):
        arrived.wait()
        copy.start()
    for copy in going:
        copy.wait()


def split_three(value):
    first = value.astype(BF16).astype(F32)
    rest = value - first
    second = rest.astype(BF16).astype(F32)
    return first, second, rest - second


def turn(value, by):
    return pltpu.roll(value, by % LANES, 1)


def pairs_of(query):
    side = lax.rem(lax.div(lax.broadcasted_iota(jnp.int32, query.shape, 1), HEAD), 2)
    return jnp.concatenate(
        [jnp.where(side == 0, query, 0.0), jnp.where(side == 1, query, 0.0)], axis=0
    ).astype(BF16)


def attention_kernel(place, heads, steps, *refs):
    nx, nz = place.nx, place.nz
    gathered = refs[:nz]
    lengths, keys, values = refs[nz : nz + 3]
    keys_out, values_out = refs[nz + 5 : nz + 7]
    messages = refs[nz + 7 : nz + 7 + nx]
    qs, ks, vs, scores, part, stats, k_rows, v_rows, sems = refs[nz + 7 + nx :]
    group, slots, width = keys.shape
    cols = width // place.seqs
    seq = lax.axis_index("seq")
    for dz in range(nz):
        span = at(place.z_partner(dz), nx * cols)
        for k, target in enumerate((qs, ks, vs)):
            target[:, span] = side_by_side(gathered[dz], k * cols, cols)

    window = k_rows.shape[1]

    def place_of(i):
        base = lengths[i] - seq * slots
        start = jnp.clip(lax.div(jnp.maximum(base, 0), 16) * 16, 0, slots - window)
        return base, pl.multiple_of(start, 16)

    def copies(i):
        _, start = place_of(i)
        return [
            pltpu.make_async_copy(
                rows.at[i], target.at[i, pl.ds(start, window), :], sems.at[k, i]
            )
            for k, (rows, target) in enumerate(((k_rows, keys_out), (v_rows, values_out)))
        ]

    for i in range(group):
        base, start = place_of(i)

        @pl.when((base > -steps) & (base < slots))
        def _():
            slot = start + lax.broadcasted_iota(jnp.int32, (window, width), 0)
            for source, fresh, rows in ((keys, ks, k_rows), (values, vs, v_rows)):
                block = source[i, pl.ds(start, window), :].astype(F32)
                for t in range(steps):
                    at_row = fresh[i * steps + t : i * steps + t + 1, :]
                    block = jnp.where(slot == base + t, at_row, block)
                rows[i] = block.astype(BF16)
            for copy in copies(i):
                copy.start()

    pack = max(1, min(group, 256 // slots))
    rows = pack * steps
    tile = 2 * HEAD
    left = lax.broadcasted_iota(jnp.int32, (rows, tile), 1) < HEAD
    many, cached = heads * rows, pack * slots
    row = lax.broadcasted_iota(jnp.int32, (many, cached + LANES), 0)
    column = lax.broadcasted_iota(jnp.int32, (many, cached + LANES), 1)
    owner = lax.div(lax.rem(row, rows), steps)
    position = lax.rem(column, slots)
    old = (column < cached) & (owner == lax.div(column, slots))
    new = column - cached
    later = lax.rem(new, steps)
    fresh = (
        (new >= 0)
        & (new < rows)
        & (lax.div(new, steps) == owner)
        & (later <= lax.rem(row, steps))
    )
    lane = lax.broadcasted_iota(jnp.int32, (rows, LANES), 1)
    blank = jnp.zeros((LANES - rows, width), BF16)
    for g in range(group // pack):
        mine = slice(g * rows, (g + 1) * rows)
        these = slice(g * pack, (g + 1) * pack)
        pair = pairs_of(qs[mine, :])
        key = keys[these].reshape(cached, width)
        value = values[these].reshape(cached, width)
        new_key = jnp.concatenate([ks[mine, :].astype(BF16), blank], axis=0)
        new_value = jnp.concatenate([vs[mine, :].astype(BF16), blank], axis=0)
        for j in range(heads // 2):
            span = slice(j * tile, (j + 1) * tile)
            these_rows = slice(j * 2 * rows, (j + 1) * 2 * rows)
            scores[these_rows, :cached] = across(pair[:, span], key[:, span])
            scores[these_rows, cached:] = across(pair[:, span], new_key[:, span])
        base = jnp.zeros_like(owner)
        for k in range(pack):
            base = jnp.where(owner == k, lengths[g * pack + k] - seq * slots, base)
        at_new = base + later
        valid = (old & (position < base)) | (fresh & (at_new >= 0) & (at_new < slots))
        masked = jnp.where(valid, scores[...] * HEAD ** (-0.5), -1e30)
        peak = jnp.max(masked, axis=-1, keepdims=True)
        expo = jnp.where(valid, jnp.exp(masked - peak), 0.0)
        total = jnp.sum(expo, axis=-1, keepdims=True)
        probs = expo.astype(BF16)
        for j in range(heads // 2):
            span = slice(j * tile, (j + 1) * tile)
            these_rows = slice(j * 2 * rows, (j + 1) * 2 * rows)
            mixed = dot(probs[these_rows, :cached], value[:, span])
            mixed = mixed + dot(probs[these_rows, cached:], new_value[:, span])
            part[mine, span] = jnp.where(left, mixed[:rows], mixed[rows:])
        line = jnp.zeros((rows, LANES), F32)
        for k, piece in enumerate(split_three(peak) + split_three(total)[:2]):
            for h in range(heads):
                line = jnp.where(lane == k * heads + h, piece[h * rows : (h + 1) * rows], line)
        stats[mine, :] = line
    share = width // nx
    for dx in range(nx):
        to = place.x_after(dx)
        messages[dx][:, :share] = part[:, at(to, share)].astype(BF16)
        messages[dx][:, share:] = pltpu.roll(
            stats[...], lax.rem(LANES - to * (heads // nx), LANES), 1
        ).astype(BF16)
    for i in range(group):
        base, _ = place_of(i)

        @pl.when((base > -steps) & (base < slots))
        def _():
            for copy in copies(i):
                copy.wait()


def expand(factor, count):
    rows = factor.shape[0]
    return jnp.concatenate(
        [jnp.broadcast_to(factor[:, h : h + 1], (rows, HEAD)) for h in range(count)], axis=1
    )


def merge(messages, heads, share):
    peaks, totals = [], []
    for message in messages:
        stats = message[:, share:].astype(F32)
        peaks.append(stats + turn(stats, -heads) + turn(stats, -2 * heads))
        totals.append(turn(stats, -3 * heads) + turn(stats, -4 * heads))
    peak = functools.reduce(jnp.maximum, peaks)
    scales = [jnp.exp(p - peak) for p in peaks]
    total = sum(t * s for t, s in zip(totals, scales))
    return peak, total, scales


def merge_x_kernel(place, heads, *refs):
    share = refs[0].shape[1] - LANES
    count = share // HEAD
    out = refs[-1]
    messages = [r[...] for r in refs[:-1]]
    peak, total, scales = merge(messages, heads, share)
    out[:, :share] = sum(
        m[:, :share].astype(F32) * expand(s, count) for m, s in zip(messages, scales)
    ).astype(BF16)
    lane = lax.broadcasted_iota(jnp.int32, peak.shape, 1)
    tile = jnp.zeros_like(peak)
    for k, piece in enumerate(split_three(peak) + split_three(total)[:2]):
        tile = tile + turn(jnp.where(lane < count, piece, 0.0), k * heads)
    out[:, share:] = tile.astype(BF16)


def merge_z_kernel(place, heads, *refs):
    share = refs[0].shape[1] - LANES
    count = share // HEAD
    out = refs[-1]
    messages = [r[...] for r in refs[:-1]]
    _, total, scales = merge(messages, heads, share)
    out[...] = sum(
        m[:, :share].astype(F32) * expand(s / total, count) for m, s in zip(messages, scales)
    ).astype(BF16)


def out_kernel(place, attn, *refs):
    nx = place.nx
    weights = refs[: 2 * nx]
    bias, out, total = refs[2 * nx :]
    depth = weights[0].shape[0]
    core = place.core()
    for k in range(nx):
        block = lax.rem(place.y() + nx - 1 - k, nx)
        total[block] = dot(attn[:, at(core, depth)], weights[2 * k][...]) + dot(
            attn[:, at(1 - core, depth)], weights[2 * k + 1][...]
        )
    total[place.x()] = total[place.x()] + bias[...]
    out[...] = total[...].astype(BF16)


def add_out_kernel(place, *refs):
    out = refs[-1]
    for dy in range(place.ny):
        total = refs[dy][...].astype(F32)
        for dx in range(1, place.nx):
            total = total + refs[dx * place.ny + dy][...].astype(F32)
        out[place.y_before(dy)] = total.astype(BF16)


def up_kernel(place, *refs):
    ny, nz = place.ny, place.nz
    toks = refs[:ny]
    gathered = refs[ny : ny + nz]
    gain, shift, own, sibling, bias, out, mid_out, proj, normed, flat = refs[ny + nz :]
    group, steps, _ = toks[0].shape
    rows = group * steps
    cols = gathered[0].shape[3]
    for dz in range(nz):
        span = at(place.z_partner(dz), place.nx * cols)
        for y in range(ny):
            proj[y * rows : (y + 1) * rows, span] = side_by_side(gathered[dz].at[y], 0, cols)
    for j in range(ny):
        here = at(place.y_before(j), rows)
        flatten(toks[j], flat, 0)
        mid = flat[...] + proj[here, :]
        if j == 0:
            mid_out[...] = mid
        normed[here, :] = layer_norm(mid, gain[...], shift[...]).astype(BF16)
    first = (place.y() == 0).astype(F32)
    out[...] = (two_halves(normed, own, sibling) + bias[...] * first).astype(BF16)


def down_kernel(place, *refs):
    nx, ny = place.nx, place.ny
    parts = refs[:ny]
    own, sibling = refs[ny : ny + 2]
    outs = refs[ny + 2 : ny + 2 + nx]
    feed = refs[-1]
    total = sum(p[...].astype(F32) for p in parts)
    hidden = (0.5 * total * (1.0 + lax.erf(total * 0.5**0.5))).astype(BF16)
    ncols = own.shape[1]
    feed[:, at(place.core(), ncols)] = dot(hidden, own[...])
    feed[:, at(1 - place.core(), ncols)] = dot(hidden, sibling[...])
    width = outs[0].shape[1]
    for dx in range(nx):
        outs[dx][...] = feed[:, at(place.x_after(dx), width)].astype(BF16)


def add_x_kernel(place, *refs):
    refs[-1][...] = sum(r[...].astype(F32) for r in refs[:-1]).astype(BF16)


def add_z_kernel(place, *refs):
    outs, total = refs[place.nz : -1], refs[-1]
    total[...] = sum(r[...].astype(F32) for r in refs[: place.nz])
    rows = outs[0].shape[0]
    for dy in range(place.ny):
        outs[dy][...] = total[at(lax.rem(place.y() + dy, place.ny), rows), :].astype(BF16)


def last_kernel(place, *refs):
    nx, ny = place.nx, place.ny
    parts = refs[: nx * ny]
    mid, bias, out, full = refs[nx * ny :]
    group, steps, _ = out.shape
    width = parts[0].shape[1]
    for dx in range(nx):
        for dy in range(ny):
            block = place.y_before(dy) * nx + place.x_before(dx)
            full[:, at(block, width)] = parts[dx * ny + dy][...].astype(F32)
    result = mid[...] + full[...] + bias[...]
    for i in range(group):
        out[i] = result[i * steps : (i + 1) * steps].astype(BF16)


def shape(sizes, kind=BF16):
    return jax.ShapeDtypeStruct(tuple(sizes), kind)


def body(
    tokens,
    lengths,
    cache_keys,
    cache_values,
    norm1_gain,
    norm1_bias,
    w_query,
    b_query,
    w_key,
    b_key,
    w_value,
    b_value,
    w_out,
    b_out,
    norm2_gain,
    norm2_bias,
    w_up,
    b_up,
    w_down,
    b_down,
):
    place = Place(lax.axis_size("seq"), lax.axis_size("req"))
    nx, ny = place.nx, place.ny
    group, steps, width = tokens.shape
    slots = cache_keys.shape[1]
    rows = group * steps
    heads = width // HEAD
    share = width // nx
    bind = functools.partial

    def row(vector):
        return vector.reshape(1, -1)

    def spread(by_dy):
        return [
            by_dy[dy] if dx == 0 and dy == 0 else place.move(by_dy[dy], dx, dy)
            for dx in range(nx)
            for dy in range(ny)
        ]

    toks = [tokens] + [place.move(tokens, dy=dy) for dy in range(1, ny)]
    cols = w_query.shape[1]
    own = [w_query, w_key, w_value]
    siblings = [place.move(weight, dc=1) for weight in own]
    scales = row(jnp.concatenate([norm1_gain, norm1_bias]))
    biases = row(jnp.concatenate([b_query, b_key, b_value]))
    normed, *own = call(
        norm_kernel,
        "norm",
        [tokens, scales, *own],
        [shape((rows, width))] + [shape(w.shape) for w in own],
        in_specs=[VMEM] * 2 + [HBM] * 3,
        scratch=[pltpu.VMEM((rows, width), F32), pltpu.SemaphoreType.DMA((3,))],
        limit=52.75,
    )
    parts = call(
        bind(qkv_kernel, place),
        "norm_qkv",
        [normed, *toks[1:], scales, biases, *own, *siblings],
        [shape((rows, 3 * cols))] * ny,
        scratch=[pltpu.VMEM(((ny - 1) * rows, width), F32), pltpu.VMEM((ny * rows, width), BF16)],
    )
    *parts, tied_up, tied_down = lax.optimization_barrier((*parts, w_up, w_down))
    w_up_sibling = place.move(tied_up, dc=1)
    w_down_sibling = place.move(tied_down, dc=1)
    parts, tied_keys, tied_values = lax.optimization_barrier((parts, cache_keys, cache_values))
    new_keys, new_values, keys, values, mark = call(
        cache_kernel,
        "caches",
        [tied_keys, tied_values],
        [shape(cache_keys.shape)] * 4 + [shape((8, LANES), F32)],
        in_specs=[HBM, HBM],
        out_specs=[HBM, HBM, VMEM, VMEM, VMEM],
        scratch=[pltpu.SemaphoreType.DMA((2, group)), pltpu.SemaphoreType.DMA((2, group))],
        moved=16 * 1024 * 1024,
        limit=46,
    )
    qkv = call(
        bind(add_columns_kernel, place),
        "add_qkv",
        [*spread(parts), mark],
        shape((nx, rows, 3 * cols)),
    )
    qkv, w_up_sibling, w_down_sibling, tied = lax.optimization_barrier(
        (qkv, w_up_sibling, w_down_sibling, w_out)
    )
    pieces = place.gather_z(qkv)
    blocks = [place.transpose(tied, nx - 1 - k) for k in range(nx)]
    pack = max(1, min(group, 256 // slots))
    window = min(32, slots)
    new_keys, new_values, *messages = call(
        bind(attention_kernel, place, heads, steps),
        "attention",
        [*pieces, lengths, keys, values, new_keys, new_values],
        [shape(cache_keys.shape)] * 2 + [shape((rows, share + LANES))] * nx,
        in_specs=[VMEM] * place.nz + [SMEM, VMEM, VMEM, HBM, HBM],
        out_specs=[HBM, HBM] + [VMEM] * nx,
        scratch=[
            pltpu.VMEM((rows, width), F32),
            pltpu.VMEM((rows, width), F32),
            pltpu.VMEM((rows, width), F32),
            pltpu.VMEM((heads * pack * steps, pack * slots + LANES), F32),
            pltpu.VMEM((rows, width), F32),
            pltpu.VMEM((rows, LANES), F32),
            pltpu.VMEM((group, window, width), BF16),
            pltpu.VMEM((group, window, width), BF16),
            pltpu.SemaphoreType.DMA((2, group)),
        ],
        aliases={place.nz + 3: 0, place.nz + 4: 1},
    )
    messages, blocks = lax.optimization_barrier((messages, blocks))
    w_outs = []
    for block in blocks:
        w_outs += [block, place.move(block, dc=1)]
    messages = [messages[0]] + [place.move(messages[dx], dx=dx) for dx in range(1, nx)]
    merged = call(
        bind(merge_x_kernel, place, heads), "merge_x", messages, shape((rows, share + LANES))
    )
    merged, *w_outs = lax.optimization_barrier((merged, *w_outs))
    pieces = place.gather_z(merged)
    attn = call(bind(merge_z_kernel, place, heads), "merge_z", pieces, shape((rows, share)))
    out_part = call(
        bind(out_kernel, place),
        "out",
        [attn, *w_outs, row(b_out)],
        shape((nx, rows, cols)),
        scratch=[pltpu.VMEM((nx, rows, cols), F32)],
    )
    projected = call(
        bind(add_out_kernel, place),
        "add_out",
        spread([out_part] * ny),
        shape((ny, nx, rows, cols)),
    )
    up_part, mid = call(
        bind(up_kernel, place),
        "norm_up",
        [
            *toks,
            *place.gather_z(projected),
            row(norm2_gain),
            row(norm2_bias),
            w_up,
            w_up_sibling,
            row(b_up),
        ],
        [shape((ny * rows, w_up.shape[1])), shape((rows, width), F32)],
        scratch=[
            pltpu.VMEM((ny * rows, width), F32),
            pltpu.VMEM((ny * rows, width), BF16),
            pltpu.VMEM((rows, width), F32),
        ],
    )
    up_parts = [up_part] + [place.move(up_part, dy=dy) for dy in range(1, ny)]
    piece = CORES * w_down.shape[1] // nx
    feeds = call(
        bind(down_kernel, place),
        "gelu_down",
        [*up_parts, w_down, w_down_sibling],
        [shape((ny * rows, piece))] * nx,
        scratch=[pltpu.VMEM((ny * rows, CORES * w_down.shape[1]), F32)],
    )
    feeds = [feeds[0]] + [place.move(feeds[dx], dx=dx) for dx in range(1, nx)]
    feed = call(bind(add_x_kernel, place), "add_x", feeds, shape((ny * rows, piece)))
    summed = call(
        bind(add_z_kernel, place),
        "add_z",
        place.gather_z(feed),
        [shape((rows, piece))] * ny,
        scratch=[pltpu.VMEM((ny * rows, piece), F32)],
    )
    hidden_out = call(
        bind(last_kernel, place),
        "last",
        [*spread(summed), mid, row(b_down)],
        shape(tokens.shape),
        scratch=[pltpu.VMEM((rows, width), F32)],
    )
    return (hidden_out, new_keys, new_values)


def solution(mesh):
    in_specs = (
        P("req", None, None),
        P("req"),
        P("req", "seq", None),
        P("req", "seq", None),
        P(),
        P(),
        P("req", "seq"),
        P("seq"),
        P("req", "seq"),
        P("seq"),
        P("req", "seq"),
        P("seq"),
        P("req", "seq"),
        P("seq"),
        P(),
        P(),
        P("req", "seq"),
        P("seq"),
        P("seq", "req"),
        P(),
    )
    out_specs = (P("req", None, None), P("req", "seq", None), P("req", "seq", None))
    return jax.shard_map(body, mesh=mesh, in_specs=in_specs, out_specs=out_specs, check_vma=False)
```

```python
import functools

import jax
import jax.numpy as jnp
from jax import lax
from jax.experimental import pallas as pl
from jax.experimental.pallas import tpu as pltpu
from jax.sharding import PartitionSpec as P

HEAD = 128
LANES = 128
CORES = 2
BF16 = jnp.bfloat16
F32 = jnp.float32
VMEM = pl.BlockSpec(memory_space=pltpu.VMEM)
SMEM = pl.BlockSpec(memory_space=pltpu.SMEM)
HBM = pl.BlockSpec(memory_space=pltpu.HBM)


class Place:
    def __init__(self, seqs, reqs):
        self.ny = reqs // CORES
        self.nx = self.ny
        self.nz = seqs // self.nx
        self.seqs = seqs

    def x(self):
        return lax.rem(lax.axis_index("seq"), self.nx)

    def y(self):
        return lax.div(lax.axis_index("req"), CORES)

    def core(self):
        return lax.rem(lax.axis_index("req"), CORES)

    def x_before(self, dx):
        return lax.rem(self.x() + self.nx - dx, self.nx)

    def x_after(self, dx):
        return lax.rem(self.x() + dx, self.nx)

    def y_before(self, dy):
        return lax.rem(self.y() + self.ny - dy, self.ny)

    def z_partner(self, dz):
        return lax.bitwise_xor(lax.div(lax.axis_index("seq"), self.nx), dz)

    def move(self, value, dx=0, dy=0, dc=0, dz=0):
        pairs = []
        for z in range(self.nz):
            for x in range(self.nx):
                for y in range(self.ny):
                    for c in range(CORES):
                        to_x, to_y, to_c = (x + dx) % self.nx, (y + dy) % self.ny, (c + dc) % CORES
                        to_z = z ^ dz
                        pairs.append(
                            (
                                ((z * self.nx + x) * self.ny + y) * CORES + c,
                                ((to_z * self.nx + to_x) * self.ny + to_y) * CORES + to_c,
                            )
                        )
        return lax.ppermute(value, ("seq", "req"), pairs)

    def transpose(self, value, k):
        n = self.nx
        pairs = []
        for z in range(self.nz):
            for x in range(n):
                for y in range(n):
                    for c in range(CORES):
                        pairs.append(
                            (
                                ((z * n + x) * n + y) * CORES + c,
                                ((z * n + y) * n + (x - k) % n) * CORES + c,
                            )
                        )
        return lax.ppermute(value, ("seq", "req"), pairs)

    def gather_z(self, value):
        return [value] + [self.move(value, dz=dz) for dz in range(1, self.nz)]


def layer_norm(values, gain, shift):
    center = values - jnp.mean(values, axis=-1, keepdims=True)
    spread = jnp.mean(center * center, axis=-1, keepdims=True)
    return center * lax.rsqrt(spread + 1e-05) * gain + shift


def dot(a, b):
    return jnp.dot(a, b, preferred_element_type=F32)


def across(a, b):
    return lax.dot_general(a, b, (((1,), (1,)), ((), ())), preferred_element_type=F32)


def at(index, size):
    return pl.ds(pl.multiple_of(index * size, size), size)


def call(kernel, name, ins, outs, in_specs=None, out_specs=None, scratch=(), moved=2**20, limit=20, aliases=None):
    single = not isinstance(outs, (list, tuple))
    specs = out_specs or (VMEM if single else [VMEM] * len(outs))
    return pl.pallas_call(
        kernel,
        name=name,
        out_shape=outs,
        in_specs=in_specs or [VMEM] * len(ins),
        out_specs=specs,
        scratch_shapes=list(scratch),
        input_output_aliases=aliases or {},
        cost_estimate=pl.CostEstimate(flops=0, bytes_accessed=moved, transcendentals=0),
        compiler_params=pltpu.CompilerParams(vmem_limit_bytes=int(limit * 1024 * 1024)),
    )(*ins)


def side_by_side(blocks, start, size):
    return jnp.concatenate(
        [blocks[x, :, start : start + size].astype(F32) for x in range(blocks.shape[0])], axis=1
    )


def two_halves(rows_by_k, own, sibling):
    depth = own.shape[0]
    req = lax.axis_index("req")
    other = req + 1 - 2 * lax.rem(req, CORES)
    return dot(rows_by_k[:, at(req, depth)], own[...]) + dot(
        rows_by_k[:, at(other, depth)], sibling[...]
    )


def flatten(block, flat, start):
    group, steps, _ = block.shape
    for i in range(group):
        flat[start + i * steps : start + (i + 1) * steps, :] = block[i].astype(F32)


def norm_kernel(tokens, scales, *refs):
    count = (len(refs) - 3) // 2
    weights, out, kept = refs[:count], refs[count], refs[count + 1 : 2 * count + 1]
    flat, sems = refs[-2:]
    copies = [
        pltpu.make_async_copy(source, target, sems.at[k])
        for k, (source, target) in enumerate(zip(weights, kept))
    ]
    for copy in copies:
        copy.start()
    width = out.shape[1]
    flatten(tokens, flat, 0)
    out[...] = layer_norm(flat[...], scales[:, :width], scales[:, width:]).astype(BF16)
    for copy in copies:
        copy.wait()


def qkv_kernel(place, *refs):
    ny = place.ny
    mine = refs[0]
    toks = refs[1:ny]
    scales, biases = refs[ny : ny + 2]
    weights = refs[ny + 2 : ny + 8]
    outs = refs[ny + 8 : 2 * ny + 8]
    flat, normed = refs[2 * ny + 8 :]
    rows, width = mine.shape
    normed[:rows, :] = mine[...]
    for j, tok in enumerate(toks):
        flatten(tok, flat, j * rows)
    normed[rows:, :] = layer_norm(flat[...], scales[:, :width], scales[:, width:]).astype(BF16)
    cols = weights[0].shape[1]
    for k in range(3):
        acc = two_halves(normed, weights[k], weights[3 + k])
        for j in range(ny):
            part = acc[j * rows : (j + 1) * rows]
            if j == 0:
                part = part + biases[:, k * cols : (k + 1) * cols]
            outs[(ny - j) % ny][:, k * cols : (k + 1) * cols] = part.astype(BF16)


def add_columns_kernel(place, *refs):
    out = refs[-1]
    for dx in range(place.nx):
        total = refs[dx * place.ny][...].astype(F32)
        for dy in range(1, place.ny):
            total = total + refs[dx * place.ny + dy][...].astype(F32)
        out[place.x_before(dx)] = total.astype(BF16)


def cache_kernel(keys_in, values_in, keys_out, values_out, keys, values, in_sems, out_sems):
    group = keys.shape[0]
    arrays = ((keys_in, keys, keys_out), (values_in, values, values_out))
    coming = [
        pltpu.make_async_copy(source.at[i], here.at[i], in_sems.at[k, i])
        for i in range(group)
        for k, (source, here, _) in enumerate(arrays)
    ]
    going = [
        pltpu.make_async_copy(here.at[i], target.at[i], out_sems.at[k, i])
        for i in range(group)
        for k, (_, here, target) in enumerate(arrays)
    ]
    for copy in coming:
        copy.start()
    for arrived, copy in zip(coming, going):
        arrived.wait()
        copy.start()
    for copy in going:
        copy.wait()


def split_three(value):
    first = value.astype(BF16).astype(F32)
    rest = value - first
    second = rest.astype(BF16).astype(F32)
    return first, second, rest - second


def turn(value, by):
    return pltpu.roll(value, by % LANES, 1)


def pairs_of(query):
    side = lax.rem(lax.div(lax.broadcasted_iota(jnp.int32, query.shape, 1), HEAD), 2)
    return jnp.concatenate(
        [jnp.where(side == 0, query, 0.0), jnp.where(side == 1, query, 0.0)], axis=0
    ).astype(BF16)


def attention_kernel(place, heads, steps, *refs):
    nx, nz = place.nx, place.nz
    gathered = refs[:nz]
    lengths, keys, values = refs[nz : nz + 3]
    keys_out, values_out = refs[nz + 5 : nz + 7]
    messages = refs[nz + 7 : nz + 7 + nx]
    qs, ks, vs, scores, part, stats, k_rows, v_rows, sems = refs[nz + 7 + nx :]
    group, slots, width = keys.shape
    cols = width // place.seqs
    seq = lax.axis_index("seq")
    for dz in range(nz):
        span = at(place.z_partner(dz), nx * cols)
        for k, target in enumerate((qs, ks, vs)):
            target[:, span] = side_by_side(gathered[dz], k * cols, cols)

    window = k_rows.shape[1]

    def place_of(i):
        base = lengths[i] - seq * slots
        start = jnp.clip(lax.div(jnp.maximum(base, 0), 16) * 16, 0, slots - window)
        return base, pl.multiple_of(start, 16)

    def copies(i):
        _, start = place_of(i)
        return [
            pltpu.make_async_copy(
                rows.at[i], target.at[i, pl.ds(start, window), :], sems.at[k, i]
            )
            for k, (rows, target) in enumerate(((k_rows, keys_out), (v_rows, values_out)))
        ]

    for i in range(group):
        base, start = place_of(i)

        @pl.when((base > -steps) & (base < slots))
        def _():
            slot = start + lax.broadcasted_iota(jnp.int32, (window, width), 0)
            for source, fresh, rows in ((keys, ks, k_rows), (values, vs, v_rows)):
                block = source[i, pl.ds(start, window), :].astype(F32)
                for t in range(steps):
                    at_row = fresh[i * steps + t : i * steps + t + 1, :]
                    block = jnp.where(slot == base + t, at_row, block)
                rows[i] = block.astype(BF16)
            for copy in copies(i):
                copy.start()

    pack = max(1, min(group, 256 // slots))
    rows = pack * steps
    tile = 2 * HEAD
    left = lax.broadcasted_iota(jnp.int32, (rows, tile), 1) < HEAD
    many, cached = heads * rows, pack * slots
    row = lax.broadcasted_iota(jnp.int32, (many, cached + LANES), 0)
    column = lax.broadcasted_iota(jnp.int32, (many, cached + LANES), 1)
    owner = lax.div(lax.rem(row, rows), steps)
    position = lax.rem(column, slots)
    old = (column < cached) & (owner == lax.div(column, slots))
    new = column - cached
    later = lax.rem(new, steps)
    fresh = (
        (new >= 0)
        & (new < rows)
        & (lax.div(new, steps) == owner)
        & (later <= lax.rem(row, steps))
    )
    lane = lax.broadcasted_iota(jnp.int32, (rows, LANES), 1)
    blank = jnp.zeros((LANES - rows, width), BF16)
    for g in range(group // pack):
        mine = slice(g * rows, (g + 1) * rows)
        these = slice(g * pack, (g + 1) * pack)
        pair = pairs_of(qs[mine, :])
        key = keys[these].reshape(cached, width)
        value = values[these].reshape(cached, width)
        new_key = jnp.concatenate([ks[mine, :].astype(BF16), blank], axis=0)
        new_value = jnp.concatenate([vs[mine, :].astype(BF16), blank], axis=0)
        for j in range(heads // 2):
            span = slice(j * tile, (j + 1) * tile)
            these_rows = slice(j * 2 * rows, (j + 1) * 2 * rows)
            scores[these_rows, :cached] = across(pair[:, span], key[:, span])
            scores[these_rows, cached:] = across(pair[:, span], new_key[:, span])
        base = jnp.zeros_like(owner)
        for k in range(pack):
            base = jnp.where(owner == k, lengths[g * pack + k] - seq * slots, base)
        at_new = base + later
        valid = (old & (position < base)) | (fresh & (at_new >= 0) & (at_new < slots))
        masked = jnp.where(valid, scores[...] * HEAD ** (-0.5), -1e30)
        peak = jnp.max(masked, axis=-1, keepdims=True)
        expo = jnp.where(valid, jnp.exp(masked - peak), 0.0)
        total = jnp.sum(expo, axis=-1, keepdims=True)
        probs = expo.astype(BF16)
        for j in range(heads // 2):
            span = slice(j * tile, (j + 1) * tile)
            these_rows = slice(j * 2 * rows, (j + 1) * 2 * rows)
            mixed = dot(probs[these_rows, :cached], value[:, span])
            mixed = mixed + dot(probs[these_rows, cached:], new_value[:, span])
            part[mine, span] = jnp.where(left, mixed[:rows], mixed[rows:])
        line = jnp.zeros((rows, LANES), F32)
        for k, piece in enumerate(split_three(peak) + split_three(total)[:2]):
            for h in range(heads):
                line = jnp.where(lane == k * heads + h, piece[h * rows : (h + 1) * rows], line)
        stats[mine, :] = line
    share = width // nx
    for dx in range(nx):
        to = place.x_after(dx)
        messages[dx][:, :share] = part[:, at(to, share)].astype(BF16)
        messages[dx][:, share:] = pltpu.roll(
            stats[...], lax.rem(LANES - to * (heads // nx), LANES), 1
        ).astype(BF16)
    for i in range(group):
        base, _ = place_of(i)

        @pl.when((base > -steps) & (base < slots))
        def _():
            for copy in copies(i):
                copy.wait()


def expand(factor, count):
    rows = factor.shape[0]
    return jnp.concatenate(
        [jnp.broadcast_to(factor[:, h : h + 1], (rows, HEAD)) for h in range(count)], axis=1
    )


def merge(messages, heads, share):
    peaks, totals = [], []
    for message in messages:
        stats = message[:, share:].astype(F32)
        peaks.append(stats + turn(stats, -heads) + turn(stats, -2 * heads))
        totals.append(turn(stats, -3 * heads) + turn(stats, -4 * heads))
    peak = functools.reduce(jnp.maximum, peaks)
    scales = [jnp.exp(p - peak) for p in peaks]
    total = sum(t * s for t, s in zip(totals, scales))
    return peak, total, scales


def merge_x_kernel(place, heads, *refs):
    share = refs[0].shape[1] - LANES
    count = share // HEAD
    out = refs[-1]
    messages = [r[...] for r in refs[:-1]]
    peak, total, scales = merge(messages, heads, share)
    out[:, :share] = sum(
        m[:, :share].astype(F32) * expand(s, count) for m, s in zip(messages, scales)
    ).astype(BF16)
    lane = lax.broadcasted_iota(jnp.int32, peak.shape, 1)
    tile = jnp.zeros_like(peak)
    for k, piece in enumerate(split_three(peak) + split_three(total)[:2]):
        tile = tile + turn(jnp.where(lane < count, piece, 0.0), k * heads)
    out[:, share:] = tile.astype(BF16)


def out_kernel(place, heads, *refs):
    nx, nz = place.nx, place.nz
    messages = [r[...] for r in refs[:nz]]
    weights = refs[nz : nz + 2 * nx]
    bias, out, total, attn = refs[nz + 2 * nx :]
    share = attn.shape[1]
    _, whole, scales = merge(messages, heads, share)
    attn[...] = sum(
        m[:, :share].astype(F32) * expand(s / whole, share // HEAD)
        for m, s in zip(messages, scales)
    ).astype(BF16)
    depth = weights[0].shape[0]
    core = place.core()
    for k in range(nx):
        block = lax.rem(place.y() + k, nx)
        total[block] = dot(attn[:, at(core, depth)], weights[2 * k][...]) + dot(
            attn[:, at(1 - core, depth)], weights[2 * k + 1][...]
        )
    total[place.x()] = total[place.x()] + bias[...]
    out[...] = total[...].astype(BF16)


def add_out_kernel(place, *refs):
    out = refs[-1]
    for dy in range(place.ny):
        total = refs[dy][...].astype(F32)
        for dx in range(1, place.nx):
            total = total + refs[dx * place.ny + dy][...].astype(F32)
        out[place.y_before(dy)] = total.astype(BF16)


def up_kernel(place, *refs):
    ny, nz = place.ny, place.nz
    toks = refs[:ny]
    gathered = refs[ny : ny + nz]
    gain, shift, own, sibling, bias, out, mid_out, proj, normed, flat = refs[ny + nz :]
    group, steps, _ = toks[0].shape
    rows = group * steps
    cols = gathered[0].shape[3]
    for dz in range(nz):
        span = at(place.z_partner(dz), place.nx * cols)
        for y in range(ny):
            proj[y * rows : (y + 1) * rows, span] = side_by_side(gathered[dz].at[y], 0, cols)
    for j in range(ny):
        here = at(place.y_before(j), rows)
        flatten(toks[j], flat, 0)
        mid = flat[...] + proj[here, :]
        if j == 0:
            mid_out[...] = mid
        normed[here, :] = layer_norm(mid, gain[...], shift[...]).astype(BF16)
    first = (place.y() == 0).astype(F32)
    out[...] = (two_halves(normed, own, sibling) + bias[...] * first).astype(BF16)


def down_kernel(place, *refs):
    nx, ny = place.nx, place.ny
    parts = refs[:ny]
    own, sibling = refs[ny : ny + 2]
    outs = refs[ny + 2 : ny + 2 + nx]
    feed = refs[-1]
    total = sum(p[...].astype(F32) for p in parts)
    hidden = (0.5 * total * (1.0 + lax.erf(total * 0.5**0.5))).astype(BF16)
    ncols = own.shape[1]
    feed[:, at(place.core(), ncols)] = dot(hidden, own[...])
    feed[:, at(1 - place.core(), ncols)] = dot(hidden, sibling[...])
    width = outs[0].shape[1]
    for dx in range(nx):
        outs[dx][...] = feed[:, at(place.x_after(dx), width)].astype(BF16)


def add_x_kernel(place, *refs):
    refs[-1][...] = sum(r[...].astype(F32) for r in refs[:-1]).astype(BF16)


def add_z_kernel(place, *refs):
    outs, total = refs[place.nz : -1], refs[-1]
    total[...] = sum(r[...].astype(F32) for r in refs[: place.nz])
    rows = outs[0].shape[0]
    for dy in range(place.ny):
        outs[dy][...] = total[at(lax.rem(place.y() + dy, place.ny), rows), :].astype(BF16)


def last_kernel(place, *refs):
    nx, ny = place.nx, place.ny
    parts = refs[: nx * ny]
    mid, bias, out, full = refs[nx * ny :]
    group, steps, _ = out.shape
    width = parts[0].shape[1]
    for dx in range(nx):
        for dy in range(ny):
            block = place.y_before(dy) * nx + place.x_before(dx)
            full[:, at(block, width)] = parts[dx * ny + dy][...].astype(F32)
    result = mid[...] + full[...] + bias[...]
    for i in range(group):
        out[i] = result[i * steps : (i + 1) * steps].astype(BF16)


def shape(sizes, kind=BF16):
    return jax.ShapeDtypeStruct(tuple(sizes), kind)


def body(
    tokens,
    lengths,
    cache_keys,
    cache_values,
    norm1_gain,
    norm1_bias,
    w_query,
    b_query,
    w_key,
    b_key,
    w_value,
    b_value,
    w_out,
    b_out,
    norm2_gain,
    norm2_bias,
    w_up,
    b_up,
    w_down,
    b_down,
):
    place = Place(lax.axis_size("seq"), lax.axis_size("req"))
    nx, ny = place.nx, place.ny
    group, steps, width = tokens.shape
    slots = cache_keys.shape[1]
    rows = group * steps
    heads = width // HEAD
    share = width // nx
    bind = functools.partial

    def row(vector):
        return vector.reshape(1, -1)

    def spread(by_dy):
        return [
            by_dy[dy] if dx == 0 and dy == 0 else place.move(by_dy[dy], dx, dy)
            for dx in range(nx)
            for dy in range(ny)
        ]

    toks = [tokens] + [place.move(tokens, dy=dy) for dy in range(1, ny)]
    cols = w_query.shape[1]
    own = [w_query, w_key, w_value]
    siblings = [place.move(weight, dc=1) for weight in own]
    scales = row(jnp.concatenate([norm1_gain, norm1_bias]))
    biases = row(jnp.concatenate([b_query, b_key, b_value]))
    normed, *own = call(
        norm_kernel,
        "norm",
        [tokens, scales, *own],
        [shape((rows, width))] + [shape(w.shape) for w in own],
        in_specs=[VMEM] * 2 + [HBM] * 3,
        scratch=[pltpu.VMEM((rows, width), F32), pltpu.SemaphoreType.DMA((3,))],
        limit=52.75,
    )
    parts = call(
        bind(qkv_kernel, place),
        "norm_qkv",
        [normed, *toks[1:], scales, biases, *own, *siblings],
        [shape((rows, 3 * cols))] * ny,
        scratch=[pltpu.VMEM(((ny - 1) * rows, width), F32), pltpu.VMEM((ny * rows, width), BF16)],
    )
    *parts, tied_up, tied_down = lax.optimization_barrier((*parts, w_up, w_down))
    w_up_sibling = place.move(tied_up, dc=1)
    w_down_sibling = place.move(tied_down, dc=1)
    qkv = call(
        bind(add_columns_kernel, place),
        "add_qkv",
        spread(parts),
        shape((nx, rows, 3 * cols)),
    )
    qkv, w_up_sibling, w_down_sibling, tied = lax.optimization_barrier(
        (qkv, w_up_sibling, w_down_sibling, w_out)
    )
    qkv, tied_keys, tied_values = lax.optimization_barrier((qkv, cache_keys, cache_values))
    new_keys, new_values, keys, values = call(
        cache_kernel,
        "caches",
        [tied_keys, tied_values],
        [shape(cache_keys.shape)] * 4,
        in_specs=[HBM, HBM],
        out_specs=[HBM, HBM, VMEM, VMEM],
        scratch=[pltpu.SemaphoreType.DMA((2, group)), pltpu.SemaphoreType.DMA((2, group))],
        moved=16 * 1024 * 1024,
        limit=46,
    )
    pieces = place.gather_z(qkv)
    blocks = [place.transpose(tied, k) for k in range(nx)]
    pack = max(1, min(group, 256 // slots))
    window = min(32, slots)
    new_keys, new_values, *messages = call(
        bind(attention_kernel, place, heads, steps),
        "attention",
        [*pieces, lengths, keys, values, new_keys, new_values],
        [shape(cache_keys.shape)] * 2 + [shape((rows, share + LANES))] * nx,
        in_specs=[VMEM] * place.nz + [SMEM, VMEM, VMEM, HBM, HBM],
        out_specs=[HBM, HBM] + [VMEM] * nx,
        scratch=[
            pltpu.VMEM((rows, width), F32),
            pltpu.VMEM((rows, width), F32),
            pltpu.VMEM((rows, width), F32),
            pltpu.VMEM((heads * pack * steps, pack * slots + LANES), F32),
            pltpu.VMEM((rows, width), F32),
            pltpu.VMEM((rows, LANES), F32),
            pltpu.VMEM((group, window, width), BF16),
            pltpu.VMEM((group, window, width), BF16),
            pltpu.SemaphoreType.DMA((2, group)),
        ],
        aliases={place.nz + 3: 0, place.nz + 4: 1},
    )
    messages, blocks = lax.optimization_barrier((messages, blocks))
    w_outs = []
    for block in blocks:
        w_outs += [block, place.move(block, dc=1)]
    messages = [messages[0]] + [place.move(messages[dx], dx=dx) for dx in range(1, nx)]
    merged = call(
        bind(merge_x_kernel, place, heads), "merge_x", messages, shape((rows, share + LANES))
    )
    merged, *w_outs = lax.optimization_barrier((merged, *w_outs))
    pieces = place.gather_z(merged)
    out_part = call(
        bind(out_kernel, place, heads),
        "out",
        [*pieces, *w_outs, row(b_out)],
        shape((nx, rows, cols)),
        scratch=[pltpu.VMEM((nx, rows, cols), F32), pltpu.VMEM((rows, share), BF16)],
    )
    projected = call(
        bind(add_out_kernel, place),
        "add_out",
        spread([out_part] * ny),
        shape((ny, nx, rows, cols)),
    )
    up_part, mid = call(
        bind(up_kernel, place),
        "norm_up",
        [
            *toks,
            *place.gather_z(projected),
            row(norm2_gain),
            row(norm2_bias),
            w_up,
            w_up_sibling,
            row(b_up),
        ],
        [shape((ny * rows, w_up.shape[1])), shape((rows, width), F32)],
        scratch=[
            pltpu.VMEM((ny * rows, width), F32),
            pltpu.VMEM((ny * rows, width), BF16),
            pltpu.VMEM((rows, width), F32),
        ],
    )
    up_parts = [up_part] + [place.move(up_part, dy=dy) for dy in range(1, ny)]
    piece = CORES * w_down.shape[1] // nx
    feeds = call(
        bind(down_kernel, place),
        "gelu_down",
        [*up_parts, w_down, w_down_sibling],
        [shape((ny * rows, piece))] * nx,
        scratch=[pltpu.VMEM((ny * rows, CORES * w_down.shape[1]), F32)],
    )
    feeds = [feeds[0]] + [place.move(feeds[dx], dx=dx) for dx in range(1, nx)]
    feed = call(bind(add_x_kernel, place), "add_x", feeds, shape((ny * rows, piece)))
    summed = call(
        bind(add_z_kernel, place),
        "add_z",
        place.gather_z(feed),
        [shape((rows, piece))] * ny,
        scratch=[pltpu.VMEM((ny * rows, piece), F32)],
    )
    hidden_out = call(
        bind(last_kernel, place),
        "last",
        [*spread(summed), mid, row(b_down)],
        shape(tokens.shape),
        scratch=[pltpu.VMEM((rows, width), F32)],
    )
    return (hidden_out, new_keys, new_values)


def solution(mesh):
    in_specs = (
        P("req", None, None),
        P("req"),
        P("req", "seq", None),
        P("req", "seq", None),
        P(),
        P(),
        P("req", "seq"),
        P("seq"),
        P("req", "seq"),
        P("seq"),
        P("req", "seq"),
        P("seq"),
        P("req", "seq"),
        P("seq"),
        P(),
        P(),
        P("req", "seq"),
        P("seq"),
        P("seq", "req"),
        P(),
    )
    out_specs = (P("req", None, None), P("req", "seq", None), P("req", "seq", None))
    return jax.shard_map(body, mesh=mesh, in_specs=in_specs, out_specs=out_specs, check_vma=False)
```

```python
import functools

import jax
import jax.numpy as jnp
from jax import lax
from jax.experimental import pallas as pl
from jax.experimental.pallas import tpu as pltpu
from jax.sharding import PartitionSpec as P

HEAD = 128
LANES = 128
CORES = 2
BF16 = jnp.bfloat16
F32 = jnp.float32
VMEM = pl.BlockSpec(memory_space=pltpu.VMEM)
SMEM = pl.BlockSpec(memory_space=pltpu.SMEM)
HBM = pl.BlockSpec(memory_space=pltpu.HBM)


class Place:
    def __init__(self, seqs, reqs):
        self.ny = reqs // CORES
        self.nx = self.ny
        self.nz = seqs // self.nx
        self.seqs = seqs

    def x(self):
        return lax.rem(lax.axis_index("seq"), self.nx)

    def y(self):
        return lax.div(lax.axis_index("req"), CORES)

    def core(self):
        return lax.rem(lax.axis_index("req"), CORES)

    def x_before(self, dx):
        return lax.rem(self.x() + self.nx - dx, self.nx)

    def x_after(self, dx):
        return lax.rem(self.x() + dx, self.nx)

    def y_before(self, dy):
        return lax.rem(self.y() + self.ny - dy, self.ny)

    def z_partner(self, dz):
        return lax.bitwise_xor(lax.div(lax.axis_index("seq"), self.nx), dz)

    def move(self, value, dx=0, dy=0, dc=0, dz=0):
        pairs = []
        for z in range(self.nz):
            for x in range(self.nx):
                for y in range(self.ny):
                    for c in range(CORES):
                        to_x, to_y, to_c = (x + dx) % self.nx, (y + dy) % self.ny, (c + dc) % CORES
                        to_z = z ^ dz
                        pairs.append(
                            (
                                ((z * self.nx + x) * self.ny + y) * CORES + c,
                                ((to_z * self.nx + to_x) * self.ny + to_y) * CORES + to_c,
                            )
                        )
        return lax.ppermute(value, ("seq", "req"), pairs)

    def transpose(self, value, k):
        n = self.nx
        pairs = []
        for z in range(self.nz):
            for x in range(n):
                for y in range(n):
                    for c in range(CORES):
                        pairs.append(
                            (
                                ((z * n + x) * n + y) * CORES + c,
                                ((z * n + y) * n + (x - k) % n) * CORES + c,
                            )
                        )
        return lax.ppermute(value, ("seq", "req"), pairs)

    def gather_z(self, value):
        return [value] + [self.move(value, dz=dz) for dz in range(1, self.nz)]


def layer_norm(values, gain, shift):
    center = values - jnp.mean(values, axis=-1, keepdims=True)
    spread = jnp.mean(center * center, axis=-1, keepdims=True)
    return center * lax.rsqrt(spread + 1e-05) * gain + shift


def dot(a, b):
    return jnp.dot(a, b, preferred_element_type=F32)


def across(a, b):
    return lax.dot_general(a, b, (((1,), (1,)), ((), ())), preferred_element_type=F32)


def at(index, size):
    return pl.ds(pl.multiple_of(index * size, size), size)


def call(kernel, name, ins, outs, in_specs=None, out_specs=None, scratch=(), moved=2**20, limit=20, aliases=None):
    single = not isinstance(outs, (list, tuple))
    specs = out_specs or (VMEM if single else [VMEM] * len(outs))
    return pl.pallas_call(
        kernel,
        name=name,
        out_shape=outs,
        in_specs=in_specs or [VMEM] * len(ins),
        out_specs=specs,
        scratch_shapes=list(scratch),
        input_output_aliases=aliases or {},
        cost_estimate=pl.CostEstimate(flops=0, bytes_accessed=moved, transcendentals=0),
        compiler_params=pltpu.CompilerParams(vmem_limit_bytes=int(limit * 1024 * 1024)),
    )(*ins)


def side_by_side(blocks, start, size):
    return jnp.concatenate(
        [blocks[x, :, start : start + size].astype(F32) for x in range(blocks.shape[0])], axis=1
    )


def two_halves(rows_by_k, own, sibling):
    depth = own.shape[0]
    req = lax.axis_index("req")
    other = req + 1 - 2 * lax.rem(req, CORES)
    return dot(rows_by_k[:, at(req, depth)], own[...]) + dot(
        rows_by_k[:, at(other, depth)], sibling[...]
    )


def flatten(block, flat, start):
    group, steps, _ = block.shape
    for i in range(group):
        flat[start + i * steps : start + (i + 1) * steps, :] = block[i].astype(F32)


def norm_kernel(tokens, scales, *refs):
    count = (len(refs) - 3) // 2
    weights, out, kept = refs[:count], refs[count], refs[count + 1 : 2 * count + 1]
    flat, sems = refs[-2:]
    copies = [
        pltpu.make_async_copy(source, target, sems.at[k])
        for k, (source, target) in enumerate(zip(weights, kept))
    ]
    for copy in copies:
        copy.start()
    width = out.shape[1]
    flatten(tokens, flat, 0)
    out[...] = layer_norm(flat[...], scales[:, :width], scales[:, width:]).astype(BF16)
    for copy in copies:
        copy.wait()


def qkv_kernel(place, *refs):
    ny = place.ny
    mine = refs[0]
    toks = refs[1:ny]
    scales, biases = refs[ny : ny + 2]
    weights = refs[ny + 2 : ny + 8]
    outs = refs[ny + 8 : 2 * ny + 8]
    flat, normed = refs[2 * ny + 8 :]
    rows, width = mine.shape
    normed[:rows, :] = mine[...]
    for j, tok in enumerate(toks):
        flatten(tok, flat, j * rows)
    normed[rows:, :] = layer_norm(flat[...], scales[:, :width], scales[:, width:]).astype(BF16)
    cols = weights[0].shape[1]
    for k in range(3):
        acc = two_halves(normed, weights[k], weights[3 + k])
        for j in range(ny):
            part = acc[j * rows : (j + 1) * rows]
            if j == 0:
                part = part + biases[:, k * cols : (k + 1) * cols]
            outs[(ny - j) % ny][:, k * cols : (k + 1) * cols] = part.astype(BF16)


def add_columns_kernel(place, *refs):
    out = refs[-1]
    for dx in range(place.nx):
        total = refs[dx * place.ny][...].astype(F32)
        for dy in range(1, place.ny):
            total = total + refs[dx * place.ny + dy][...].astype(F32)
        out[place.x_before(dx)] = total.astype(BF16)


def cache_kernel(keys_in, values_in, keys_out, values_out, keys, values, mark, in_sems, out_sems):
    group = keys.shape[0]
    arrays = ((keys_in, keys, keys_out), (values_in, values, values_out))
    coming = [
        pltpu.make_async_copy(source.at[i], here.at[i], in_sems.at[k, i])
        for i in range(group)
        for k, (source, here, _) in enumerate(arrays)
    ]
    going = [
        pltpu.make_async_copy(here.at[i], target.at[i], out_sems.at[k, i])
        for i in range(group)
        for k, (_, here, target) in enumerate(arrays)
    ]
    for copy in coming:
        copy.start()
    mark[...] = jnp.zeros_like(mark)
    for arrived, copy in zip(coming, going):
        arrived.wait()
        copy.start()
    for copy in going:
        copy.wait()


def split_three(value):
    first = value.astype(BF16).astype(F32)
    rest = value - first
    second = rest.astype(BF16).astype(F32)
    return first, second, rest - second


def turn(value, by):
    return pltpu.roll(value, by % LANES, 1)


def pairs_of(query):
    side = lax.rem(lax.div(lax.broadcasted_iota(jnp.int32, query.shape, 1), HEAD), 2)
    return jnp.concatenate(
        [jnp.where(side == 0, query, 0.0), jnp.where(side == 1, query, 0.0)], axis=0
    ).astype(BF16)


def attention_kernel(place, heads, steps, *refs):
    nx, nz = place.nx, place.nz
    gathered = refs[:nz]
    lengths, keys, values = refs[nz : nz + 3]
    keys_out, values_out = refs[nz + 5 : nz + 7]
    messages = refs[nz + 7 : nz + 7 + nx]
    qs, ks, vs, scores, part, stats, k_rows, v_rows, sems = refs[nz + 7 + nx :]
    group, slots, width = keys.shape
    cols = width // place.seqs
    seq = lax.axis_index("seq")
    for dz in range(nz):
        span = at(place.z_partner(dz), nx * cols)
        for k, target in enumerate((qs, ks, vs)):
            target[:, span] = side_by_side(gathered[dz], k * cols, cols)

    window = k_rows.shape[1]

    def place_of(i):
        base = lengths[i] - seq * slots
        start = jnp.clip(lax.div(jnp.maximum(base, 0), 16) * 16, 0, slots - window)
        return base, pl.multiple_of(start, 16)

    def copies(i):
        _, start = place_of(i)
        return [
            pltpu.make_async_copy(
                rows.at[i], target.at[i, pl.ds(start, window), :], sems.at[k, i]
            )
            for k, (rows, target) in enumerate(((k_rows, keys_out), (v_rows, values_out)))
        ]

    for i in range(group):
        base, start = place_of(i)

        @pl.when((base > -steps) & (base < slots))
        def _():
            slot = start + lax.broadcasted_iota(jnp.int32, (window, width), 0)
            for source, fresh, rows in ((keys, ks, k_rows), (values, vs, v_rows)):
                block = source[i, pl.ds(start, window), :].astype(F32)
                for t in range(steps):
                    at_row = fresh[i * steps + t : i * steps + t + 1, :]
                    block = jnp.where(slot == base + t, at_row, block)
                rows[i] = block.astype(BF16)
            for copy in copies(i):
                copy.start()

    pack = max(1, min(group, 256 // slots))
    rows = pack * steps
    tile = 2 * HEAD
    left = lax.broadcasted_iota(jnp.int32, (rows, tile), 1) < HEAD
    many, cached = heads * rows, pack * slots
    row = lax.broadcasted_iota(jnp.int32, (many, cached + LANES), 0)
    column = lax.broadcasted_iota(jnp.int32, (many, cached + LANES), 1)
    owner = lax.div(lax.rem(row, rows), steps)
    position = lax.rem(column, slots)
    old = (column < cached) & (owner == lax.div(column, slots))
    new = column - cached
    later = lax.rem(new, steps)
    fresh = (
        (new >= 0)
        & (new < rows)
        & (lax.div(new, steps) == owner)
        & (later <= lax.rem(row, steps))
    )
    lane = lax.broadcasted_iota(jnp.int32, (rows, LANES), 1)
    blank = jnp.zeros((LANES - rows, width), BF16)
    for g in range(group // pack):
        mine = slice(g * rows, (g + 1) * rows)
        these = slice(g * pack, (g + 1) * pack)
        pair = pairs_of(qs[mine, :])
        key = keys[these].reshape(cached, width)
        value = values[these].reshape(cached, width)
        new_key = jnp.concatenate([ks[mine, :].astype(BF16), blank], axis=0)
        new_value = jnp.concatenate([vs[mine, :].astype(BF16), blank], axis=0)
        for j in range(heads // 2):
            span = slice(j * tile, (j + 1) * tile)
            these_rows = slice(j * 2 * rows, (j + 1) * 2 * rows)
            scores[these_rows, :cached] = across(pair[:, span], key[:, span])
            scores[these_rows, cached:] = across(pair[:, span], new_key[:, span])
        base = jnp.zeros_like(owner)
        for k in range(pack):
            base = jnp.where(owner == k, lengths[g * pack + k] - seq * slots, base)
        at_new = base + later
        valid = (old & (position < base)) | (fresh & (at_new >= 0) & (at_new < slots))
        masked = jnp.where(valid, scores[...] * HEAD ** (-0.5), -1e30)
        peak = jnp.max(masked, axis=-1, keepdims=True)
        expo = jnp.where(valid, jnp.exp(masked - peak), 0.0)
        total = jnp.sum(expo, axis=-1, keepdims=True)
        probs = expo.astype(BF16)
        for j in range(heads // 2):
            span = slice(j * tile, (j + 1) * tile)
            these_rows = slice(j * 2 * rows, (j + 1) * 2 * rows)
            mixed = dot(probs[these_rows, :cached], value[:, span])
            mixed = mixed + dot(probs[these_rows, cached:], new_value[:, span])
            part[mine, span] = jnp.where(left, mixed[:rows], mixed[rows:])
        line = jnp.zeros((rows, LANES), F32)
        for k, piece in enumerate(split_three(peak) + split_three(total)[:2]):
            for h in range(heads):
                line = jnp.where(lane == k * heads + h, piece[h * rows : (h + 1) * rows], line)
        stats[mine, :] = line
    share = width // nx
    for dx in range(nx):
        to = place.x_after(dx)
        messages[dx][:, :share] = part[:, at(to, share)].astype(BF16)
        messages[dx][:, share:] = pltpu.roll(
            stats[...], lax.rem(LANES - to * (heads // nx), LANES), 1
        ).astype(BF16)
    for i in range(group):
        base, _ = place_of(i)

        @pl.when((base > -steps) & (base < slots))
        def _():
            for copy in copies(i):
                copy.wait()


def expand(factor, count):
    rows = factor.shape[0]
    return jnp.concatenate(
        [jnp.broadcast_to(factor[:, h : h + 1], (rows, HEAD)) for h in range(count)], axis=1
    )


def merge(messages, heads, share):
    peaks, totals = [], []
    for message in messages:
        stats = message[:, share:].astype(F32)
        peaks.append(stats + turn(stats, -heads) + turn(stats, -2 * heads))
        totals.append(turn(stats, -3 * heads) + turn(stats, -4 * heads))
    peak = functools.reduce(jnp.maximum, peaks)
    scales = [jnp.exp(p - peak) for p in peaks]
    total = sum(t * s for t, s in zip(totals, scales))
    return peak, total, scales


def merge_x_kernel(place, heads, *refs):
    share = refs[0].shape[1] - LANES
    count = share // HEAD
    out = refs[-1]
    messages = [r[...] for r in refs[:-1]]
    peak, total, scales = merge(messages, heads, share)
    out[:, :share] = sum(
        m[:, :share].astype(F32) * expand(s, count) for m, s in zip(messages, scales)
    ).astype(BF16)
    lane = lax.broadcasted_iota(jnp.int32, peak.shape, 1)
    tile = jnp.zeros_like(peak)
    for k, piece in enumerate(split_three(peak) + split_three(total)[:2]):
        tile = tile + turn(jnp.where(lane < count, piece, 0.0), k * heads)
    out[:, share:] = tile.astype(BF16)


def out_kernel(place, heads, *refs):
    nx, nz = place.nx, place.nz
    messages = [r[...] for r in refs[:nz]]
    weights = refs[nz : nz + 2 * nx]
    bias, out, total, attn = refs[nz + 2 * nx :]
    share = attn.shape[1]
    _, whole, scales = merge(messages, heads, share)
    attn[...] = sum(
        m[:, :share].astype(F32) * expand(s / whole, share // HEAD)
        for m, s in zip(messages, scales)
    ).astype(BF16)
    depth = weights[0].shape[0]
    core = place.core()
    for k in range(nx):
        block = lax.rem(place.y() + k, nx)
        total[block] = dot(attn[:, at(core, depth)], weights[2 * k][...]) + dot(
            attn[:, at(1 - core, depth)], weights[2 * k + 1][...]
        )
    total[place.x()] = total[place.x()] + bias[...]
    out[...] = total[...].astype(BF16)


def add_out_kernel(place, *refs):
    out = refs[-1]
    for dy in range(place.ny):
        total = refs[dy][...].astype(F32)
        for dx in range(1, place.nx):
            total = total + refs[dx * place.ny + dy][...].astype(F32)
        out[place.y_before(dy)] = total.astype(BF16)


def up_kernel(place, *refs):
    ny, nz = place.ny, place.nz
    toks = refs[:ny]
    gathered = refs[ny : ny + nz]
    gain, shift, own, sibling, bias, out, mid_out, proj, normed, flat = refs[ny + nz :]
    group, steps, _ = toks[0].shape
    rows = group * steps
    cols = gathered[0].shape[3]
    for dz in range(nz):
        span = at(place.z_partner(dz), place.nx * cols)
        for y in range(ny):
            proj[y * rows : (y + 1) * rows, span] = side_by_side(gathered[dz].at[y], 0, cols)
    for j in range(ny):
        here = at(place.y_before(j), rows)
        flatten(toks[j], flat, 0)
        mid = flat[...] + proj[here, :]
        if j == 0:
            mid_out[...] = mid
        normed[here, :] = layer_norm(mid, gain[...], shift[...]).astype(BF16)
    first = (place.y() == 0).astype(F32)
    out[...] = (two_halves(normed, own, sibling) + bias[...] * first).astype(BF16)


def down_kernel(place, *refs):
    nx, ny = place.nx, place.ny
    parts = refs[:ny]
    own, sibling = refs[ny : ny + 2]
    outs = refs[ny + 2 : ny + 2 + nx]
    feed = refs[-1]
    total = sum(p[...].astype(F32) for p in parts)
    hidden = (0.5 * total * (1.0 + lax.erf(total * 0.5**0.5))).astype(BF16)
    ncols = own.shape[1]
    feed[:, at(place.core(), ncols)] = dot(hidden, own[...])
    feed[:, at(1 - place.core(), ncols)] = dot(hidden, sibling[...])
    width = outs[0].shape[1]
    for dx in range(nx):
        outs[dx][...] = feed[:, at(place.x_after(dx), width)].astype(BF16)


def add_x_kernel(place, *refs):
    refs[-1][...] = sum(r[...].astype(F32) for r in refs[:-1]).astype(BF16)


def add_z_kernel(place, *refs):
    outs, total = refs[place.nz : -1], refs[-1]
    total[...] = sum(r[...].astype(F32) for r in refs[: place.nz])
    rows = outs[0].shape[0]
    for dy in range(place.ny):
        outs[dy][...] = total[at(lax.rem(place.y() + dy, place.ny), rows), :].astype(BF16)


def last_kernel(place, *refs):
    nx, ny = place.nx, place.ny
    parts = refs[: nx * ny]
    mid, bias, out, full = refs[nx * ny :]
    group, steps, _ = out.shape
    width = parts[0].shape[1]
    for dx in range(nx):
        for dy in range(ny):
            block = place.y_before(dy) * nx + place.x_before(dx)
            full[:, at(block, width)] = parts[dx * ny + dy][...].astype(F32)
    result = mid[...] + full[...] + bias[...]
    for i in range(group):
        out[i] = result[i * steps : (i + 1) * steps].astype(BF16)


def shape(sizes, kind=BF16):
    return jax.ShapeDtypeStruct(tuple(sizes), kind)


def body(
    tokens,
    lengths,
    cache_keys,
    cache_values,
    norm1_gain,
    norm1_bias,
    w_query,
    b_query,
    w_key,
    b_key,
    w_value,
    b_value,
    w_out,
    b_out,
    norm2_gain,
    norm2_bias,
    w_up,
    b_up,
    w_down,
    b_down,
):
    place = Place(lax.axis_size("seq"), lax.axis_size("req"))
    nx, ny = place.nx, place.ny
    group, steps, width = tokens.shape
    slots = cache_keys.shape[1]
    rows = group * steps
    heads = width // HEAD
    share = width // nx
    bind = functools.partial

    def row(vector):
        return vector.reshape(1, -1)

    def spread(by_dy):
        return [
            by_dy[dy] if dx == 0 and dy == 0 else place.move(by_dy[dy], dx, dy)
            for dx in range(nx)
            for dy in range(ny)
        ]

    toks = [tokens] + [place.move(tokens, dy=dy) for dy in range(1, ny)]
    cols = w_query.shape[1]
    own = [w_query, w_key, w_value]
    siblings = [place.move(weight, dc=1) for weight in own]
    scales = row(jnp.concatenate([norm1_gain, norm1_bias]))
    biases = row(jnp.concatenate([b_query, b_key, b_value]))
    normed, *own = call(
        norm_kernel,
        "norm",
        [tokens, scales, *own],
        [shape((rows, width))] + [shape(w.shape) for w in own],
        in_specs=[VMEM] * 2 + [HBM] * 3,
        scratch=[pltpu.VMEM((rows, width), F32), pltpu.SemaphoreType.DMA((3,))],
        limit=52.75,
    )
    parts = call(
        bind(qkv_kernel, place),
        "norm_qkv",
        [normed, *toks[1:], scales, biases, *own, *siblings],
        [shape((rows, 3 * cols))] * ny,
        scratch=[pltpu.VMEM(((ny - 1) * rows, width), F32), pltpu.VMEM((ny * rows, width), BF16)],
    )
    *parts, tied_up, tied_down = lax.optimization_barrier((*parts, w_up, w_down))
    w_up_sibling = place.move(tied_up, dc=1)
    w_down_sibling = place.move(tied_down, dc=1)
    parts, tied_keys, tied_values = lax.optimization_barrier((parts, cache_keys, cache_values))
    new_keys, new_values, keys, values, mark = call(
        cache_kernel,
        "caches",
        [tied_keys, tied_values],
        [shape(cache_keys.shape)] * 4 + [shape((8, LANES), F32)],
        in_specs=[HBM, HBM],
        out_specs=[HBM, HBM, VMEM, VMEM, VMEM],
        scratch=[pltpu.SemaphoreType.DMA((2, group)), pltpu.SemaphoreType.DMA((2, group))],
        moved=16 * 1024 * 1024,
        limit=46,
    )
    qkv = call(
        bind(add_columns_kernel, place),
        "add_qkv",
        [*spread(parts), mark],
        shape((nx, rows, 3 * cols)),
    )
    qkv, w_up_sibling, w_down_sibling, tied = lax.optimization_barrier(
        (qkv, w_up_sibling, w_down_sibling, w_out)
    )
    pieces = place.gather_z(qkv)
    blocks = [place.transpose(tied, k) for k in range(nx)]
    pack = max(1, min(group, 256 // slots))
    window = min(32, slots)
    new_keys, new_values, *messages = call(
        bind(attention_kernel, place, heads, steps),
        "attention",
        [*pieces, lengths, keys, values, new_keys, new_values],
        [shape(cache_keys.shape)] * 2 + [shape((rows, share + LANES))] * nx,
        in_specs=[VMEM] * place.nz + [SMEM, VMEM, VMEM, HBM, HBM],
        out_specs=[HBM, HBM] + [VMEM] * nx,
        scratch=[
            pltpu.VMEM((rows, width), F32),
            pltpu.VMEM((rows, width), F32),
            pltpu.VMEM((rows, width), F32),
            pltpu.VMEM((heads * pack * steps, pack * slots + LANES), F32),
            pltpu.VMEM((rows, width), F32),
            pltpu.VMEM((rows, LANES), F32),
            pltpu.VMEM((group, window, width), BF16),
            pltpu.VMEM((group, window, width), BF16),
            pltpu.SemaphoreType.DMA((2, group)),
        ],
        aliases={place.nz + 3: 0, place.nz + 4: 1},
    )
    messages, blocks = lax.optimization_barrier((messages, blocks))
    w_outs = []
    for block in blocks:
        w_outs += [block, place.move(block, dc=1)]
    messages = [messages[0]] + [place.move(messages[dx], dx=dx) for dx in range(1, nx)]
    merged = call(
        bind(merge_x_kernel, place, heads), "merge_x", messages, shape((rows, share + LANES))
    )
    merged, *w_outs = lax.optimization_barrier((merged, *w_outs))
    pieces = place.gather_z(merged)
    out_part = call(
        bind(out_kernel, place, heads),
        "out",
        [*pieces, *w_outs, row(b_out)],
        shape((nx, rows, cols)),
        scratch=[pltpu.VMEM((nx, rows, cols), F32), pltpu.VMEM((rows, share), BF16)],
    )
    projected = call(
        bind(add_out_kernel, place),
        "add_out",
        spread([out_part] * ny),
        shape((ny, nx, rows, cols)),
    )
    up_part, mid = call(
        bind(up_kernel, place),
        "norm_up",
        [
            *toks,
            *place.gather_z(projected),
            row(norm2_gain),
            row(norm2_bias),
            w_up,
            w_up_sibling,
            row(b_up),
        ],
        [shape((ny * rows, w_up.shape[1])), shape((rows, width), F32)],
        scratch=[
            pltpu.VMEM((ny * rows, width), F32),
            pltpu.VMEM((ny * rows, width), BF16),
            pltpu.VMEM((rows, width), F32),
        ],
    )
    up_parts = [up_part] + [place.move(up_part, dy=dy) for dy in range(1, ny)]
    piece = CORES * w_down.shape[1] // nx
    feeds = call(
        bind(down_kernel, place),
        "gelu_down",
        [*up_parts, w_down, w_down_sibling],
        [shape((ny * rows, piece))] * nx,
        scratch=[pltpu.VMEM((ny * rows, CORES * w_down.shape[1]), F32)],
    )
    feeds = [feeds[0]] + [place.move(feeds[dx], dx=dx) for dx in range(1, nx)]
    feed = call(bind(add_x_kernel, place), "add_x", feeds, shape((ny * rows, piece)))
    summed = call(
        bind(add_z_kernel, place),
        "add_z",
        place.gather_z(feed),
        [shape((rows, piece))] * ny,
        scratch=[pltpu.VMEM((ny * rows, piece), F32)],
    )
    hidden_out = call(
        bind(last_kernel, place),
        "last",
        [*spread(summed), mid, row(b_down)],
        shape(tokens.shape),
        scratch=[pltpu.VMEM((rows, width), F32)],
    )
    return (hidden_out, new_keys, new_values)


def solution(mesh):
    in_specs = (
        P("req", None, None),
        P("req"),
        P("req", "seq", None),
        P("req", "seq", None),
        P(),
        P(),
        P("req", "seq"),
        P("seq"),
        P("req", "seq"),
        P("seq"),
        P("req", "seq"),
        P("seq"),
        P("req", "seq"),
        P("seq"),
        P(),
        P(),
        P("req", "seq"),
        P("seq"),
        P("seq", "req"),
        P(),
    )
    out_specs = (P("req", None, None), P("req", "seq", None), P("req", "seq", None))
    return jax.shard_map(body, mesh=mesh, in_specs=in_specs, out_specs=out_specs, check_vma=False)
```

```python
import functools

import jax
import jax.numpy as jnp
from jax import lax
from jax.experimental import pallas as pl
from jax.experimental.pallas import tpu as pltpu
from jax.sharding import PartitionSpec as P

HEAD = 128
LANES = 128
CORES = 2
BF16 = jnp.bfloat16
F32 = jnp.float32
VMEM = pl.BlockSpec(memory_space=pltpu.VMEM)
SMEM = pl.BlockSpec(memory_space=pltpu.SMEM)
HBM = pl.BlockSpec(memory_space=pltpu.HBM)


class Place:
    def __init__(self, seqs, reqs):
        self.ny = reqs // CORES
        self.nx = self.ny
        self.nz = seqs // self.nx
        self.seqs = seqs

    def x(self):
        return lax.rem(lax.axis_index("seq"), self.nx)

    def y(self):
        return lax.div(lax.axis_index("req"), CORES)

    def core(self):
        return lax.rem(lax.axis_index("req"), CORES)

    def x_before(self, dx):
        return lax.rem(self.x() + self.nx - dx, self.nx)

    def x_after(self, dx):
        return lax.rem(self.x() + dx, self.nx)

    def y_before(self, dy):
        return lax.rem(self.y() + self.ny - dy, self.ny)

    def z_partner(self, dz):
        return lax.bitwise_xor(lax.div(lax.axis_index("seq"), self.nx), dz)

    def move(self, value, dx=0, dy=0, dc=0, dz=0):
        pairs = []
        for z in range(self.nz):
            for x in range(self.nx):
                for y in range(self.ny):
                    for c in range(CORES):
                        to_x, to_y, to_c = (x + dx) % self.nx, (y + dy) % self.ny, (c + dc) % CORES
                        to_z = z ^ dz
                        pairs.append(
                            (
                                ((z * self.nx + x) * self.ny + y) * CORES + c,
                                ((to_z * self.nx + to_x) * self.ny + to_y) * CORES + to_c,
                            )
                        )
        return lax.ppermute(value, ("seq", "req"), pairs)

    def transpose(self, value, k):
        n = self.nx
        pairs = []
        for z in range(self.nz):
            for x in range(n):
                for y in range(n):
                    for c in range(CORES):
                        pairs.append(
                            (
                                ((z * n + x) * n + y) * CORES + c,
                                ((z * n + y) * n + (x - k) % n) * CORES + c,
                            )
                        )
        return lax.ppermute(value, ("seq", "req"), pairs)

    def gather_z(self, value):
        return [value] + [self.move(value, dz=dz) for dz in range(1, self.nz)]


def layer_norm(values, gain, shift):
    center = values - jnp.mean(values, axis=-1, keepdims=True)
    spread = jnp.mean(center * center, axis=-1, keepdims=True)
    return center * lax.rsqrt(spread + 1e-05) * gain + shift


def dot(a, b):
    return jnp.dot(a, b, preferred_element_type=F32)


def across(a, b):
    return lax.dot_general(a, b, (((1,), (1,)), ((), ())), preferred_element_type=F32)


def at(index, size):
    return pl.ds(pl.multiple_of(index * size, size), size)


def call(kernel, name, ins, outs, in_specs=None, out_specs=None, scratch=(), moved=2**20, limit=20, aliases=None):
    single = not isinstance(outs, (list, tuple))
    specs = out_specs or (VMEM if single else [VMEM] * len(outs))
    return pl.pallas_call(
        kernel,
        name=name,
        out_shape=outs,
        in_specs=in_specs or [VMEM] * len(ins),
        out_specs=specs,
        scratch_shapes=list(scratch),
        input_output_aliases=aliases or {},
        cost_estimate=pl.CostEstimate(flops=0, bytes_accessed=moved, transcendentals=0),
        compiler_params=pltpu.CompilerParams(vmem_limit_bytes=int(limit * 1024 * 1024)),
    )(*ins)


def side_by_side(blocks, start, size, kind=F32):
    return jnp.concatenate(
        [blocks[x, :, start : start + size].astype(kind) for x in range(blocks.shape[0])], axis=1
    )


def two_halves(rows_by_k, own, sibling):
    depth = own.shape[0]
    req = lax.axis_index("req")
    other = req + 1 - 2 * lax.rem(req, CORES)
    return dot(rows_by_k[:, at(req, depth)], own[...]) + dot(
        rows_by_k[:, at(other, depth)], sibling[...]
    )


def flatten(block, flat, start):
    group, steps, _ = block.shape
    for i in range(group):
        flat[start + i * steps : start + (i + 1) * steps, :] = block[i].astype(F32)


def norm_kernel(tokens, scales, *refs):
    count = (len(refs) - 3) // 2
    weights, out, kept = refs[:count], refs[count], refs[count + 1 : 2 * count + 1]
    flat, sems = refs[-2:]
    copies = [
        pltpu.make_async_copy(source, target, sems.at[k])
        for k, (source, target) in enumerate(zip(weights, kept))
    ]
    for copy in copies:
        copy.start()
    width = out.shape[1]
    flatten(tokens, flat, 0)
    out[...] = layer_norm(flat[...], scales[:, :width], scales[:, width:]).astype(BF16)
    for copy in copies:
        copy.wait()


def qkv_kernel(place, *refs):
    ny = place.ny
    mine = refs[0]
    toks = refs[1:ny]
    scales, biases = refs[ny : ny + 2]
    weights = refs[ny + 2 : ny + 8]
    outs = refs[ny + 8 : 2 * ny + 8]
    flat, normed = refs[2 * ny + 8 :]
    rows, width = mine.shape
    normed[:rows, :] = mine[...]
    for j, tok in enumerate(toks):
        flatten(tok, flat, j * rows)
    normed[rows:, :] = layer_norm(flat[...], scales[:, :width], scales[:, width:]).astype(BF16)
    cols = weights[0].shape[1]
    for k in range(3):
        acc = two_halves(normed, weights[k], weights[3 + k])
        for j in range(ny):
            part = acc[j * rows : (j + 1) * rows]
            if j == 0:
                part = part + biases[:, k * cols : (k + 1) * cols]
            outs[(ny - j) % ny][:, k * cols : (k + 1) * cols] = part.astype(BF16)


def add_columns_kernel(place, *refs):
    out = refs[-1]
    for dx in range(place.nx):
        total = refs[dx * place.ny][...].astype(F32)
        for dy in range(1, place.ny):
            total = total + refs[dx * place.ny + dy][...].astype(F32)
        out[place.x_before(dx)] = total.astype(BF16)


def cache_kernel(keys_in, values_in, keys_out, values_out, keys, values, mark, in_sems, out_sems):
    group = keys.shape[0]
    arrays = ((keys_in, keys, keys_out), (values_in, values, values_out))
    coming = [
        pltpu.make_async_copy(source.at[i], here.at[i], in_sems.at[k, i])
        for i in range(group)
        for k, (source, here, _) in enumerate(arrays)
    ]
    going = [
        pltpu.make_async_copy(here.at[i], target.at[i], out_sems.at[k, i])
        for i in range(group)
        for k, (_, here, target) in enumerate(arrays)
    ]
    for copy in coming:
        copy.start()
    mark[...] = jnp.zeros_like(mark)
    for arrived, copy in zip(coming, going):
        arrived.wait()
        copy.start()
    for copy in going:
        copy.wait()


def split_three(value):
    first = value.astype(BF16).astype(F32)
    rest = value - first
    second = rest.astype(BF16).astype(F32)
    return first, second, rest - second


def turn(value, by):
    return pltpu.roll(value, by % LANES, 1)


def pairs_of(query):
    side = lax.rem(lax.div(lax.broadcasted_iota(jnp.int32, query.shape, 1), HEAD), 2)
    return jnp.concatenate(
        [jnp.where(side == 0, query, 0.0), jnp.where(side == 1, query, 0.0)], axis=0
    ).astype(BF16)


def attention_kernel(place, heads, steps, *refs):
    nx, nz = place.nx, place.nz
    gathered = refs[:nz]
    lengths, keys, values = refs[nz : nz + 3]
    keys_out, values_out = refs[nz + 5 : nz + 7]
    messages = refs[nz + 7 : nz + 7 + nx]
    qs, ks, vs, scores, part, stats, k_rows, v_rows, sems = refs[nz + 7 + nx :]
    group, slots, width = keys.shape
    cols = width // place.seqs
    seq = lax.axis_index("seq")
    for dz in range(nz):
        span = at(place.z_partner(dz), nx * cols)
        for k, target in enumerate((qs, ks, vs)):
            target[:, span] = side_by_side(gathered[dz], k * cols, cols, target.dtype)

    window = k_rows.shape[1]

    def place_of(i):
        base = lengths[i] - seq * slots
        start = jnp.clip(lax.div(jnp.maximum(base, 0), 16) * 16, 0, slots - window)
        return base, pl.multiple_of(start, 16)

    def copies(i):
        _, start = place_of(i)
        return [
            pltpu.make_async_copy(
                rows.at[i], target.at[i, pl.ds(start, window), :], sems.at[k, i]
            )
            for k, (rows, target) in enumerate(((k_rows, keys_out), (v_rows, values_out)))
        ]

    for i in range(group):
        base, start = place_of(i)

        @pl.when((base > -steps) & (base < slots))
        def _():
            slot = start + lax.broadcasted_iota(jnp.int32, (window, width), 0)
            for source, fresh, rows in ((keys, ks, k_rows), (values, vs, v_rows)):
                block = source[i, pl.ds(start, window), :].astype(F32)
                first = i * steps // 16 * 16
                some = fresh[first : first + 16, :].astype(F32)
                for t in range(steps):
                    row_at = i * steps + t - first
                    at_row = some[row_at : row_at + 1, :]
                    block = jnp.where(slot == base + t, at_row, block)
                rows[i] = block.astype(BF16)
            for copy in copies(i):
                copy.start()

    pack = max(1, min(group, 256 // slots))
    rows = pack * steps
    tile = 2 * HEAD
    left = lax.broadcasted_iota(jnp.int32, (rows, tile), 1) < HEAD
    many, cached = heads * rows, pack * slots
    row = lax.broadcasted_iota(jnp.int32, (many, cached + LANES), 0)
    column = lax.broadcasted_iota(jnp.int32, (many, cached + LANES), 1)
    owner = lax.div(lax.rem(row, rows), steps)
    position = lax.rem(column, slots)
    old = (column < cached) & (owner == lax.div(column, slots))
    new = column - cached
    later = lax.rem(new, steps)
    fresh = (
        (new >= 0)
        & (new < rows)
        & (lax.div(new, steps) == owner)
        & (later <= lax.rem(row, steps))
    )
    lane = lax.broadcasted_iota(jnp.int32, (rows, LANES), 1)
    blank = jnp.zeros((LANES - rows, width), BF16)
    for g in range(group // pack):
        mine = slice(g * rows, (g + 1) * rows)
        these = slice(g * pack, (g + 1) * pack)
        pair = pairs_of(qs[mine, :])
        key = keys[these].reshape(cached, width)
        value = values[these].reshape(cached, width)
        new_key = jnp.concatenate([ks[mine, :], blank], axis=0)
        new_value = jnp.concatenate([vs[mine, :], blank], axis=0)
        for j in range(heads // 2):
            span = slice(j * tile, (j + 1) * tile)
            these_rows = slice(j * 2 * rows, (j + 1) * 2 * rows)
            scores[these_rows, :cached] = across(pair[:, span], key[:, span])
            scores[these_rows, cached:] = across(pair[:, span], new_key[:, span])
        base = jnp.zeros_like(owner)
        for k in range(pack):
            base = jnp.where(owner == k, lengths[g * pack + k] - seq * slots, base)
        at_new = base + later
        valid = (old & (position < base)) | (fresh & (at_new >= 0) & (at_new < slots))
        masked = jnp.where(valid, scores[...] * HEAD ** (-0.5), -1e30)
        peak = jnp.max(masked, axis=-1, keepdims=True)
        expo = jnp.where(valid, jnp.exp(masked - peak), 0.0)
        total = jnp.sum(expo, axis=-1, keepdims=True)
        probs = expo.astype(BF16)
        for j in range(heads // 2):
            span = slice(j * tile, (j + 1) * tile)
            these_rows = slice(j * 2 * rows, (j + 1) * 2 * rows)
            mixed = dot(probs[these_rows, :cached], value[:, span])
            mixed = mixed + dot(probs[these_rows, cached:], new_value[:, span])
            part[mine, span] = jnp.where(left, mixed[:rows], mixed[rows:])
        line = jnp.zeros((rows, LANES), F32)
        for k, piece in enumerate(split_three(peak) + split_three(total)[:2]):
            for h in range(heads):
                line = jnp.where(lane == k * heads + h, piece[h * rows : (h + 1) * rows], line)
        stats[mine, :] = line
    share = width // nx
    for dx in range(nx):
        to = place.x_after(dx)
        messages[dx][:, :share] = part[:, at(to, share)].astype(BF16)
        messages[dx][:, share:] = pltpu.roll(
            stats[...], lax.rem(LANES - to * (heads // nx), LANES), 1
        ).astype(BF16)
    for i in range(group):
        base, _ = place_of(i)

        @pl.when((base > -steps) & (base < slots))
        def _():
            for copy in copies(i):
                copy.wait()


def expand(factor, count):
    rows = factor.shape[0]
    return jnp.concatenate(
        [jnp.broadcast_to(factor[:, h : h + 1], (rows, HEAD)) for h in range(count)], axis=1
    )


def merge(messages, heads, share):
    peaks, totals = [], []
    for message in messages:
        stats = message[:, share:].astype(F32)
        peaks.append(stats + turn(stats, -heads) + turn(stats, -2 * heads))
        totals.append(turn(stats, -3 * heads) + turn(stats, -4 * heads))
    peak = functools.reduce(jnp.maximum, peaks)
    scales = [jnp.exp(p - peak) for p in peaks]
    total = sum(t * s for t, s in zip(totals, scales))
    return peak, total, scales


def merge_x_kernel(place, heads, *refs):
    share = refs[0].shape[1] - LANES
    count = share // HEAD
    out = refs[-1]
    messages = [r[...] for r in refs[:-1]]
    peak, total, scales = merge(messages, heads, share)
    out[:, :share] = sum(
        m[:, :share].astype(F32) * expand(s, count) for m, s in zip(messages, scales)
    ).astype(BF16)
    lane = lax.broadcasted_iota(jnp.int32, peak.shape, 1)
    tile = jnp.zeros_like(peak)
    for k, piece in enumerate(split_three(peak) + split_three(total)[:2]):
        tile = tile + turn(jnp.where(lane < count, piece, 0.0), k * heads)
    out[:, share:] = tile.astype(BF16)


def out_kernel(place, heads, *refs):
    nx, nz = place.nx, place.nz
    messages = [r[...] for r in refs[:nz]]
    weights = refs[nz : nz + 2 * nx]
    bias, out, total, attn = refs[nz + 2 * nx :]
    share = attn.shape[1]
    _, whole, scales = merge(messages, heads, share)
    attn[...] = sum(
        m[:, :share].astype(F32) * expand(s / whole, share // HEAD)
        for m, s in zip(messages, scales)
    ).astype(BF16)
    depth = weights[0].shape[0]
    core = place.core()
    for k in range(nx):
        block = lax.rem(place.y() + k, nx)
        total[block] = dot(attn[:, at(core, depth)], weights[2 * k][...]) + dot(
            attn[:, at(1 - core, depth)], weights[2 * k + 1][...]
        )
    total[place.x()] = total[place.x()] + bias[...]
    out[...] = total[...].astype(BF16)


def add_out_kernel(place, *refs):
    out = refs[-1]
    for dy in range(place.ny):
        total = refs[dy][...].astype(F32)
        for dx in range(1, place.nx):
            total = total + refs[dx * place.ny + dy][...].astype(F32)
        out[place.y_before(dy)] = total.astype(BF16)


def up_kernel(place, *refs):
    ny, nz = place.ny, place.nz
    tokens, flats = refs[:2]
    gathered = refs[2 : 2 + nz]
    gain, shift, own, sibling, bias, out, mid_out, proj, normed, flat = refs[2 + nz :]
    group, steps, _ = tokens.shape
    rows = group * steps
    cols = gathered[0].shape[3]
    for dz in range(nz):
        span = at(place.z_partner(dz), place.nx * cols)
        for y in range(ny):
            proj[y * rows : (y + 1) * rows, span] = side_by_side(gathered[dz].at[y], 0, cols)
    for j in range(ny):
        here = at(place.y_before(j), rows)
        if j == 0:
            flatten(tokens, flat, 0)
        mine = flat[...] if j == 0 else flats[(j - 1) * rows : j * rows, :]
        mid = mine + proj[here, :]
        if j == 0:
            mid_out[...] = mid
        normed[here, :] = layer_norm(mid, gain[...], shift[...]).astype(BF16)
    first = (place.y() == 0).astype(F32)
    out[...] = (two_halves(normed, own, sibling) + bias[...] * first).astype(BF16)


def down_kernel(place, *refs):
    nx, ny = place.nx, place.ny
    parts = refs[:ny]
    own, sibling = refs[ny : ny + 2]
    outs = refs[ny + 2 : ny + 2 + nx]
    feed = refs[-1]
    total = sum(p[...].astype(F32) for p in parts)
    hidden = (0.5 * total * (1.0 + lax.erf(total * 0.5**0.5))).astype(BF16)
    ncols = own.shape[1]
    feed[:, at(place.core(), ncols)] = dot(hidden, own[...])
    feed[:, at(1 - place.core(), ncols)] = dot(hidden, sibling[...])
    width = outs[0].shape[1]
    for dx in range(nx):
        outs[dx][...] = feed[:, at(place.x_after(dx), width)].astype(BF16)


def add_x_kernel(place, *refs):
    refs[-1][...] = sum(r[...].astype(F32) for r in refs[:-1]).astype(BF16)


def add_z_kernel(place, *refs):
    outs, total = refs[place.nz : -1], refs[-1]
    total[...] = sum(r[...].astype(F32) for r in refs[: place.nz])
    rows = outs[0].shape[0]
    for dy in range(place.ny):
        outs[dy][...] = total[at(lax.rem(place.y() + dy, place.ny), rows), :].astype(BF16)


def last_kernel(place, *refs):
    nx, ny = place.nx, place.ny
    parts = refs[: nx * ny]
    mid, bias, out, full = refs[nx * ny :]
    group, steps, _ = out.shape
    width = parts[0].shape[1]
    for dx in range(nx):
        for dy in range(ny):
            block = place.y_before(dy) * nx + place.x_before(dx)
            full[:, at(block, width)] = parts[dx * ny + dy][...].astype(F32)
    result = mid[...] + full[...] + bias[...]
    for i in range(group):
        out[i] = result[i * steps : (i + 1) * steps].astype(BF16)


def shape(sizes, kind=BF16):
    return jax.ShapeDtypeStruct(tuple(sizes), kind)


def body(
    tokens,
    lengths,
    cache_keys,
    cache_values,
    norm1_gain,
    norm1_bias,
    w_query,
    b_query,
    w_key,
    b_key,
    w_value,
    b_value,
    w_out,
    b_out,
    norm2_gain,
    norm2_bias,
    w_up,
    b_up,
    w_down,
    b_down,
):
    place = Place(lax.axis_size("seq"), lax.axis_size("req"))
    nx, ny = place.nx, place.ny
    group, steps, width = tokens.shape
    slots = cache_keys.shape[1]
    rows = group * steps
    heads = width // HEAD
    share = width // nx
    bind = functools.partial

    def row(vector):
        return vector.reshape(1, -1)

    def spread(by_dy):
        return [
            by_dy[dy] if dx == 0 and dy == 0 else place.move(by_dy[dy], dx, dy)
            for dx in range(nx)
            for dy in range(ny)
        ]

    toks = [tokens] + [place.move(tokens, dy=dy) for dy in range(1, ny)]
    cols = w_query.shape[1]
    own = [w_query, w_key, w_value]
    siblings = [place.move(weight, dc=1) for weight in own]
    scales = row(jnp.concatenate([norm1_gain, norm1_bias]))
    biases = row(jnp.concatenate([b_query, b_key, b_value]))
    normed, *own = call(
        norm_kernel,
        "norm",
        [tokens, scales, *own],
        [shape((rows, width))] + [shape(w.shape) for w in own],
        in_specs=[VMEM] * 2 + [HBM] * 3,
        scratch=[pltpu.VMEM((rows, width), F32), pltpu.SemaphoreType.DMA((3,))],
        limit=52.75,
    )
    *parts, flats = call(
        bind(qkv_kernel, place),
        "norm_qkv",
        [normed, *toks[1:], scales, biases, *own, *siblings],
        [shape((rows, 3 * cols))] * ny + [shape(((ny - 1) * rows, width), F32)],
        scratch=[pltpu.VMEM((ny * rows, width), BF16)],
    )
    *parts, tied_up, tied_down = lax.optimization_barrier((*parts, w_up, w_down))
    w_up_sibling = place.move(tied_up, dc=1)
    w_down_sibling = place.move(tied_down, dc=1)
    parts, tied_keys, tied_values = lax.optimization_barrier((parts, cache_keys, cache_values))
    new_keys, new_values, keys, values, mark = call(
        cache_kernel,
        "caches",
        [tied_keys, tied_values],
        [shape(cache_keys.shape)] * 4 + [shape((8, LANES), F32)],
        in_specs=[HBM, HBM],
        out_specs=[HBM, HBM, VMEM, VMEM, VMEM],
        scratch=[pltpu.SemaphoreType.DMA((2, group)), pltpu.SemaphoreType.DMA((2, group))],
        moved=16 * 1024 * 1024,
        limit=46,
    )
    qkv = call(
        bind(add_columns_kernel, place),
        "add_qkv",
        [*spread(parts), mark],
        shape((nx, rows, 3 * cols)),
    )
    qkv, w_up_sibling, w_down_sibling, tied = lax.optimization_barrier(
        (qkv, w_up_sibling, w_down_sibling, w_out)
    )
    pieces = place.gather_z(qkv)
    blocks = [place.transpose(tied, k) for k in range(nx)]
    pack = max(1, min(group, 256 // slots))
    window = min(32, slots)
    new_keys, new_values, *messages = call(
        bind(attention_kernel, place, heads, steps),
        "attention",
        [*pieces, lengths, keys, values, new_keys, new_values],
        [shape(cache_keys.shape)] * 2 + [shape((rows, share + LANES))] * nx,
        in_specs=[VMEM] * place.nz + [SMEM, VMEM, VMEM, HBM, HBM],
        out_specs=[HBM, HBM] + [VMEM] * nx,
        scratch=[
            pltpu.VMEM((rows, width), F32),
            pltpu.VMEM((rows, width), BF16),
            pltpu.VMEM((rows, width), BF16),
            pltpu.VMEM((heads * pack * steps, pack * slots + LANES), F32),
            pltpu.VMEM((rows, width), F32),
            pltpu.VMEM((rows, LANES), F32),
            pltpu.VMEM((group, window, width), BF16),
            pltpu.VMEM((group, window, width), BF16),
            pltpu.SemaphoreType.DMA((2, group)),
        ],
        aliases={place.nz + 3: 0, place.nz + 4: 1},
    )
    messages, blocks = lax.optimization_barrier((messages, blocks))
    w_outs = []
    for block in blocks:
        w_outs += [block, place.move(block, dc=1)]
    messages = [messages[0]] + [place.move(messages[dx], dx=dx) for dx in range(1, nx)]
    merged = call(
        bind(merge_x_kernel, place, heads), "merge_x", messages, shape((rows, share + LANES))
    )
    merged, *w_outs = lax.optimization_barrier((merged, *w_outs))
    pieces = place.gather_z(merged)
    out_part = call(
        bind(out_kernel, place, heads),
        "out",
        [*pieces, *w_outs, row(b_out)],
        shape((nx, rows, cols)),
        scratch=[pltpu.VMEM((nx, rows, cols), F32), pltpu.VMEM((rows, share), BF16)],
    )
    projected = call(
        bind(add_out_kernel, place),
        "add_out",
        spread([out_part] * ny),
        shape((ny, nx, rows, cols)),
    )
    up_part, mid = call(
        bind(up_kernel, place),
        "norm_up",
        [
            tokens,
            flats,
            *place.gather_z(projected),
            row(norm2_gain),
            row(norm2_bias),
            w_up,
            w_up_sibling,
            row(b_up),
        ],
        [shape((ny * rows, w_up.shape[1])), shape((rows, width), F32)],
        scratch=[
            pltpu.VMEM((ny * rows, width), F32),
            pltpu.VMEM((ny * rows, width), BF16),
            pltpu.VMEM((rows, width), F32),
        ],
    )
    up_parts = [up_part] + [place.move(up_part, dy=dy) for dy in range(1, ny)]
    piece = CORES * w_down.shape[1] // nx
    feeds = call(
        bind(down_kernel, place),
        "gelu_down",
        [*up_parts, w_down, w_down_sibling],
        [shape((ny * rows, piece))] * nx,
        scratch=[pltpu.VMEM((ny * rows, CORES * w_down.shape[1]), F32)],
    )
    feeds = [feeds[0]] + [place.move(feeds[dx], dx=dx) for dx in range(1, nx)]
    feed = call(bind(add_x_kernel, place), "add_x", feeds, shape((ny * rows, piece)))
    summed = call(
        bind(add_z_kernel, place),
        "add_z",
        place.gather_z(feed),
        [shape((rows, piece))] * ny,
        scratch=[pltpu.VMEM((ny * rows, piece), F32)],
    )
    hidden_out = call(
        bind(last_kernel, place),
        "last",
        [*spread(summed), mid, row(b_down)],
        shape(tokens.shape),
        scratch=[pltpu.VMEM((rows, width), F32)],
    )
    return (hidden_out, new_keys, new_values)


def solution(mesh):
    in_specs = (
        P("req", None, None),
        P("req"),
        P("req", "seq", None),
        P("req", "seq", None),
        P(),
        P(),
        P("req", "seq"),
        P("seq"),
        P("req", "seq"),
        P("seq"),
        P("req", "seq"),
        P("seq"),
        P("req", "seq"),
        P("seq"),
        P(),
        P(),
        P("req", "seq"),
        P("seq"),
        P("seq", "req"),
        P(),
    )
    out_specs = (P("req", None, None), P("req", "seq", None), P("req", "seq", None))
    return jax.shard_map(body, mesh=mesh, in_specs=in_specs, out_specs=out_specs, check_vma=False)
```

```python
import functools

import jax
import jax.numpy as jnp
from jax import lax
from jax.experimental import pallas as pl
from jax.experimental.pallas import tpu as pltpu
from jax.sharding import PartitionSpec as P

HEAD = 128
LANES = 128
CORES = 2
BF16 = jnp.bfloat16
F32 = jnp.float32
VMEM = pl.BlockSpec(memory_space=pltpu.VMEM)
SMEM = pl.BlockSpec(memory_space=pltpu.SMEM)
HBM = pl.BlockSpec(memory_space=pltpu.HBM)


class Place:
    def __init__(self, seqs, reqs):
        self.ny = reqs // CORES
        self.nx = self.ny
        self.nz = seqs // self.nx
        self.seqs = seqs

    def x(self):
        return lax.rem(lax.axis_index("seq"), self.nx)

    def y(self):
        return lax.div(lax.axis_index("req"), CORES)

    def core(self):
        return lax.rem(lax.axis_index("req"), CORES)

    def x_before(self, dx):
        return lax.rem(self.x() + self.nx - dx, self.nx)

    def x_after(self, dx):
        return lax.rem(self.x() + dx, self.nx)

    def y_before(self, dy):
        return lax.rem(self.y() + self.ny - dy, self.ny)

    def z_partner(self, dz):
        return lax.bitwise_xor(lax.div(lax.axis_index("seq"), self.nx), dz)

    def move(self, value, dx=0, dy=0, dc=0, dz=0):
        pairs = []
        for z in range(self.nz):
            for x in range(self.nx):
                for y in range(self.ny):
                    for c in range(CORES):
                        to_x, to_y, to_c = (x + dx) % self.nx, (y + dy) % self.ny, (c + dc) % CORES
                        to_z = z ^ dz
                        pairs.append(
                            (
                                ((z * self.nx + x) * self.ny + y) * CORES + c,
                                ((to_z * self.nx + to_x) * self.ny + to_y) * CORES + to_c,
                            )
                        )
        return lax.ppermute(value, ("seq", "req"), pairs)

    def transpose(self, value, k):
        n = self.nx
        pairs = []
        for z in range(self.nz):
            for x in range(n):
                for y in range(n):
                    for c in range(CORES):
                        pairs.append(
                            (
                                ((z * n + x) * n + y) * CORES + c,
                                ((z * n + y) * n + (x - k) % n) * CORES + c,
                            )
                        )
        return lax.ppermute(value, ("seq", "req"), pairs)

    def gather_z(self, value):
        return [value] + [self.move(value, dz=dz) for dz in range(1, self.nz)]


def layer_norm(values, gain, shift):
    center = values - jnp.mean(values, axis=-1, keepdims=True)
    spread = jnp.mean(center * center, axis=-1, keepdims=True)
    return center * lax.rsqrt(spread + 1e-05) * gain + shift


def dot(a, b):
    return jnp.dot(a, b, preferred_element_type=F32)


def across(a, b):
    return lax.dot_general(a, b, (((1,), (1,)), ((), ())), preferred_element_type=F32)


def at(index, size):
    return pl.ds(pl.multiple_of(index * size, size), size)


def call(kernel, name, ins, outs, in_specs=None, out_specs=None, scratch=(), moved=2**20, limit=20, aliases=None):
    single = not isinstance(outs, (list, tuple))
    specs = out_specs or (VMEM if single else [VMEM] * len(outs))
    return pl.pallas_call(
        kernel,
        name=name,
        out_shape=outs,
        in_specs=in_specs or [VMEM] * len(ins),
        out_specs=specs,
        scratch_shapes=list(scratch),
        input_output_aliases=aliases or {},
        cost_estimate=pl.CostEstimate(flops=0, bytes_accessed=moved, transcendentals=0),
        compiler_params=pltpu.CompilerParams(vmem_limit_bytes=int(limit * 1024 * 1024)),
    )(*ins)


def side_by_side(blocks, start, size):
    return jnp.concatenate(
        [blocks[x, :, start : start + size].astype(F32) for x in range(blocks.shape[0])], axis=1
    )


def two_halves(rows_by_k, own, sibling):
    depth = own.shape[0]
    req = lax.axis_index("req")
    other = req + 1 - 2 * lax.rem(req, CORES)
    return dot(rows_by_k[:, at(req, depth)], own[...]) + dot(
        rows_by_k[:, at(other, depth)], sibling[...]
    )


def flatten(block, flat, start):
    group, steps, _ = block.shape
    for i in range(group):
        flat[start + i * steps : start + (i + 1) * steps, :] = block[i].astype(F32)


def norm_kernel(tokens, scales, *refs):
    count = (len(refs) - 3) // 2
    weights, out, kept = refs[:count], refs[count], refs[count + 1 : 2 * count + 1]
    flat, sems = refs[-2:]
    copies = [
        pltpu.make_async_copy(source, target, sems.at[k])
        for k, (source, target) in enumerate(zip(weights, kept))
    ]
    for copy in copies:
        copy.start()
    width = out.shape[1]
    flatten(tokens, flat, 0)
    out[...] = layer_norm(flat[...], scales[:, :width], scales[:, width:]).astype(BF16)
    for copy in copies:
        copy.wait()


def qkv_kernel(place, *refs):
    ny = place.ny
    mine = refs[0]
    toks = refs[1:ny]
    scales, biases = refs[ny : ny + 2]
    weights = refs[ny + 2 : ny + 8]
    outs = refs[ny + 8 : 2 * ny + 8]
    flat, normed = refs[2 * ny + 8 :]
    rows, width = mine.shape
    normed[:rows, :] = mine[...]
    for j, tok in enumerate(toks):
        flatten(tok, flat, j * rows)
    normed[rows:, :] = layer_norm(flat[...], scales[:, :width], scales[:, width:]).astype(BF16)
    cols = weights[0].shape[1]
    for k in range(3):
        acc = two_halves(normed, weights[k], weights[3 + k])
        for j in range(ny):
            part = acc[j * rows : (j + 1) * rows]
            if j == 0:
                part = part + biases[:, k * cols : (k + 1) * cols]
            outs[(ny - j) % ny][:, k * cols : (k + 1) * cols] = part.astype(BF16)


def add_columns_kernel(place, *refs):
    out = refs[-1]
    for dx in range(place.nx):
        total = refs[dx * place.ny][...].astype(F32)
        for dy in range(1, place.ny):
            total = total + refs[dx * place.ny + dy][...].astype(F32)
        out[place.x_before(dx)] = total.astype(BF16)


def cache_kernel(keys_in, values_in, keys_out, values_out, keys, values, mark, in_sems, out_sems):
    group = keys.shape[0]
    arrays = ((keys_in, keys, keys_out), (values_in, values, values_out))
    coming = [
        pltpu.make_async_copy(source.at[i], here.at[i], in_sems.at[k, i])
        for i in range(group)
        for k, (source, here, _) in enumerate(arrays)
    ]
    going = [
        pltpu.make_async_copy(here.at[i], target.at[i], out_sems.at[k, i])
        for i in range(group)
        for k, (_, here, target) in enumerate(arrays)
    ]
    for copy in coming:
        copy.start()
    mark[...] = jnp.zeros_like(mark)
    for arrived, copy in zip(coming, going):
        arrived.wait()
        copy.start()
    for copy in going:
        copy.wait()


def split_three(value):
    first = value.astype(BF16).astype(F32)
    rest = value - first
    second = rest.astype(BF16).astype(F32)
    return first, second, rest - second


def turn(value, by):
    return pltpu.roll(value, by % LANES, 1)


def pairs_of(query):
    side = lax.rem(lax.div(lax.broadcasted_iota(jnp.int32, query.shape, 1), HEAD), 2)
    return jnp.concatenate(
        [jnp.where(side == 0, query, 0.0), jnp.where(side == 1, query, 0.0)], axis=0
    ).astype(BF16)


def attention_kernel(place, heads, steps, *refs):
    nx, nz = place.nx, place.nz
    gathered = refs[:nz]
    lengths, keys, values = refs[nz : nz + 3]
    keys_out, values_out = refs[nz + 5 : nz + 7]
    messages = refs[nz + 7 : nz + 7 + nx]
    qs, ks, vs, scores, part, stats, k_rows, v_rows, sems = refs[nz + 7 + nx :]
    group, slots, width = keys.shape
    cols = width // place.seqs
    seq = lax.axis_index("seq")
    for dz in range(nz):
        span = at(place.z_partner(dz), nx * cols)
        for k, target in enumerate((qs, ks, vs)):
            target[:, span] = side_by_side(gathered[dz], k * cols, cols)

    window = k_rows.shape[1]

    def place_of(i):
        base = lengths[i] - seq * slots
        start = jnp.clip(lax.div(jnp.maximum(base, 0), 16) * 16, 0, slots - window)
        return base, pl.multiple_of(start, 16)

    def copies(i):
        _, start = place_of(i)
        return [
            pltpu.make_async_copy(
                rows.at[i], target.at[i, pl.ds(start, window), :], sems.at[k, i]
            )
            for k, (rows, target) in enumerate(((k_rows, keys_out), (v_rows, values_out)))
        ]

    for i in range(group):
        base, start = place_of(i)

        @pl.when((base > -steps) & (base < slots))
        def _():
            slot = start + lax.broadcasted_iota(jnp.int32, (window, width), 0)
            for source, fresh, rows in ((keys, ks, k_rows), (values, vs, v_rows)):
                block = source[i, pl.ds(start, window), :].astype(F32)
                for t in range(steps):
                    at_row = fresh[i * steps + t : i * steps + t + 1, :]
                    block = jnp.where(slot == base + t, at_row, block)
                rows[i] = block.astype(BF16)
            for copy in copies(i):
                copy.start()

    pack = max(1, min(group, 256 // slots))
    rows = pack * steps
    tile = 2 * HEAD
    left = lax.broadcasted_iota(jnp.int32, (rows, tile), 1) < HEAD
    many, cached = heads * rows, pack * slots
    row = lax.broadcasted_iota(jnp.int32, (many, cached + LANES), 0)
    column = lax.broadcasted_iota(jnp.int32, (many, cached + LANES), 1)
    owner = lax.div(lax.rem(row, rows), steps)
    position = lax.rem(column, slots)
    old = (column < cached) & (owner == lax.div(column, slots))
    new = column - cached
    later = lax.rem(new, steps)
    fresh = (
        (new >= 0)
        & (new < rows)
        & (lax.div(new, steps) == owner)
        & (later <= lax.rem(row, steps))
    )
    lane = lax.broadcasted_iota(jnp.int32, (rows, LANES), 1)
    blank = jnp.zeros((LANES - rows, width), BF16)
    for g in range(group // pack):
        mine = slice(g * rows, (g + 1) * rows)
        these = slice(g * pack, (g + 1) * pack)
        pair = pairs_of(qs[mine, :])
        key = keys[these].reshape(cached, width)
        value = values[these].reshape(cached, width)
        new_key = jnp.concatenate([ks[mine, :].astype(BF16), blank], axis=0)
        new_value = jnp.concatenate([vs[mine, :].astype(BF16), blank], axis=0)
        for j in range(heads // 2):
            span = slice(j * tile, (j + 1) * tile)
            these_rows = slice(j * 2 * rows, (j + 1) * 2 * rows)
            scores[these_rows, :cached] = across(pair[:, span], key[:, span])
            scores[these_rows, cached:] = across(pair[:, span], new_key[:, span])
        base = jnp.zeros_like(owner)
        for k in range(pack):
            base = jnp.where(owner == k, lengths[g * pack + k] - seq * slots, base)
        at_new = base + later
        valid = (old & (position < base)) | (fresh & (at_new >= 0) & (at_new < slots))
        masked = jnp.where(valid, scores[...] * HEAD ** (-0.5), -1e30)
        peak = jnp.max(masked, axis=-1, keepdims=True)
        expo = jnp.where(valid, jnp.exp(masked - peak), 0.0)
        total = jnp.sum(expo, axis=-1, keepdims=True)
        probs = expo.astype(BF16)
        for j in range(heads // 2):
            span = slice(j * tile, (j + 1) * tile)
            these_rows = slice(j * 2 * rows, (j + 1) * 2 * rows)
            mixed = dot(probs[these_rows, :cached], value[:, span])
            mixed = mixed + dot(probs[these_rows, cached:], new_value[:, span])
            part[mine, span] = jnp.where(left, mixed[:rows], mixed[rows:])
        line = jnp.zeros((rows, LANES), F32)
        for k, piece in enumerate(split_three(peak) + split_three(total)[:2]):
            for h in range(heads):
                line = jnp.where(lane == k * heads + h, piece[h * rows : (h + 1) * rows], line)
        stats[mine, :] = line
    share = width // nx
    for dx in range(nx):
        to = place.x_after(dx)
        messages[dx][:, :share] = part[:, at(to, share)].astype(BF16)
        messages[dx][:, share:] = pltpu.roll(
            stats[...], lax.rem(LANES - to * (heads // nx), LANES), 1
        ).astype(BF16)
    for i in range(group):
        base, _ = place_of(i)

        @pl.when((base > -steps) & (base < slots))
        def _():
            for copy in copies(i):
                copy.wait()


def expand(factor, count):
    rows = factor.shape[0]
    return jnp.concatenate(
        [jnp.broadcast_to(factor[:, h : h + 1], (rows, HEAD)) for h in range(count)], axis=1
    )


def merge(messages, heads, share):
    peaks, totals = [], []
    for message in messages:
        stats = message[:, share:].astype(F32)
        peaks.append(stats + turn(stats, -heads) + turn(stats, -2 * heads))
        totals.append(turn(stats, -3 * heads) + turn(stats, -4 * heads))
    peak = functools.reduce(jnp.maximum, peaks)
    scales = [jnp.exp(p - peak) for p in peaks]
    total = sum(t * s for t, s in zip(totals, scales))
    return peak, total, scales


def merge_x_kernel(place, heads, *refs):
    share = refs[0].shape[1] - LANES
    count = share // HEAD
    out = refs[-1]
    messages = [r[...] for r in refs[:-1]]
    peak, total, scales = merge(messages, heads, share)
    out[:, :share] = sum(
        m[:, :share].astype(F32) * expand(s, count) for m, s in zip(messages, scales)
    ).astype(BF16)
    lane = lax.broadcasted_iota(jnp.int32, peak.shape, 1)
    tile = jnp.zeros_like(peak)
    for k, piece in enumerate(split_three(peak) + split_three(total)[:2]):
        tile = tile + turn(jnp.where(lane < count, piece, 0.0), k * heads)
    out[:, share:] = tile.astype(BF16)


def out_kernel(place, heads, *refs):
    nx, nz = place.nx, place.nz
    messages = [r[...] for r in refs[:nz]]
    weights = refs[nz : nz + 2 * nx]
    bias, out, total, attn = refs[nz + 2 * nx :]
    share = attn.shape[1]
    _, whole, scales = merge(messages, heads, share)
    attn[...] = sum(
        m[:, :share].astype(F32) * expand(s / whole, share // HEAD)
        for m, s in zip(messages, scales)
    ).astype(BF16)
    depth = weights[0].shape[0]
    core = place.core()
    for k in range(nx):
        block = lax.rem(place.y() + nx - 1 - k, nx)
        total[block] = dot(attn[:, at(core, depth)], weights[2 * k][...]) + dot(
            attn[:, at(1 - core, depth)], weights[2 * k + 1][...]
        )
    total[place.x()] = total[place.x()] + bias[...]
    out[...] = total[...].astype(BF16)


def add_out_kernel(place, *refs):
    out = refs[-1]
    for dy in range(place.ny):
        total = refs[dy][...].astype(F32)
        for dx in range(1, place.nx):
            total = total + refs[dx * place.ny + dy][...].astype(F32)
        out[place.y_before(dy)] = total.astype(BF16)


def up_kernel(place, *refs):
    ny, nz = place.ny, place.nz
    toks = refs[:ny]
    gathered = refs[ny : ny + nz]
    gain, shift, own, sibling, bias, out, mid_out, proj, normed, flat = refs[ny + nz :]
    group, steps, _ = toks[0].shape
    rows = group * steps
    cols = gathered[0].shape[3]
    for dz in range(nz):
        span = at(place.z_partner(dz), place.nx * cols)
        for y in range(ny):
            proj[y * rows : (y + 1) * rows, span] = side_by_side(gathered[dz].at[y], 0, cols)
    for j in range(ny):
        here = at(place.y_before(j), rows)
        flatten(toks[j], flat, 0)
        mid = flat[...] + proj[here, :]
        if j == 0:
            mid_out[...] = mid
        normed[here, :] = layer_norm(mid, gain[...], shift[...]).astype(BF16)
    first = (place.y() == 0).astype(F32)
    out[...] = (two_halves(normed, own, sibling) + bias[...] * first).astype(BF16)


def down_kernel(place, *refs):
    nx, ny = place.nx, place.ny
    parts = refs[:ny]
    own, sibling = refs[ny : ny + 2]
    outs = refs[ny + 2 : ny + 2 + nx]
    feed = refs[-1]
    total = sum(p[...].astype(F32) for p in parts)
    hidden = (0.5 * total * (1.0 + lax.erf(total * 0.5**0.5))).astype(BF16)
    ncols = own.shape[1]
    feed[:, at(place.core(), ncols)] = dot(hidden, own[...])
    feed[:, at(1 - place.core(), ncols)] = dot(hidden, sibling[...])
    width = outs[0].shape[1]
    for dx in range(nx):
        outs[dx][...] = feed[:, at(place.x_after(dx), width)].astype(BF16)


def add_x_kernel(place, *refs):
    refs[-1][...] = sum(r[...].astype(F32) for r in refs[:-1]).astype(BF16)


def add_z_kernel(place, *refs):
    outs, total = refs[place.nz : -1], refs[-1]
    total[...] = sum(r[...].astype(F32) for r in refs[: place.nz])
    rows = outs[0].shape[0]
    for dy in range(place.ny):
        outs[dy][...] = total[at(lax.rem(place.y() + dy, place.ny), rows), :].astype(BF16)


def last_kernel(place, *refs):
    nx, ny = place.nx, place.ny
    parts = refs[: nx * ny]
    mid, bias, out, full = refs[nx * ny :]
    group, steps, _ = out.shape
    width = parts[0].shape[1]
    for dx in range(nx):
        for dy in range(ny):
            block = place.y_before(dy) * nx + place.x_before(dx)
            full[:, at(block, width)] = parts[dx * ny + dy][...].astype(F32)
    result = mid[...] + full[...] + bias[...]
    for i in range(group):
        out[i] = result[i * steps : (i + 1) * steps].astype(BF16)


def shape(sizes, kind=BF16):
    return jax.ShapeDtypeStruct(tuple(sizes), kind)


def body(
    tokens,
    lengths,
    cache_keys,
    cache_values,
    norm1_gain,
    norm1_bias,
    w_query,
    b_query,
    w_key,
    b_key,
    w_value,
    b_value,
    w_out,
    b_out,
    norm2_gain,
    norm2_bias,
    w_up,
    b_up,
    w_down,
    b_down,
):
    place = Place(lax.axis_size("seq"), lax.axis_size("req"))
    nx, ny = place.nx, place.ny
    group, steps, width = tokens.shape
    slots = cache_keys.shape[1]
    rows = group * steps
    heads = width // HEAD
    share = width // nx
    bind = functools.partial

    def row(vector):
        return vector.reshape(1, -1)

    def spread(by_dy):
        return [
            by_dy[dy] if dx == 0 and dy == 0 else place.move(by_dy[dy], dx, dy)
            for dx in range(nx)
            for dy in range(ny)
        ]

    toks = [tokens] + [place.move(tokens, dy=dy) for dy in range(1, ny)]
    cols = w_query.shape[1]
    own = [w_query, w_key, w_value]
    siblings = [place.move(weight, dc=1) for weight in own]
    scales = row(jnp.concatenate([norm1_gain, norm1_bias]))
    biases = row(jnp.concatenate([b_query, b_key, b_value]))
    normed, *own = call(
        norm_kernel,
        "norm",
        [tokens, scales, *own],
        [shape((rows, width))] + [shape(w.shape) for w in own],
        in_specs=[VMEM] * 2 + [HBM] * 3,
        scratch=[pltpu.VMEM((rows, width), F32), pltpu.SemaphoreType.DMA((3,))],
        limit=52.75,
    )
    parts = call(
        bind(qkv_kernel, place),
        "norm_qkv",
        [normed, *toks[1:], scales, biases, *own, *siblings],
        [shape((rows, 3 * cols))] * ny,
        scratch=[pltpu.VMEM(((ny - 1) * rows, width), F32), pltpu.VMEM((ny * rows, width), BF16)],
    )
    *parts, tied_up, tied_down = lax.optimization_barrier((*parts, w_up, w_down))
    w_up_sibling = place.move(tied_up, dc=1)
    w_down_sibling = place.move(tied_down, dc=1)
    parts, tied_keys, tied_values = lax.optimization_barrier((parts, cache_keys, cache_values))
    new_keys, new_values, keys, values, mark = call(
        cache_kernel,
        "caches",
        [tied_keys, tied_values],
        [shape(cache_keys.shape)] * 4 + [shape((8, LANES), F32)],
        in_specs=[HBM, HBM],
        out_specs=[HBM, HBM, VMEM, VMEM, VMEM],
        scratch=[pltpu.SemaphoreType.DMA((2, group)), pltpu.SemaphoreType.DMA((2, group))],
        moved=16 * 1024 * 1024,
        limit=46,
    )
    qkv = call(
        bind(add_columns_kernel, place),
        "add_qkv",
        [*spread(parts), mark],
        shape((nx, rows, 3 * cols)),
    )
    qkv, w_up_sibling, w_down_sibling, tied = lax.optimization_barrier(
        (qkv, w_up_sibling, w_down_sibling, w_out)
    )
    pieces = place.gather_z(qkv)
    blocks = [place.transpose(tied, nx - 1 - k) for k in range(nx)]
    pack = max(1, min(group, 256 // slots))
    window = min(32, slots)
    new_keys, new_values, *messages = call(
        bind(attention_kernel, place, heads, steps),
        "attention",
        [*pieces, lengths, keys, values, new_keys, new_values],
        [shape(cache_keys.shape)] * 2 + [shape((rows, share + LANES))] * nx,
        in_specs=[VMEM] * place.nz + [SMEM, VMEM, VMEM, HBM, HBM],
        out_specs=[HBM, HBM] + [VMEM] * nx,
        scratch=[
            pltpu.VMEM((rows, width), F32),
            pltpu.VMEM((rows, width), F32),
            pltpu.VMEM((rows, width), F32),
            pltpu.VMEM((heads * pack * steps, pack * slots + LANES), F32),
            pltpu.VMEM((rows, width), F32),
            pltpu.VMEM((rows, LANES), F32),
            pltpu.VMEM((group, window, width), BF16),
            pltpu.VMEM((group, window, width), BF16),
            pltpu.SemaphoreType.DMA((2, group)),
        ],
        aliases={place.nz + 3: 0, place.nz + 4: 1},
    )
    messages, blocks = lax.optimization_barrier((messages, blocks))
    w_outs = []
    for block in blocks:
        w_outs += [block, place.move(block, dc=1)]
    messages = [messages[0]] + [place.move(messages[dx], dx=dx) for dx in range(1, nx)]
    merged = call(
        bind(merge_x_kernel, place, heads), "merge_x", messages, shape((rows, share + LANES))
    )
    merged, *w_outs = lax.optimization_barrier((merged, *w_outs))
    pieces = place.gather_z(merged)
    out_part = call(
        bind(out_kernel, place, heads),
        "out",
        [*pieces, *w_outs, row(b_out)],
        shape((nx, rows, cols)),
        scratch=[pltpu.VMEM((nx, rows, cols), F32), pltpu.VMEM((rows, share), BF16)],
    )
    projected = call(
        bind(add_out_kernel, place),
        "add_out",
        spread([out_part] * ny),
        shape((ny, nx, rows, cols)),
    )
    up_part, mid = call(
        bind(up_kernel, place),
        "norm_up",
        [
            *toks,
            *place.gather_z(projected),
            row(norm2_gain),
            row(norm2_bias),
            w_up,
            w_up_sibling,
            row(b_up),
        ],
        [shape((ny * rows, w_up.shape[1])), shape((rows, width), F32)],
        scratch=[
            pltpu.VMEM((ny * rows, width), F32),
            pltpu.VMEM((ny * rows, width), BF16),
            pltpu.VMEM((rows, width), F32),
        ],
    )
    up_parts = [up_part] + [place.move(up_part, dy=dy) for dy in range(1, ny)]
    piece = CORES * w_down.shape[1] // nx
    feeds = call(
        bind(down_kernel, place),
        "gelu_down",
        [*up_parts, w_down, w_down_sibling],
        [shape((ny * rows, piece))] * nx,
        scratch=[pltpu.VMEM((ny * rows, CORES * w_down.shape[1]), F32)],
    )
    feeds = [feeds[0]] + [place.move(feeds[dx], dx=dx) for dx in range(1, nx)]
    feed = call(bind(add_x_kernel, place), "add_x", feeds, shape((ny * rows, piece)))
    summed = call(
        bind(add_z_kernel, place),
        "add_z",
        place.gather_z(feed),
        [shape((rows, piece))] * ny,
        scratch=[pltpu.VMEM((ny * rows, piece), F32)],
    )
    hidden_out = call(
        bind(last_kernel, place),
        "last",
        [*spread(summed), mid, row(b_down)],
        shape(tokens.shape),
        scratch=[pltpu.VMEM((rows, width), F32)],
    )
    return (hidden_out, new_keys, new_values)


def solution(mesh):
    in_specs = (
        P("req", None, None),
        P("req"),
        P("req", "seq", None),
        P("req", "seq", None),
        P(),
        P(),
        P("req", "seq"),
        P("seq"),
        P("req", "seq"),
        P("seq"),
        P("req", "seq"),
        P("seq"),
        P("req", "seq"),
        P("seq"),
        P(),
        P(),
        P("req", "seq"),
        P("seq"),
        P("seq", "req"),
        P(),
    )
    out_specs = (P("req", None, None), P("req", "seq", None), P("req", "seq", None))
    return jax.shard_map(body, mesh=mesh, in_specs=in_specs, out_specs=out_specs, check_vma=False)
```
